32 devices in a mesh: batch: 8 (over z, x), row: 4 (over y, core).
Axes of the slice: x: 2, y: 2, z: 4, core: 2. Of those that a mesh axis runs over, the one named last changes fastest.
Arguments:
- inputs: bfloat16 [576, 16, 16, 256], P('batch', 'row'), may hold values from -6 to 6
- partners: int32 [576], P('batch'), may hold values from 0 to 575, as said below
- boxes: int32 [576, 4], P('batch'), may hold values from 0 to 16, as said below
- drops: int32 [576, 2], P('batch'), may hold values 0 or 1
- norm1_gain: bfloat16 [256], replicated, may hold values from 0.5 to 1.5
- norm1_bias: bfloat16 [256], replicated, may hold values from -3 to 3
- qkv_weight: bfloat16 [256, 768], replicated, may hold values from -0.5 to 0.5
- lepe_weight: bfloat16 [3, 3, 256], replicated, may hold values from -1.5 to 1.5
- lepe_bias: bfloat16 [256], replicated, may hold values from -3 to 3
- proj_weight: bfloat16 [256, 256], replicated, may hold values from -0.5 to 0.5
- proj_bias: bfloat16 [256], replicated, may hold values from -3 to 3
- norm2_gain: bfloat16 [256], replicated, may hold values from 0.5 to 1.5
- norm2_bias: bfloat16 [256], replicated, may hold values from -3 to 3
- fc1_weight: bfloat16 [256, 1024], replicated, may hold values from -0.375 to 0.375
- fc1_bias: bfloat16 [1024], replicated, may hold values from -3 to 3
- fc2_weight: bfloat16 [1024, 256], replicated, may hold values from -0.1875 to 0.1875
- fc2_bias: bfloat16 [256], replicated, may hold values from -3 to 3
- cotangent: bfloat16 [576, 16, 16, 256], P('batch', 'row'), may hold values from -6 to 6
Outputs:
- block_out: bfloat16 [576, 16, 16, 256], P('batch', 'row')
- input_grad: bfloat16 [576, 16, 16, 256], P('batch', 'row')
- gain1_grad: float32 [256], replicated
- bias1_grad: float32 [256], replicated
- qkv_grad: float32 [256, 768], replicated
- conv_grad: float32 [3, 3, 256], replicated
- convbias_grad: float32 [256], replicated
- proj_grad: float32 [256, 256], replicated
- projbias_grad: float32 [256], replicated
- gain2_grad: float32 [256], replicated
- bias2_grad: float32 [256], replicated
- fc1_grad: float32 [256, 1024], replicated
- fc1bias_grad: float32 [1024], replicated
- fc2_grad: float32 [1024, 256], replicated
- fc2bias_grad: float32 [256], replicated
The draws below stay inside these ranges and needn't reach their ends.
Inputs may be any that keep to these rules, and one draw needn't show every extreme that they name: Within each aligned block of 72 images the partners are a permutation of that block's image indices. `boxes`: each row holds first row < end row and first column < end column; every box covers grid row and column 8.
All inputs are finite; a program needn't handle non-finite values. No bound on the sum of `drops` on one device may be relied on, other than what follows from the above.
Results may differ from the reference program's by a relative error of at most 0.013.
Values may be sent and summed in bfloat16 or wider, within the bound.
A program may use at most 320 MiB of HBM per device.

```python
import math
import jax
import jax.numpy as jnp
from jax import lax

D = 256
FF = 1024
HEADS = 8
STRIPE = 2
SIDE = 16
IMG_DEV = 72
HDIM = 32
IMAGES = 576


def draw_partners(key, part):
    key = jax.random.fold_in(key, 11)
    blocks = IMAGES // IMG_DEV
    keys = jax.random.split(key, blocks)
    shuffled = jax.vmap(lambda block_key: jax.random.permutation(block_key, IMG_DEV))(keys)
    offsets = IMG_DEV * jnp.arange(blocks, dtype=jnp.int32)[:, None]
    return (shuffled.astype(jnp.int32) + offsets).reshape(IMAGES).astype(jnp.int32)


def draw_boxes(key, part):
    key = jax.random.fold_in(key, 12)
    first_key, second_key, third_key, fourth_key = jax.random.split(key, 4)
    row_first = jax.random.randint(first_key, (IMAGES,), 0, SIDE // 2 + 1)
    row_end = jax.random.randint(second_key, (IMAGES,), SIDE // 2 + 1, SIDE + 1)
    col_first = jax.random.randint(third_key, (IMAGES,), 0, SIDE // 2 + 1)
    col_end = jax.random.randint(fourth_key, (IMAGES,), SIDE // 2 + 1, SIDE + 1)
    return jnp.stack([row_first, row_end, col_first, col_end], axis=1).astype(jnp.int32)


def with_ends(entries, key, low, high):
    longest = entries.shape.index(max(entries.shape))
    spots = []
    for shift in (0, 1):
        where = [jax.random.randint(jax.random.fold_in(key, axis), (), 0, length) for axis, length in enumerate(entries.shape)]
        where[longest] = (where[longest] + shift) % entries.shape[longest]
        spots.append(tuple(where))
    return entries.at[spots[0]].set(low).at[spots[1]].set(high)


def steps_of(key, extent, cuts, least, high):
    factor_of = 1.0
    for axis_at, shards_of in cuts:
        heights = jax.random.uniform(jax.random.fold_in(jax.random.fold_in(key, 6), axis_at), (shards_of,), jnp.float32, least / len(cuts), high / len(cuts))
        factor_of = factor_of * jnp.repeat(jnp.exp(heights), extent[axis_at] // shards_of).reshape((-1,) + (1,) * (len(extent) - 1 - axis_at))
    return factor_of


def normal_values(stream_key, dims, width, most, pieces=(), kind=jnp.bfloat16):
    entries = width * jax.random.normal(stream_key, dims, jnp.float32)
    if pieces:
        entries = entries * steps_of(stream_key, dims, pieces, -0.22, 0.18)
    return jnp.clip(entries, -most, most).astype(kind)


def setup_inputs(seed: int = 0) -> dict:
    key_of = jax.random.split(jax.random.key(seed), 19)
    inputs = normal_values(key_of[0], (IMAGES, SIDE, SIDE, D), 1.0, 6.0, ((0, 8), (1, 4)))
    partners = draw_partners(jax.random.fold_in(key_of[18], 71), 0)
    boxes = draw_boxes(jax.random.fold_in(key_of[18], 71), 0)
    drops = with_ends((jax.random.randint(key_of[3], (IMAGES, 2), 0, 5) < 4).astype(jnp.int32), jax.random.fold_in(key_of[3], 1), 0, 1)
    norm1_gain = jnp.clip(1.0 + 0.1 * jax.random.normal(key_of[4], (D,), jnp.float32), 0.5, 1.5).astype(jnp.bfloat16)
    norm1_bias = normal_values(key_of[5], (D,), 0.3, 3.0)
    qkv_weight = normal_values(key_of[6], (D, 3 * D), (D // 2) ** -0.5, 0.5)
    lepe_weight = normal_values(key_of[7], (3, 3, D), 18 ** -0.5, 1.5)
    lepe_bias = normal_values(key_of[8], (D,), 0.3, 3.0)
    proj_weight = normal_values(key_of[9], (D, D), (D // 2) ** -0.5, 0.5)
    proj_bias = normal_values(key_of[10], (D,), 0.3, 3.0)
    norm2_gain = jnp.clip(1.0 + 0.1 * jax.random.normal(key_of[11], (D,), jnp.float32), 0.5, 1.5).astype(jnp.bfloat16)
    norm2_bias = normal_values(key_of[12], (D,), 0.3, 3.0)
    fc1_weight = normal_values(key_of[13], (D, FF), D ** -0.5, 0.375)
    fc1_bias = normal_values(key_of[14], (FF,), 0.3, 3.0)
    fc2_weight = normal_values(key_of[15], (FF, D), FF ** -0.5, 0.1875)
    fc2_bias = normal_values(key_of[16], (D,), 0.3, 3.0)
    cotangent = normal_values(key_of[17], (IMAGES, SIDE, SIDE, D), 1.0, 6.0, ((0, 8), (1, 4)))
    return dict(inputs=inputs, partners=partners, boxes=boxes, drops=drops, norm1_gain=norm1_gain, norm1_bias=norm1_bias, qkv_weight=qkv_weight, lepe_weight=lepe_weight, lepe_bias=lepe_bias, proj_weight=proj_weight, proj_bias=proj_bias, norm2_gain=norm2_gain, norm2_bias=norm2_bias, fc1_weight=fc1_weight, fc1_bias=fc1_bias, fc2_weight=fc2_weight, fc2_bias=fc2_bias, cotangent=cotangent)


@jax.custom_vjp
def low(v):
    return lax.optimization_barrier(v.astype(jnp.bfloat16)).astype(jnp.float32)

@jax.custom_vjp
def low_back(v):
    return v

def low_keep(v):
    return (low(v), None)

def low_pass(kept, grad):
    return (grad,)

def back_keep(v):
    return (v, None)

def back_low(kept, grad):
    return (low(grad),)
low.defvjp(low_keep, low_pass)
low_back.defvjp(back_keep, back_low)

def layer_norm(value, gain, bias):
    center = value - lax.optimization_barrier(jnp.mean(value, axis=-1, keepdims=True))
    spread = lax.optimization_barrier(jnp.mean(center * center, axis=-1, keepdims=True))
    return center * lax.rsqrt(spread + 1e-05) * gain + bias

def matmul(left, right):
    return jnp.einsum('gxyd,de->gxye', left, right, precision=lax.Precision.HIGHEST)

def attend(queries, key_part, values):
    score_scale = HDIM ** (-0.5)
    scores = low_back(jnp.einsum('...qhe,...khe->...hqk', queries, key_part, precision=lax.Precision.HIGHEST) * score_scale)
    log_total = jax.nn.logsumexp(scores, axis=-1, keepdims=True)
    probs = low(jnp.exp(scores - log_total))
    return jnp.einsum('...hqk,...khe->...qhe', probs, values, precision=lax.Precision.HIGHEST)

def row_windows(value):
    count = value.shape[0]
    return value.reshape(count, SIDE // STRIPE, STRIPE * SIDE, HEADS // 2, HDIM)

def row_layout(value):
    count = value.shape[0]
    return value.reshape(count, SIDE, SIDE, D // 2)

def col_windows(value):
    count = value.shape[0]
    shaped = value.reshape(count, SIDE, SIDE // STRIPE, STRIPE, HEADS // 2, HDIM)
    return shaped.transpose(0, 2, 1, 3, 4, 5).reshape(count, SIDE // STRIPE, STRIPE * SIDE, HEADS // 2, HDIM)

def col_layout(value):
    count = value.shape[0]
    shaped = value.reshape(count, SIDE // STRIPE, SIDE, STRIPE, D // 2)
    return shaped.transpose(0, 2, 1, 3, 4).reshape(count, SIDE, SIDE, D // 2)

def lepe_filter(values, weight, bias):
    padded = jnp.pad(values, ((0, 0), (1, 1), (1, 1), (0, 0)))
    positions = jnp.arange(SIDE)
    channel = jnp.arange(D)[None, None, :] < D // 2
    total = jnp.zeros(values.shape, jnp.float32)
    for down_step in (-1, 0, 1):
        for side_step in (-1, 0, 1):
            window = padded[:, 1 + down_step:1 + down_step + SIDE, 1 + side_step:1 + side_step + SIDE, :]
            by_row = ((positions + down_step) // STRIPE == positions // STRIPE)[:, None, None]
            by_col = ((positions + side_step) // STRIPE == positions // STRIPE)[None, :, None]
            allowed = jnp.where(channel, by_row, by_col)
            total = total + jnp.where(allowed[None], window, 0.0) * weight[down_step + 1, side_step + 1]
    return total + bias

def block_layer(mixed, keep_rates, params):
    norm1_gain, norm1_bias, qkv_weight, lepe_weight, lepe_bias, proj_weight, proj_bias, norm2_gain, norm2_bias, fc1_weight, fc1_bias, fc2_weight, fc2_bias = params
    half_width = D // 2
    normed1 = layer_norm(mixed, norm1_gain, norm1_bias)
    qkv = low(low_back(matmul(low(normed1), qkv_weight)))
    queries = qkv[..., :D]
    key_part = qkv[..., D:2 * D]
    values = qkv[..., 2 * D:]
    flat_ctx = row_layout(attend(row_windows(queries[..., :half_width]), row_windows(key_part[..., :half_width]), row_windows(values[..., :half_width])))
    tall_ctx = col_layout(attend(col_windows(queries[..., half_width:]), col_windows(key_part[..., half_width:]), col_windows(values[..., half_width:])))
    context = jnp.concatenate([flat_ctx, tall_ctx], axis=-1)
    attended = low(low_back(context + lepe_filter(values, lepe_weight, lepe_bias)))
    branch1 = low_back(matmul(attended, proj_weight) + proj_bias)
    hidden1 = mixed + keep_rates[:, 0, None, None, None] * branch1
    normed2 = layer_norm(hidden1, norm2_gain, norm2_bias)
    pre = low_back(matmul(low(normed2), fc1_weight) + fc1_bias)
    act = low(jax.nn.gelu(pre, approximate=False))
    branch2 = low_back(matmul(act, fc2_weight) + fc2_bias)
    return hidden1 + keep_rates[:, 1, None, None, None] * branch2

def reference(inputs, partners, boxes, drops, norm1_gain, norm1_bias, qkv_weight, lepe_weight, lepe_bias, proj_weight, proj_bias, norm2_gain, norm2_bias, fc1_weight, fc1_bias, fc2_weight, fc2_bias, cotangent):
    source = inputs.astype(jnp.float32)
    params = tuple((weight_arg.astype(jnp.float32) for weight_arg in (norm1_gain, norm1_bias, qkv_weight, lepe_weight, lepe_bias, proj_weight, proj_bias, norm2_gain, norm2_bias, fc1_weight, fc1_bias, fc2_weight, fc2_bias)))
    keep_rates = drops.astype(jnp.float32) * 1.25
    positions = jnp.arange(SIDE)
    inside = ((positions[None, :, None] >= boxes[:, 0, None, None]) & (positions[None, :, None] < boxes[:, 1, None, None]) & (positions[None, None, :] >= boxes[:, 2, None, None]) & (positions[None, None, :] < boxes[:, 3, None, None]))[..., None]
    group_size = math.gcd(IMAGES, 16)

    def forward(source, params):
        partner_rows = source[partners]
        mixed = jnp.where(inside, partner_rows, 0.7 * source + 0.3 * partner_rows)
        stacked = mixed.reshape(IMAGES // group_size, group_size, SIDE, SIDE, D)
        keep_groups = keep_rates.reshape(IMAGES // group_size, group_size, 2)

        def step_group(bundle):
            return block_layer(bundle[0], bundle[1], params)
        result = lax.map(jax.checkpoint(step_group), (stacked, keep_groups))
        return result.reshape(IMAGES, SIDE, SIDE, D)
    result, pull = jax.vjp(forward, source, params)
    input_grad, grads = pull(cotangent.astype(jnp.float32))
    return (result.astype(jnp.bfloat16), input_grad.astype(jnp.bfloat16), grads[0], grads[1], grads[2], grads[3], grads[4], grads[5], grads[6], grads[7], grads[8], grads[9], grads[10], grads[11], grads[12])
```

```python
import functools, math

import jax
import jax.numpy as jnp
from jax import lax
from jax.experimental import pallas as pl
from jax.experimental.pallas import tpu as pltpu
from jax.sharding import PartitionSpec as P
from types import SimpleNamespace as NS

F32 = jnp.float32
BF = jnp.bfloat16
EPS = 1e-5
SCALE = 32 ** -0.5
LOG2E = math.log2(math.e)
ERF_P = 0.3275911 / math.sqrt(2.0)
ERF_C = [0.5 * c for c in (0.254829592, -0.284496736, 1.421413741, -1.453152027, 1.061405429)]


def dot(a, b, ca=1, cb=0):
    return lax.dot_general(a, b, (((ca,), (cb,)), ((), ())), preferred_element_type=F32)


def gelu_parts(v):
    t = 1.0 / (1.0 + ERF_P * jnp.abs(v))
    e = jnp.exp2(v * v * (-0.5 * LOG2E))
    poly = ERF_C[4]
    for c in ERF_C[3::-1]:
        poly = poly * t + c
    h = poly * t * e
    cdf = jnp.where(v >= 0.0, 1.0 - h, h)
    act = v * cdf
    slope = cdf + v * (e * (1.0 / math.sqrt(2.0 * math.pi)))
    return act, slope


def normalise(x):
    mean = jnp.mean(x, axis=-1, keepdims=True)
    center = x - mean
    var = jnp.mean(center * center, axis=-1, keepdims=True)
    rstd = lax.rsqrt(var + EPS)
    return center * rstd, rstd


def normalise_back(d, u, rstd, gain):
    e = d * gain
    m1 = jnp.mean(e, axis=-1, keepdims=True)
    m2 = jnp.mean(e * u, axis=-1, keepdims=True)
    return (e - m1 - u * m2) * rstd


def rowsum(x):
    return jnp.sum(x, axis=0, keepdims=True)


def expand(w, hm):
    return jnp.concatenate([w, w, w, w], axis=0) * hm


def diagonal(r, lane):
    o = r[0:32]
    for h in (1, 2, 3):
        o = jnp.where(lane >= 32 * h, r[32 * h : 32 * h + 32], o)
    return o


def shifts(a, pos):
    n = a.shape[0]
    before = jnp.where(pos == 0, 0.0, pltpu.roll(a, 1, 0))
    after = jnp.where(pos == 15, 0.0, pltpu.roll(a, n - 1, 0))
    return before, a, after


def swap_rows(a):
    n, c = a.shape
    a4 = a.reshape(n // 32, 2, 16, c)
    return a4[:, 0], a4[:, 1]


def join_rows(a0, a1):
    n = a0.shape[0]
    return jnp.stack([a0, a1], axis=1).reshape(n * 32, a0.shape[-1])


def psum8(x):
    n, c = x.shape
    return jnp.sum(x.reshape(n // 8, 8, c), axis=0)


G1, B1, G2, B2, PB, FB2, CB, CONV = 0, 1, 2, 3, 4, 5, 6, 7


class Params:
    def __init__(self, refs):
        (
            self.perm,
            self.hm,
            self.vec,
            self.taps,
            self.wf,
            self.wt,
            self.wq,
            self.wp,
            self.w1,
            self.bf1,
            self.w2,
        ) = refs


def permute(perm, x):
    n = x.shape[0] // 256
    return jnp.concatenate(
        [dot(perm, x[256 * i : 256 * i + 256]).astype(BF) for i in range(n)], axis=0
    )


def phase_one(c, p, s, a, keep1, keep2):
    tokens = s.x.shape[1]
    windows = tokens // 32
    perm = p.perm[...]
    hm = p.hm[...]
    vec = lambda i: p.vec[i : i + 1]
    x = s.x[c].astype(F32)
    u1, _ = normalise(x)
    n1 = (u1 * vec(G1) + vec(B1)).astype(BF)
    s.n1[c] = n1
    n1p = permute(perm, n1)
    qkv_f = dot(n1, p.wf[...]).astype(BF)
    qkv_t = dot(n1p, p.wt[...]).astype(BF)
    s.q[c] = jnp.concatenate([qkv_f[:, 0:128], qkv_t[:, 0:128]], axis=1)
    s.k[c] = jnp.concatenate([qkv_f[:, 128:256], qkv_t[:, 128:256]], axis=1)
    s.v[c] = jnp.concatenate([qkv_f[:, 256:384], qkv_t[:, 256:384]], axis=1)
    lane = lax.broadcasted_iota(jnp.int32, (32, 128), 1)
    pos = lax.broadcasted_iota(jnp.int32, (tokens, 256), 0) % 16
    out = []
    for w in range(windows):
        halves = []
        rows = slice(32 * w, 32 * w + 32)
        for half in range(2):
            cols = slice(128 * half, 128 * half + 128)
            qx = expand(s.q[c, rows, cols], hm)
            st = dot(s.k[c, rows, cols], qx, 1, 1)
            top = jnp.max(st, axis=0, keepdims=True)
            e = jnp.exp2((st - top) * (SCALE * LOG2E))
            pr = (e * (1.0 / jnp.sum(e, axis=0, keepdims=True))).astype(BF)
            s.p[c, rows, cols] = pr
            halves.append(diagonal(dot(pr, s.v[c, rows, cols], 0, 0), lane))
        out.append(jnp.concatenate(halves, axis=1))
    ctx = jnp.concatenate(out, axis=0)
    tap = lambda i, j: p.taps[3 * (i + 1) + j + 1 : 3 * (i + 1) + j + 2]
    vs = shifts(s.v[c].astype(F32), pos)
    line = lambda i, pick: sum(pick(vs[j + 1]) * tap(i, j) for j in (-1, 0, 1))
    first = lambda z: swap_rows(z)[0].reshape(tokens // 2, 256)
    second = lambda z: swap_rows(z)[1].reshape(tokens // 2, 256)
    o0 = line(0, first) + line(1, second)
    o1 = line(0, second) + line(-1, first)
    o0 = o0.reshape(windows, 16, 256)
    o1 = o1.reshape(windows, 16, 256)
    lepe = join_rows(o0, o1) + vec(CB)
    att = (ctx + lepe).astype(BF)
    att = jnp.concatenate([att[:, :128], permute(perm, att[:, 128:])], axis=1)
    branch1 = dot(att, p.wp[...]) + vec(PB)
    h1 = x + keep1 * branch1
    u2, rstd2 = normalise(h1)
    n2 = (u2 * vec(G2) + vec(B2)).astype(BF)
    cot = s.cot[c].astype(F32)
    db2f = keep2 * cot
    db2 = db2f.astype(BF)
    a.small[FB2] += psum8(db2.astype(F32))
    ones = jnp.ones((16, tokens), BF)
    n2t = jnp.concatenate([n2.T, ones], axis=0)
    db2t = db2.T
    branch2 = jnp.zeros((tokens, 256), F32)
    dn2 = jnp.zeros((tokens, 256), F32)
    for f in range(4):
        fs = slice(256 * f, 256 * f + 256)
        pre = dot(n2, p.w1[:, fs]) + p.bf1[:, fs]
        act, slope = gelu_parts(pre)
        act = act.astype(BF)
        dpre = (slope * dot(db2, p.w2[fs, :], 1, 1)).astype(BF)
        branch2 = branch2 + dot(act, p.w2[fs, :])
        dn2 = dn2 + dot(dpre, p.w1[:, fs], 1, 1)
        a.w1[:, fs] += dot(n2t, dpre)
        a.w2t[:, fs] += dot(db2t, act)
    s.out[c] = (h1 + keep2 * (branch2 + vec(FB2))).astype(BF)
    a.small[G2] += psum8(dn2 * u2)
    a.small[B2] += psum8(dn2)
    dh1 = cot + normalise_back(dn2, u2, rstd2, vec(G2))
    s.dh1[c] = dh1
    db1 = (keep1 * dh1).astype(BF)
    a.small[PB] += psum8(db1.astype(F32))
    a.wp[...] += dot(att, db1, 0, 0)
    datt = dot(db1, p.wp[...], 1, 1).astype(BF)
    s.da[c] = jnp.concatenate([datt[:, :128], permute(perm, datt[:, 128:])], axis=1)


def phase_two(c, p, s, a):
    tokens = s.x.shape[1]
    windows = tokens // 32
    perm = p.perm[...]
    hm = p.hm[...]
    vec = lambda i: p.vec[i : i + 1]
    lane = lax.broadcasted_iota(jnp.int32, (32, 128), 1)
    pos = lax.broadcasted_iota(jnp.int32, (tokens, 256), 0) % 16
    dq, dk, dv = [], [], []
    for w in range(windows):
        hq, hk, hv = [], [], []
        rows = slice(32 * w, 32 * w + 32)
        for half in range(2):
            cols = slice(128 * half, 128 * half + 128)
            dax = expand(s.da[c, rows, cols], hm)
            qx = expand(s.q[c, rows, cols], hm)
            dp = dot(s.v[c, rows, cols], dax, 1, 1)
            pb = s.p[c, rows, cols]
            pr = pb.astype(F32)
            t = pr * dp
            ds = (t - pr * jnp.sum(t, axis=0, keepdims=True)).astype(BF)
            hv.append(dot(pb, dax))
            hk.append(dot(ds, qx))
            hq.append(diagonal(dot(ds, s.k[c, rows, cols], 0, 0), lane))
        dq.append(jnp.concatenate(hq, axis=1))
        dk.append(jnp.concatenate(hk, axis=1))
        dv.append(jnp.concatenate(hv, axis=1))
    dq = (jnp.concatenate(dq, axis=0) * SCALE).astype(BF)
    dk = (jnp.concatenate(dk, axis=0) * SCALE).astype(BF)
    dv = jnp.concatenate(dv, axis=0)
    tap = lambda i, j: p.taps[3 * (i + 1) + j + 1 : 3 * (i + 1) + j + 2]
    da = s.da[c].astype(F32)
    a.small[CB] += psum8(da)
    before, here, after = shifts(da, pos)
    moved = {-1: after, 0: here, 1: before}
    first = lambda z: swap_rows(z)[0].reshape(tokens // 2, 256)
    second = lambda z: swap_rows(z)[1].reshape(tokens // 2, 256)
    v = s.v[c].astype(F32)
    v0, v1 = first(v), second(v)
    line = lambda i, pick: sum(pick(moved[j]) * tap(i, j) for j in (-1, 0, 1))
    o0 = line(0, first) + line(-1, second)
    o1 = line(1, first) + line(0, second)
    dv = dv + join_rows(o0.reshape(windows, 16, 256), o1.reshape(windows, 16, 256))
    for j in (-1, 0, 1):
        m0, m1 = first(moved[j]), second(moved[j])
        a.small[CONV + 3 + j + 1] += psum8(m0 * v0) + psum8(m1 * v1)
        a.small[CONV + 6 + j + 1] += psum8(m0 * v1)
        a.small[CONV + 0 + j + 1] += psum8(m1 * v0)
    dv = dv.astype(BF)
    tall = permute(perm, jnp.concatenate([dq[:, 128:], dk[:, 128:], dv[:, 128:]], axis=1))
    dqkv = jnp.concatenate(
        [dq[:, :128], tall[:, :128], dk[:, :128], tall[:, 128:256], dv[:, :128], tall[:, 256:]],
        axis=1,
    )
    n1t = s.n1[c].T
    for f in range(3):
        fs = slice(256 * f, 256 * f + 256)
        a.wq[:, fs] += dot(n1t, dqkv[:, fs])
    dn1 = dot(dqkv, p.wq[...], 1, 1)
    u1, rstd1 = normalise(s.x[c].astype(F32))
    a.small[G1] += psum8(dn1 * u1)
    a.small[B1] += psum8(dn1)
    dx = s.dh1[c] + normalise_back(dn1, u1, rstd1, vec(G1))
    s.dx[c] = dx.astype(BF)
def prep(inputs_dict):
    d = inputs_dict
    g = lambda n: d[n].astype(F32)
    t = jnp.arange(256)
    perm = (((t % 16) * 16 + t // 16)[:, None] == t[None, :]).astype(BF)
    r = jnp.arange(128)
    hm = (r[:, None] // 32 == r[None, :] // 32).astype(BF)
    vec = jnp.stack([g("norm1_gain"), g("norm1_bias"), g("norm2_gain"), g("norm2_bias"), g("proj_bias"), g("fc2_bias"), g("lepe_bias"), jnp.zeros((256,), F32)])
    lw = g("lepe_weight")
    taps = jnp.concatenate([lw[..., :128], lw.transpose(1, 0, 2)[..., 128:]], axis=-1).reshape(9, 256)
    wq = d["qkv_weight"]
    wf = jnp.concatenate([wq[:, 0:128], wq[:, 256:384], wq[:, 512:640]], axis=1)
    wt = jnp.concatenate([wq[:, 128:256], wq[:, 384:512], wq[:, 640:768]], axis=1)
    return [perm, hm, vec, taps, wf, wt, wq, d["proj_weight"], d["fc1_weight"], g("fc1_bias")[None], d["fc2_weight"]]

def kernel(nimg, x_ref, cot_ref, drops_ref, *refs):
    p = Params(refs[:11])
    out, dx, w1, w2t, wq, wp, small = refs[11:18]
    q, k, v, pr, n1, dh1, da = refs[18:]
    s = NS(x=x_ref, cot=cot_ref, out=out, dx=dx, q=q, k=k, v=v, p=pr, n1=n1, dh1=dh1, da=da)
    a = NS(w1=w1, w2t=w2t, wq=wq, wp=wp, small=small)
    for r in (w1, w2t, wq, wp, small):
        r[...] = jnp.zeros_like(r)
    chunks = x_ref.shape[0]
    def keep(c, j):
        return jnp.concatenate([jnp.full((256, 1), drops_ref[c * nimg + i, j].astype(F32) * 1.25) for i in range(nimg)], axis=0)
    def one(c, _):
        phase_one(c, p, s, a, keep(c, 0), keep(c, 1))
        return 0
    def two(c, _):
        phase_two(c, p, s, a)
        return 0
    lax.fori_loop(0, chunks, one, 0)
    lax.fori_loop(0, chunks, two, 0)

def run(x, cot, drops, ws, nimg=2):
    chunks = x.size // (65536 * nimg)
    x = x.reshape(chunks, 256 * nimg, 256); cot = cot.reshape(x.shape)
    V = pl.BlockSpec(memory_space=pltpu.VMEM)
    sds = jax.ShapeDtypeStruct
    T = 256 * nimg
    vm = lambda dt: pltpu.VMEM((chunks, T, 256), dt)
    return pl.pallas_call(functools.partial(kernel, nimg),
        in_specs=[V, V, pl.BlockSpec(memory_space=pltpu.SMEM)] + [V] * 11,
        out_specs=[V] * 7,
        out_shape=[sds(x.shape, BF), sds(x.shape, BF), sds((272, 1024), F32), sds((256, 1024), F32), sds((256, 768), F32), sds((256, 256), F32), sds((16, 8, 256), F32)],
        scratch_shapes=[vm(BF), vm(BF), vm(BF), vm(BF), vm(BF), vm(F32), vm(BF)],
        compiler_params=pltpu.CompilerParams(vmem_limit_bytes=60 * 2**20),
    )(x, cot, drops, *ws)


def per_device(inputs, partners, boxes, drops, norm1_gain, norm1_bias, qkv_weight, lepe_weight, lepe_bias, proj_weight, proj_bias, norm2_gain, norm2_bias, fc1_weight, fc1_bias, fc2_weight, fc2_bias, cotangent):
    image_count, row_count, side, width = inputs.shape
    shares = lax.axis_size("row")
    mine = image_count // shares
    row = lax.axis_index("row")
    local_partner = partners - lax.axis_index("batch") * image_count
    row_ids = row * row_count + jnp.arange(row_count)
    col_ids = jnp.arange(side)
    source = inputs.astype(F32)
    partner_rows = inputs[local_partner].astype(F32)
    inside = (
        (row_ids[None, :, None] >= boxes[:, 0, None, None])
        & (row_ids[None, :, None] < boxes[:, 1, None, None])
        & (col_ids[None, None, :] >= boxes[:, 2, None, None])
        & (col_ids[None, None, :] < boxes[:, 3, None, None])
    )[..., None]
    mixed = jnp.where(inside, partner_rows, 0.7 * source + 0.3 * partner_rows).astype(BF)
    x = lax.all_to_all(mixed, "row", split_axis=0, concat_axis=1, tiled=True)
    cot = lax.all_to_all(cotangent, "row", split_axis=0, concat_axis=1, tiled=True)
    my_drops = lax.dynamic_slice_in_dim(drops, row * mine, mine, 0)
    names = dict(norm1_gain=norm1_gain, norm1_bias=norm1_bias, qkv_weight=qkv_weight, lepe_weight=lepe_weight, lepe_bias=lepe_bias, proj_weight=proj_weight, proj_bias=proj_bias, norm2_gain=norm2_gain, norm2_bias=norm2_bias, fc1_weight=fc1_weight, fc1_bias=fc1_bias, fc2_weight=fc2_weight, fc2_bias=fc2_bias)
    out, dx, w1, w2t, wq, wp, small = run(x, cot, my_drops, prep(names), 2)
    shape = (mine, side, side, width)
    out = lax.all_to_all(out.reshape(shape), "row", split_axis=1, concat_axis=0, tiled=True)
    dx = lax.all_to_all(dx.reshape(shape), "row", split_axis=1, concat_axis=0, tiled=True).astype(F32)
    small = jnp.sum(small, axis=1)
    w1, w2t, wq, wp, small = lax.psum((w1, w2t, wq, wp, small), ("batch", "row"))
    own_part = 0.7 * jnp.where(inside, 0.0, dx)
    toward = jnp.where(inside, dx, 0.3 * dx)
    image_ids = jnp.arange(image_count)
    hits = local_partner[:, None] == image_ids[None, :]
    inverse = jnp.sum(jnp.where(hits, image_ids[:, None], 0), axis=0)
    input_grad = (own_part + toward[inverse]).astype(BF)
    conv = small[CONV : CONV + 9].reshape(3, 3, 256)
    conv = jnp.concatenate([conv[..., :128], conv.transpose(1, 0, 2)[..., 128:]], axis=-1)
    return (
        out,
        input_grad,
        small[G1],
        small[B1],
        wq,
        conv,
        small[CB],
        wp,
        small[PB],
        small[G2],
        small[B2],
        w1[:256],
        w1[256],
        w2t.T,
        small[FB2],
    )


def solution(mesh):
    tokens = P("batch", "row", None, None)
    return jax.shard_map(
        per_device,
        mesh=mesh,
        in_specs=(tokens, P("batch"), P("batch", None), P("batch", None)) + (P(),) * 13 + (tokens,),
        out_specs=(tokens, tokens) + (P(),) * 13,
        check_vma=False,
    )
```

```python
import functools
import math

import jax
import jax.numpy as jnp
from jax import lax
from jax.experimental import pallas as pl
from jax.experimental.pallas import tpu as pltpu
from jax.sharding import PartitionSpec as P

F32 = jnp.float32
BF = jnp.bfloat16
EPS = 1e-5
SCALE = 32**-0.5
LOG2E = math.log2(math.e)
ERF_P = 0.3275911 / math.sqrt(2.0)
ERF_C = [0.5 * c for c in (0.254829592, -0.284496736, 1.421413741, -1.453152027, 1.061405429)]
G1, B1, G2, B2, PB, FB2, CB, CONV, FB1 = 0, 1, 2, 3, 4, 5, 6, 7, 16
N1, AT, DA, DN = 0, 1, 2, 3


def dot(a, b, ca=1, cb=0):
    return lax.dot_general(a, b, (((ca,), (cb,)), ((), ())), preferred_element_type=F32)


def gelu_parts(v):
    t = 1.0 / (1.0 + ERF_P * jnp.abs(v))
    e = jnp.exp2(v * v * (-0.5 * LOG2E))
    poly = ERF_C[4]
    for c in ERF_C[3::-1]:
        poly = poly * t + c
    h = poly * t * e
    cdf = jnp.where(v >= 0.0, 1.0 - h, h)
    return v * cdf, cdf + v * (e * (1.0 / math.sqrt(2.0 * math.pi)))


def normalise(x):
    center = x - jnp.mean(x, axis=-1, keepdims=True)
    rstd = lax.rsqrt(jnp.mean(center * center, axis=-1, keepdims=True) + EPS)
    return center * rstd, rstd


def normalise_back(d, u, rstd, gain):
    e = d * gain
    m1 = jnp.mean(e, axis=-1, keepdims=True)
    m2 = jnp.mean(e * u, axis=-1, keepdims=True)
    return (e - m1 - u * m2) * rstd


def sum8(x):
    n, c = x.shape
    return jnp.sum(x.reshape(n // 8, 8, c), axis=0)


def split_heads(w, lm):
    return [w * lm[h : h + 1] for h in range(4)]


def skewed(parts, w):
    return jnp.concatenate([parts[j ^ w] for j in range(4)], axis=0)


def stacked(parts, j):
    return jnp.concatenate([parts[w][j ^ w] for w in range(4)], axis=0)


def unskew(o, w, lane):
    r = o[w]
    for h in (1, 2, 3):
        r = jnp.where(lane >= 32 * h, o[h ^ w], r)
    return r


def four(x):
    return [x[32 * w : 32 * w + 32] for w in range(4)]


def attend_group(q, k, v, lm, lane):
    ps = []
    for w, (qw, kw) in enumerate(zip(four(q), four(k))):
        st = dot(kw, skewed(split_heads(qw, lm), w), 1, 1)
        top = jnp.max(st, axis=0, keepdims=True)
        e = jnp.exp2((st - top) * (SCALE * LOG2E))
        ps.append((e * (1.0 / jnp.sum(e, axis=0, keepdims=True))).astype(BF))
    p = jnp.concatenate(ps, axis=0)
    pt = four(p.T)
    vh = [split_heads(vw, lm) for vw in four(v)]
    o = [dot(pt[j], stacked(vh, j)) for j in range(4)]
    return p, jnp.concatenate([unskew(o, w, lane) for w in range(4)], axis=0)


def attend_group_back(q, k, v, p, da, lm, lane):
    dss, dks, dvs = [], [], []
    for w, (qw, vw, pw, dw) in enumerate(zip(four(q), four(v), four(p), four(da))):
        dx = skewed(split_heads(dw, lm), w)
        dp = dot(vw, dx, 1, 1)
        pr = pw.astype(F32)
        t = pr * dp
        ds = (t - pr * jnp.sum(t, axis=0, keepdims=True)).astype(BF)
        dss.append(ds)
        dvs.append(dot(pw, dx))
        dks.append(dot(ds, skewed(split_heads(qw, lm), w)))
    dst = four(jnp.concatenate(dss, axis=0).T)
    kh = [split_heads(kw, lm) for kw in four(k)]
    o = [dot(dst[j], stacked(kh, j)) for j in range(4)]
    dq = jnp.concatenate([unskew(o, w, lane) for w in range(4)], axis=0)
    return dq, jnp.concatenate(dks, axis=0), jnp.concatenate(dvs, axis=0)


def shifts(a):
    n = a.shape[0]
    pos = lax.broadcasted_iota(jnp.int32, a.shape, 0) % 16
    return {
        -1: jnp.where(pos == 0, 0.0, pltpu.roll(a, 1, 0)),
        0: a,
        1: jnp.where(pos == 15, 0.0, pltpu.roll(a, n - 1, 0)),
    }


def lines(a):
    n, c = a.shape
    b = a.reshape(n // 32, 2, 16, c)
    return b[:, 0].reshape(n // 2, c), b[:, 1].reshape(n // 2, c)


def woven(a0, a1):
    n, c = a0.shape
    return jnp.stack([a0.reshape(n // 16, 16, c), a1.reshape(n // 16, 16, c)], axis=1).reshape(2 * n, c)


def attend_half(s, lm, taps, shift):
    tokens = s["q"].shape[0]
    lane = lax.broadcasted_iota(jnp.int32, (32, 128), 1)
    out = []
    for g in range(tokens // 128):
        rows = slice(128 * g, 128 * g + 128)
        p, o = attend_group(s["q"][rows], s["k"][rows], s["v"][rows], lm, lane)
        s["p"][rows] = p
        out.append(o)
    tap = lambda i, j: taps[3 * (i + 1) + j + 1][None]
    near = {j: lines(z) for j, z in shifts(s["v"][...].astype(F32)).items()}
    line = lambda i, n: sum(near[j][n] * tap(i, j) for j in (-1, 0, 1))
    lepe = woven(line(0, 0) + line(1, 1), line(0, 1) + line(-1, 0))
    return (jnp.concatenate(out, axis=0) + (lepe + shift)).astype(BF)


def attend_half_back(s, lm, taps, small, cols):
    tokens = s["q"].shape[0]
    lane = lax.broadcasted_iota(jnp.int32, (32, 128), 1)
    parts = []
    for g in range(tokens // 128):
        rows = slice(128 * g, 128 * g + 128)
        parts.append(attend_group_back(s["q"][rows], s["k"][rows], s["v"][rows], s["p"][rows], s["da"][rows], lm, lane))
    dq, dk, dv = (jnp.concatenate(z, axis=0) for z in zip(*parts))
    tap = lambda i, j: taps[3 * (i + 1) + j + 1][None]
    da = s["da"][...].astype(F32)
    small[CB, :, cols] += sum8(da)
    moved = {-j: lines(z) for j, z in shifts(da).items()}
    v0, v1 = lines(s["v"][...].astype(F32))
    line = lambda i, n: sum(moved[j][n] * tap(i, j) for j in (-1, 0, 1))
    dv = dv + woven(line(0, 0) + line(-1, 1), line(1, 0) + line(0, 1))
    for j in (-1, 0, 1):
        m0, m1 = moved[j]
        small[CONV + 3 + j + 1, :, cols] += sum8(m0 * v0 + m1 * v1)
        small[CONV + 6 + j + 1, :, cols] += sum8(m0 * v1)
        small[CONV + 0 + j + 1, :, cols] += sum8(m1 * v0)
    return jnp.concatenate([(dq * SCALE).astype(BF), (dk * SCALE).astype(BF), dv.astype(BF)], axis=1)


class Exchange:
    def __init__(self, me, shares, send_sem, recv_sem):
        self.me, self.shares, self.send_sem, self.recv_sem = me, shares, send_sem, recv_sem

    def copy(self, kind, c, d, src, dst, arriving):
        to = lax.rem(self.me + d, self.shares)
        far = lax.rem(self.me + self.shares - d, self.shares) if arriving else self.me
        if kind in (N1, DA):
            source, target = src.at[c, to], dst.at[c, :, far]
        else:
            source, target = src.at[c, :, to], dst.at[c, far]
        return pltpu.make_async_remote_copy(
            src_ref=source,
            dst_ref=target,
            send_sem=self.send_sem.at[kind, c, d - 1],
            recv_sem=self.recv_sem.at[kind, c, d - 1],
            device_id={"row": to},
            device_id_type=pl.DeviceIdType.MESH,
        )

    def send(self, kind, c, src, dst):
        me = self.me
        if kind in (N1, DA):
            dst[c, :, me] = src[c, me]
        else:
            dst[c, me] = src[c, :, me]
        for d in range(1, self.shares):
            self.copy(kind, c, d, src, dst, False).start()

    def receive(self, kind, c, src, dst):
        for d in range(1, self.shares):
            self.copy(kind, c, d, src, dst, True).wait_recv()

    def sent(self, kind, c, src, dst):
        for d in range(1, self.shares):
            self.copy(kind, c, d, src, dst, False).wait_send()


def block_kernel(
    shares,
    ahead,
    boxes,
    drops,
    partners,
    inverse,
    x_ref,
    cot_ref,
    vec,
    wq,
    wp,
    w1,
    w2,
    out,
    ig,
    gw1,
    gw2t,
    gqf,
    gqt,
    gp,
    small,
    perm_ref,
    wf_ref,
    wt_ref,
    mixed,
    n1h,
    n1t,
    n1p,
    qf,
    kf,
    vf,
    pf,
    qt,
    kt,
    vt,
    pt,
    att_f,
    att_ts,
    att_th,
    dh1,
    da_f,
    da_ts,
    da_tt,
    dn_ts,
    dn_th,
    send_sem,
    recv_sem,
):
    chunks, _, pair, strip = n1h.shape[:4]
    images = x_ref.shape[0]
    mine = images // shares
    tokens = shares * pair * strip
    me = lax.axis_index("row")
    ex = Exchange(me, shares, send_sem, recv_sem)

    barrier = pltpu.get_barrier_semaphore()
    for d in range(1, shares):
        pl.semaphore_signal(
            barrier, inc=1, device_id={"row": lax.rem(me + d, shares)}, device_id_type=pl.DeviceIdType.MESH
        )
    pl.semaphore_wait(barrier, shares - 1)

    v = lambda i: vec[i : i + 1]
    lm = (
        lax.broadcasted_iota(jnp.int32, (8, 128), 0) == lax.broadcasted_iota(jnp.int32, (8, 128), 1) // 32
    ).astype(F32).astype(BF)
    to_row = lax.broadcasted_iota(jnp.int32, (256, 256), 0)
    to_col = lax.broadcasted_iota(jnp.int32, (256, 256), 1)
    perm_ref[...] = jnp.where((to_row % 16) * 16 + to_row // 16 == to_col, 1.0, 0.0).astype(BF)
    for ref in (gw1, gw2t, gqf, gqt, gp, small):
        ref[...] = jnp.zeros_like(ref)
    for part in range(3):
        cols = slice(128 * part, 128 * part + 128)
        wf_ref[:, cols] = wq[:, 256 * part : 256 * part + 128]
        wt_ref[:, cols] = wq[:, 256 * part + 128 : 256 * part + 256]
    taps = [vec[CONV + i] for i in range(9)]
    taps_f = [z[:128] for z in taps]
    taps_t = [z[128:] for z in taps]

    spot = lax.broadcasted_iota(jnp.int32, (strip, 1), 0)
    grid_row = me * (strip // 16) + spot // 16
    grid_col = spot % 16

    def shares_of(image):
        inside = (
            (grid_row >= boxes[image, 0])
            & (grid_row < boxes[image, 1])
            & (grid_col >= boxes[image, 2])
            & (grid_col < boxes[image, 3])
        )
        return jnp.where(inside, 0.0, 0.7), jnp.where(inside, 1.0, 0.3)

    def home(c):
        return [(q, i, mine * q + pair * c + i) for q in range(shares) for i in range(pair)]

    def permute(value):
        whole = perm_ref[...]
        return jnp.concatenate(
            [dot(whole, value[256 * i : 256 * i + 256]).astype(BF) for i in range(pair)], axis=0
        )

    def keep(c, j):
        return jnp.concatenate(
            [jnp.full((strip, 1), drops[image, j].astype(F32) * 1.25) for _, _, image in home(c)], axis=0
        )

    def half(c, tall):
        refs = (qt, kt, vt, pt) if tall else (qf, kf, vf, pf)
        return dict(zip("qkvp", [r.at[c] for r in refs]))

    def mix(c, _):
        for q, i, image in home(c):
            own, other = shares_of(image)
            m = own * x_ref[image].astype(F32) + other * x_ref[partners[image]].astype(F32)
            mixed[image] = m
            u, _ = normalise(m)
            n1h[c, q, i] = (u * v(G1) + v(B1)).astype(BF)
        ex.send(N1, c, n1h, n1t)
        return 0

    def flat(c, _):
        qkv = dot(n1h[c].reshape(tokens, 256), wf_ref[...]).astype(BF)
        qf[c], kf[c], vf[c] = qkv[:, :128], qkv[:, 128:256], qkv[:, 256:]
        att_f[c] = attend_half(half(c, False), lm, taps_f, vec[CB : CB + 1, :128])
        return 0

    def tall(c, _):
        ex.receive(N1, c, n1h, n1t)
        n1 = permute(n1t[c].reshape(tokens, 256))
        n1p[c] = n1
        qkv = dot(n1, wt_ref[...]).astype(BF)
        qt[c], kt[c], vt[c] = qkv[:, :128], qkv[:, 128:256], qkv[:, 256:]
        att = attend_half(half(c, True), lm, taps_t, vec[CB : CB + 1, 128:])
        att_ts[c] = permute(att).reshape(att_ts.shape[1:])
        ex.send(AT, c, att_ts, att_th)
        return 0

    def mlp(c, _):
        ex.receive(AT, c, att_ts, att_th)
        keep1, keep2 = keep(c, 0), keep(c, 1)
        att = jnp.concatenate([att_f[c], att_th[c].reshape(tokens, 128)], axis=1)
        m = jnp.concatenate([mixed[image] for _, _, image in home(c)], axis=0)
        h1 = m + keep1 * (dot(att, wp[...]) + v(PB))
        u2, rstd2 = normalise(h1)
        n2 = (u2 * v(G2) + v(B2)).astype(BF)
        cot = jnp.concatenate([cot_ref[image] for _, _, image in home(c)], axis=0).astype(F32)
        db2 = (keep2 * cot).astype(BF)
        small[FB2] += sum8(db2.astype(F32))
        n2t = jnp.concatenate([n2.T, jnp.ones((16, tokens), BF)], axis=0)
        db2t = db2.T
        branch2 = jnp.zeros((tokens, 256), F32)
        dn2 = jnp.zeros((tokens, 256), F32)
        for f in range(w1.shape[1] // 256):
            fs = slice(256 * f, 256 * f + 256)
            act, slope = gelu_parts(dot(n2, w1[:, fs]) + v(FB1 + f))
            act = act.astype(BF)
            dpre = (slope * dot(db2, w2[fs, :], 1, 1)).astype(BF)
            branch2 = branch2 + dot(act, w2[fs, :])
            dn2 = dn2 + dot(dpre, w1[:, fs], 1, 1)
            gw1[:, fs] += dot(n2t, dpre)
            gw2t[:, fs] += dot(db2t, act)
        done = (h1 + keep2 * (branch2 + v(FB2))).astype(BF)
        for n, (_, _, image) in enumerate(home(c)):
            out[image] = done[strip * n : strip * n + strip]
        small[G2] += sum8(dn2 * u2)
        small[B2] += sum8(dn2)
        d = cot + normalise_back(dn2, u2, rstd2, v(G2))
        dh1[c] = d
        db1 = (keep1 * d).astype(BF)
        small[PB] += sum8(db1.astype(F32))
        gp[...] += dot(att, db1, 0, 0)
        datt = dot(db1, wp[...], 1, 1).astype(BF)
        da_f[c] = datt[:, :128]
        da_ts[c] = datt[:, 128:].reshape(da_ts.shape[1:])
        ex.send(DA, c, da_ts, da_tt)
        return 0

    def tall_back(c, _):
        ex.receive(DA, c, da_ts, da_tt)
        da = permute(da_tt[c].reshape(tokens, 128))
        s = dict(half(c, True), da=da)
        dqkv = attend_half_back(s, lm, taps_t, small, slice(128, 256))
        gqt[...] += dot(n1p[c], dqkv, 0, 0)
        dn_ts[c] = permute(dot(dqkv, wt_ref[...], 1, 1).astype(BF)).reshape(dn_ts.shape[1:])
        ex.send(DN, c, dn_ts, dn_th)
        return 0

    def flat_back(c, _):
        s = dict(half(c, False), da=da_f.at[c])
        dqkv = attend_half_back(s, lm, taps_f, small, slice(0, 128))
        gqf[...] += dot(n1h[c].reshape(tokens, 256), dqkv, 0, 0)
        dn1 = dot(dqkv, wf_ref[...], 1, 1)
        ex.receive(DN, c, dn_ts, dn_th)
        dn1 = dn1 + dn_th[c].reshape(tokens, 256).astype(F32)
        m = jnp.concatenate([mixed[image] for _, _, image in home(c)], axis=0)
        u1, rstd1 = normalise(m)
        small[G1] += sum8(dn1 * u1)
        small[B1] += sum8(dn1)
        d = dh1[c] + normalise_back(dn1, u1, rstd1, v(G1))
        for n, (_, _, image) in enumerate(home(c)):
            mixed[image] = d[strip * n : strip * n + strip]
        return 0

    def unmix(image, _):
        other = inverse[image]
        ig[image] = (shares_of(image)[0] * mixed[image] + shares_of(other)[1] * mixed[other]).astype(BF)
        return 0

    def both(first, second, lead):
        lax.fori_loop(0, lead, first, 0)

        def step(c, _):
            first(c + lead, 0)
            second(c, 0)
            return 0

        lax.fori_loop(0, chunks - lead, step, 0)
        lax.fori_loop(chunks - lead, chunks, second, 0)

    lax.fori_loop(0, chunks, mix, 0)
    lax.fori_loop(0, chunks, flat, 0)
    both(tall, mlp, ahead)
    both(tall_back, flat_back, ahead)
    lax.fori_loop(0, images, unmix, 0)

    def drain(c, _):
        for kind, src, dst in ((N1, n1h, n1t), (AT, att_ts, att_th), (DA, da_ts, da_tt), (DN, dn_ts, dn_th)):
            ex.sent(kind, c, src, dst)
        return 0

    lax.fori_loop(0, chunks, drain, 0)


def block(inputs, cotangent, boxes, drops, partners, inverse, vec, wq, wp, w1, w2, pair=2, ahead=2):
    images, grid_rows, side, width = inputs.shape
    shares = lax.axis_size("row")
    strip = grid_rows * side
    chunks = images // shares // pair
    tokens = shares * pair * strip
    hidden = w1.shape[1]
    sds = jax.ShapeDtypeStruct
    vmem = pl.BlockSpec(memory_space=pltpu.VMEM)
    smem = pl.BlockSpec(memory_space=pltpu.SMEM)
    x = inputs.reshape(images, strip, width)
    cot = cotangent.reshape(images, strip, width)
    rows = lambda ch, dt=BF: pltpu.VMEM((chunks, tokens, ch), dt)
    at_home = lambda ch: pltpu.VMEM((chunks, shares, pair, strip, ch), BF)
    at_tall = lambda ch: pltpu.VMEM((chunks, pair, shares, strip, ch), BF)
    return pl.pallas_call(
        functools.partial(block_kernel, shares, ahead),
        in_specs=[smem] * 4 + [vmem] * 7,
        out_specs=[vmem] * 8,
        out_shape=[
            sds(x.shape, BF),
            sds(x.shape, BF),
            sds((width + 16, hidden), F32),
            sds((width, hidden), F32),
            sds((width, 384), F32),
            sds((width, 384), F32),
            sds((width, width), F32),
            sds((16, 8, width), F32),
        ],
        scratch_shapes=[
            pltpu.VMEM((256, 256), BF),
            pltpu.VMEM((width, 384), BF),
            pltpu.VMEM((width, 384), BF),
            pltpu.VMEM(x.shape, F32),
            at_home(width),
            at_tall(width),
            rows(width),
        ]
        + [rows(128)] * 9
        + [at_tall(128), at_home(128), rows(width, F32), rows(128), at_home(128), at_tall(128), at_tall(width), at_home(width)]
        + [pltpu.SemaphoreType.DMA((4, chunks, shares - 1))] * 2,
        compiler_params=pltpu.CompilerParams(
            collective_id=0, has_side_effects=True, vmem_limit_bytes=62 * 2**20
        ),
    )(boxes, drops, partners, inverse, x, cot, vec, wq, wp, w1, w2)


def per_device(
    inputs,
    partners,
    boxes,
    drops,
    norm1_gain,
    norm1_bias,
    qkv_weight,
    lepe_weight,
    lepe_bias,
    proj_weight,
    proj_bias,
    norm2_gain,
    norm2_bias,
    fc1_weight,
    fc1_bias,
    fc2_weight,
    fc2_bias,
    cotangent,
):
    images = inputs.shape[0]
    ids = lax.axis_index("batch") * images + jnp.arange(images)
    inverse = jnp.sum(jnp.where(partners[:, None] == ids[None, :], jnp.arange(images)[:, None], 0), axis=0)
    wide = lambda z: z.astype(F32).reshape(-1, 256)
    taps = jnp.concatenate([lepe_weight[..., :128], lepe_weight.transpose(1, 0, 2)[..., 128:]], axis=-1)
    vec = jnp.concatenate(
        [wide(z) for z in (norm1_gain, norm1_bias, norm2_gain, norm2_bias, proj_bias, fc2_bias, lepe_bias, taps, fc1_bias)]
    )
    vec = jnp.pad(vec, ((0, -vec.shape[0] % 8), (0, 0)))
    out, ig, gw1, gw2t, gqf, gqt, gp, small = block(
        inputs, cotangent, boxes, drops, partners - lax.axis_index("batch") * images, inverse, vec, qkv_weight, proj_weight, fc1_weight, fc2_weight
    )
    small = jnp.sum(small, axis=1)
    gw1, gw2t, gqf, gqt, gp, small = lax.psum((gw1, gw2t, gqf, gqt, gp, small), ("batch", "row"))
    conv = small[CONV : CONV + 9].reshape(3, 3, 256)
    conv = jnp.concatenate([conv[..., :128], conv.transpose(1, 0, 2)[..., 128:]], axis=-1)
    gq = jnp.stack([gqf.reshape(256, 3, 128), gqt.reshape(256, 3, 128)], axis=2).reshape(256, 768)
    return (
        out.reshape(inputs.shape),
        ig.reshape(inputs.shape),
        small[G1],
        small[B1],
        gq,
        conv,
        small[CB],
        gp,
        small[PB],
        small[G2],
        small[B2],
        gw1[:256],
        gw1[256],
        gw2t.T,
        small[FB2],
    )


def solution(mesh):
    tokens = P("batch", "row", None, None)
    return jax.shard_map(
        per_device,
        mesh=mesh,
        in_specs=(tokens, P("batch"), P("batch", None), P("batch", None)) + (P(),) * 13 + (tokens,),
        out_specs=(tokens, tokens) + (P(),) * 13,
        check_vma=False,
    )
```

```python
import functools
import math

import jax
import jax.numpy as jnp
from jax import lax
from jax.experimental import pallas as pl
from jax.experimental.pallas import tpu as pltpu
from jax.sharding import PartitionSpec as P

F32 = jnp.float32
BF = jnp.bfloat16
EPS = 1e-5
SCALE = 32**-0.5
LOG2E = math.log2(math.e)
ERF_P = 0.3275911 / math.sqrt(2.0)
ERF_C = [0.5 * c for c in (0.254829592, -0.284496736, 1.421413741, -1.453152027, 1.061405429)]
G1, B1, G2, B2, PB, FB2, CB, CONV, FB1 = 0, 1, 2, 3, 4, 5, 6, 7, 16
N1, AT, DA, DN = 0, 1, 2, 3


def dot(a, b, ca=1, cb=0):
    return lax.dot_general(a, b, (((ca,), (cb,)), ((), ())), preferred_element_type=F32)


def gelu_parts(v):
    t = 1.0 / (1.0 + ERF_P * jnp.abs(v))
    e = jnp.exp2(v * v * (-0.5 * LOG2E))
    poly = ERF_C[4]
    for c in ERF_C[3::-1]:
        poly = poly * t + c
    h = poly * t * e
    cdf = jnp.where(v >= 0.0, 1.0 - h, h)
    return v * cdf, cdf + v * (e * (1.0 / math.sqrt(2.0 * math.pi)))


def normalise(x):
    center = x - jnp.mean(x, axis=-1, keepdims=True)
    rstd = lax.rsqrt(jnp.mean(center * center, axis=-1, keepdims=True) + EPS)
    return center * rstd, rstd


def normalise_back(d, u, rstd, gain):
    e = d * gain
    m1 = jnp.mean(e, axis=-1, keepdims=True)
    m2 = jnp.mean(e * u, axis=-1, keepdims=True)
    return (e - m1 - u * m2) * rstd


def sum8(x):
    n, c = x.shape
    return jnp.sum(x.reshape(n // 8, 8, c), axis=0)


def split_heads(w, lm):
    return [w * lm[h : h + 1] for h in range(4)]


def skewed(parts, w):
    return jnp.concatenate([parts[j ^ w] for j in range(4)], axis=0)


def stacked(parts, j):
    return jnp.concatenate([parts[w][j ^ w] for w in range(4)], axis=0)


def unskew(o, w, lane):
    r = o[w]
    for h in (1, 2, 3):
        r = jnp.where(lane >= 32 * h, o[h ^ w], r)
    return r


def four(x):
    return [x[32 * w : 32 * w + 32] for w in range(4)]


def attend_group(q, k, v, lm, lane):
    ps = []
    for w, (qw, kw) in enumerate(zip(four(q), four(k))):
        st = dot(kw, skewed(split_heads(qw, lm), w), 1, 1)
        top = jnp.max(st, axis=0, keepdims=True)
        e = jnp.exp2((st - top) * (SCALE * LOG2E))
        ps.append((e * (1.0 / jnp.sum(e, axis=0, keepdims=True))).astype(BF))
    p = jnp.concatenate(ps, axis=0)
    pt = four(p.T)
    vh = [split_heads(vw, lm) for vw in four(v)]
    o = [dot(pt[j], stacked(vh, j)) for j in range(4)]
    return p, jnp.concatenate([unskew(o, w, lane) for w in range(4)], axis=0)


def attend_group_back(q, k, v, p, da, lm, lane):
    dss, dks, dvs = [], [], []
    for w, (qw, vw, pw, dw) in enumerate(zip(four(q), four(v), four(p), four(da))):
        dx = skewed(split_heads(dw, lm), w)
        dp = dot(vw, dx, 1, 1)
        pr = pw.astype(F32)
        t = pr * dp
        ds = (t - pr * jnp.sum(t, axis=0, keepdims=True)).astype(BF)
        dss.append(ds)
        dvs.append(dot(pw, dx))
        dks.append(dot(ds, skewed(split_heads(qw, lm), w)))
    dst = four(jnp.concatenate(dss, axis=0).T)
    kh = [split_heads(kw, lm) for kw in four(k)]
    o = [dot(dst[j], stacked(kh, j)) for j in range(4)]
    dq = jnp.concatenate([unskew(o, w, lane) for w in range(4)], axis=0)
    return dq, jnp.concatenate(dks, axis=0), jnp.concatenate(dvs, axis=0)


def shifts(a):
    n = a.shape[0]
    pos = lax.broadcasted_iota(jnp.int32, a.shape, 0) % 16
    return {
        -1: jnp.where(pos == 0, 0.0, pltpu.roll(a, 1, 0)),
        0: a,
        1: jnp.where(pos == 15, 0.0, pltpu.roll(a, n - 1, 0)),
    }


def lines(a):
    n, c = a.shape
    b = a.reshape(n // 32, 2, 16, c)
    return b[:, 0].reshape(n // 2, c), b[:, 1].reshape(n // 2, c)


def woven(a0, a1):
    n, c = a0.shape
    return jnp.stack([a0.reshape(n // 16, 16, c), a1.reshape(n // 16, 16, c)], axis=1).reshape(2 * n, c)


def attend_half(s, lm, taps, shift):
    tokens = s["q"].shape[0]
    lane = lax.broadcasted_iota(jnp.int32, (32, 128), 1)
    out = []
    for g in range(tokens // 128):
        rows = slice(128 * g, 128 * g + 128)
        p, o = attend_group(s["q"][rows], s["k"][rows], s["v"][rows], lm, lane)
        s["p"][rows] = p
        out.append(o)
    tap = lambda i, j: taps[3 * (i + 1) + j + 1][None]
    near = {j: lines(z) for j, z in shifts(s["v"][...].astype(F32)).items()}
    line = lambda i, n: sum(near[j][n] * tap(i, j) for j in (-1, 0, 1))
    lepe = woven(line(0, 0) + line(1, 1), line(0, 1) + line(-1, 0))
    return (jnp.concatenate(out, axis=0) + (lepe + shift)).astype(BF)


def attend_half_back(s, lm, taps, small, cols):
    tokens = s["q"].shape[0]
    lane = lax.broadcasted_iota(jnp.int32, (32, 128), 1)
    parts = []
    for g in range(tokens // 128):
        rows = slice(128 * g, 128 * g + 128)
        parts.append(attend_group_back(s["q"][rows], s["k"][rows], s["v"][rows], s["p"][rows], s["da"][rows], lm, lane))
    dq, dk, dv = (jnp.concatenate(z, axis=0) for z in zip(*parts))
    tap = lambda i, j: taps[3 * (i + 1) + j + 1][None]
    da = s["da"][...].astype(F32)
    small[CB, :, cols] += sum8(da)
    moved = {-j: lines(z) for j, z in shifts(da).items()}
    v0, v1 = lines(s["v"][...].astype(F32))
    line = lambda i, n: sum(moved[j][n] * tap(i, j) for j in (-1, 0, 1))
    dv = dv + woven(line(0, 0) + line(-1, 1), line(1, 0) + line(0, 1))
    for j in (-1, 0, 1):
        m0, m1 = moved[j]
        small[CONV + 3 + j + 1, :, cols] += sum8(m0 * v0 + m1 * v1)
        small[CONV + 6 + j + 1, :, cols] += sum8(m0 * v1)
        small[CONV + 0 + j + 1, :, cols] += sum8(m1 * v0)
    return jnp.concatenate([(dq * SCALE).astype(BF), (dk * SCALE).astype(BF), dv.astype(BF)], axis=1)


class Exchange:
    def __init__(self, me, shares, send_sem, recv_sem):
        self.me, self.shares, self.send_sem, self.recv_sem = me, shares, send_sem, recv_sem

    def copy(self, kind, c, d, src, dst, arriving):
        to = lax.rem(self.me + d, self.shares)
        far = lax.rem(self.me + self.shares - d, self.shares) if arriving else self.me
        if kind in (N1, DA):
            source, target = src.at[c, to], dst.at[c, :, far]
        else:
            source, target = src.at[c, :, to], dst.at[c, far]
        return pltpu.make_async_remote_copy(
            src_ref=source,
            dst_ref=target,
            send_sem=self.send_sem.at[kind, c, d - 1],
            recv_sem=self.recv_sem.at[kind, c, d - 1],
            device_id={"row": to},
            device_id_type=pl.DeviceIdType.MESH,
        )

    def send(self, kind, c, src, dst):
        me = self.me
        if kind in (N1, DA):
            dst[c, :, me] = src[c, me]
        else:
            dst[c, me] = src[c, :, me]
        for d in range(1, self.shares):
            self.copy(kind, c, d, src, dst, False).start()

    def receive(self, kind, c, src, dst):
        for d in range(1, self.shares):
            self.copy(kind, c, d, src, dst, True).wait_recv()

    def sent(self, kind, c, src, dst):
        for d in range(1, self.shares):
            self.copy(kind, c, d, src, dst, False).wait_send()


class Reduce:
    def __init__(self, group, me, mb, shares, stage, whole, r1, r2, r3, z, send_sem, recv_sem):
        self.whole = whole
        self.group, self.me, self.mb, self.shares = group, me, mb, shares
        self.stage, self.r1, self.r2, self.r3, self.z = stage, r1, r2, r3, z
        self.send_sem, self.recv_sem = send_sem, recv_sem
        self.core = lax.rem(me, 2)
        self.batch = stage.shape[1]

    def copy(self, slot, src, dst, device):
        return pltpu.make_async_remote_copy(
            src_ref=src,
            dst_ref=dst,
            send_sem=self.send_sem.at[self.group, slot],
            recv_sem=self.recv_sem.at[self.group, slot],
            device_id=device,
            device_id_type=pl.DeviceIdType.MESH,
        )

    def near(self):
        mate = {"row": self.me + 1 - 2 * self.core}
        return self.copy(0, self.stage.at[1 - self.core], self.r1, mate)

    def across(self):
        return self.copy(1, self.z, self.r3, {"row": lax.rem(self.me + 2, self.shares)})

    def back(self, arriving):
        mate = {"row": self.me + 1 - 2 * self.core}
        half = 1 - self.core if arriving else self.core
        return self.copy(2, self.whole.at[self.core], self.whole.at[half], mate)

    def peers(self, body):
        def one(d, _):
            body(d, lax.rem(self.mb + d, self.batch), lax.rem(self.mb + self.batch - d, self.batch))
            return 0

        lax.fori_loop(1, self.batch, one, 0)

    def scatter(self, d, to, far):
        return self.copy(2 + d, self.stage.at[self.core, to], self.r2.at[far], {"batch": to})

    def gather(self, d, to, far):
        return self.copy(1 + self.batch + d, self.whole.at[self.core, self.mb], self.whole.at[self.core, far], {"batch": to})

    def step(self, n):
        core, mb = self.core, self.mb
        if n == 0:
            self.near().start()
        if n == 1:
            self.near().wait_recv()

            def add(b, _):
                self.stage[core, b] = (self.stage[core, b].astype(F32) + self.r1[b].astype(F32)).astype(BF)
                return 0

            lax.fori_loop(0, self.batch, add, 0)
            self.peers(lambda d, to, far: self.scatter(d, to, mb).start())
        if n == 2:
            self.peers(lambda d, to, far: self.scatter(d, to, far).wait_recv())

            def more(d, total):
                return total + self.r2[lax.rem(mb + d, self.batch)].astype(F32)

            self.z[...] = lax.fori_loop(1, self.batch, more, self.stage[core, mb].astype(F32)).astype(BF)
            self.across().start()
        if n == 3:
            self.across().wait_recv()
            self.whole[core, mb] = (self.z[...].astype(F32) + self.r3[...].astype(F32)).astype(BF)
            self.peers(lambda d, to, far: self.gather(d, to, mb).start())
        if n == 4:
            self.peers(lambda d, to, far: self.gather(d, to, far).wait_recv())
            self.back(False).start()
        if n == 5:
            self.back(True).wait_recv()
            self.near().wait_send()
            self.across().wait_send()
            self.back(False).wait_send()
            self.peers(lambda d, to, far: self.scatter(d, to, mb).wait_send())
            self.peers(lambda d, to, far: self.gather(d, to, mb).wait_send())


def block_kernel(
    shares,
    ahead,
    boxes_ref,
    drops_ref,
    index_ref,
    x_ref,
    cot_ref,
    norm1_gain,
    norm1_bias,
    norm2_gain,
    norm2_bias,
    proj_bias,
    fc2_bias,
    lepe_bias,
    lepe_weight,
    fc1_bias,
    wq,
    wp,
    w1,
    w2,
    out,
    ig,
    whole1,
    whole2,
    stage1,
    stage2,
    boxes,
    drops,
    index,
    vec,
    gw1,
    gb1,
    gw2t,
    gq,
    gp,
    small,
    perm_ref,
    wf_ref,
    wt_ref,
    mixed,
    n1h,
    n1t,
    n1p,
    qf,
    kf,
    vf,
    pf,
    qt,
    kt,
    vt,
    pt,
    att_f,
    att_ts,
    att_th,
    dh1,
    da_f,
    da_ts,
    da_tt,
    dn_ts,
    dn_th,
    r11,
    r12,
    r13,
    z1,
    r21,
    r22,
    r23,
    z2,
    send_sem,
    recv_sem,
    sum_send,
    sum_recv,
    load_sem,
    store_sem,
):
    chunks, _, pair, strip = n1h.shape[:4]
    images = x_ref.shape[0]
    mine = images // shares
    tokens = shares * pair * strip
    me = lax.axis_index("row")
    ex = Exchange(me, shares, send_sem, recv_sem)

    mb = lax.axis_index("batch")
    batch = stage1.shape[1]
    red1 = Reduce(0, me, mb, shares, stage1, whole1, r11, r12, r13, z1, sum_send, sum_recv)
    red2 = Reduce(1, me, mb, shares, stage2, whole2, r21, r22, r23, z2, sum_send, sum_recv)

    loads = [
        pltpu.make_async_copy(src, dst, load_sem.at[n])
        for n, (src, dst) in enumerate(((boxes_ref, boxes), (drops_ref, drops), (index_ref, index)))
    ]
    for load in loads:
        load.start()
    barrier = pltpu.get_barrier_semaphore()
    for d in range(1, shares):
        pl.semaphore_signal(
            barrier, inc=1, device_id={"row": lax.rem(me + d, shares)}, device_id_type=pl.DeviceIdType.MESH
        )

    def greet(d, _):
        pl.semaphore_signal(
            barrier, inc=1, device_id={"batch": lax.rem(mb + d, batch)}, device_id_type=pl.DeviceIdType.MESH
        )
        return 0

    lax.fori_loop(1, batch, greet, 0)
    pl.semaphore_wait(barrier, shares + batch - 2)
    for load in loads:
        load.wait()

    params = (norm1_gain, norm1_bias, norm2_gain, norm2_bias, proj_bias, fc2_bias, lepe_bias)
    for n, ref in enumerate(params):
        vec[n : n + 1] = ref[...].astype(F32).reshape(1, 256)
    for i in range(3):
        for j in range(3):
            n = CONV + 3 * i + j
            vec[n : n + 1, :128] = lepe_weight[i, j : j + 1, :128].astype(F32)
            vec[n : n + 1, 128:] = lepe_weight[j, i : i + 1, 128:].astype(F32)
    for n in range(4):
        vec[FB1 + n : FB1 + n + 1] = fc1_bias[256 * n : 256 * n + 256].astype(F32).reshape(1, 256)
    v = lambda i: vec[i : i + 1]
    lm = (
        lax.broadcasted_iota(jnp.int32, (8, 128), 0) == lax.broadcasted_iota(jnp.int32, (8, 128), 1) // 32
    ).astype(F32).astype(BF)
    to_row = lax.broadcasted_iota(jnp.int32, (256, 256), 0)
    to_col = lax.broadcasted_iota(jnp.int32, (256, 256), 1)
    perm_ref[...] = jnp.where((to_row % 16) * 16 + to_row // 16 == to_col, 1.0, 0.0).astype(BF)
    for ref in (gw1, gb1, gw2t, gq, gp, small):
        ref[...] = jnp.zeros_like(ref)
    for part in range(3):
        cols = slice(128 * part, 128 * part + 128)
        wf_ref[:, cols] = wq[:, 256 * part : 256 * part + 128]
        wt_ref[:, cols] = wq[:, 256 * part + 128 : 256 * part + 256]
    taps = [vec[CONV + i] for i in range(9)]
    taps_f = [z[:128] for z in taps]
    taps_t = [z[128:] for z in taps]

    spot = lax.broadcasted_iota(jnp.int32, (strip, 1), 0)
    grid_row = me * (strip // 16) + spot // 16
    grid_col = spot % 16

    def shares_of(image):
        inside = (
            (grid_row >= boxes[image, 0])
            & (grid_row < boxes[image, 1])
            & (grid_col >= boxes[image, 2])
            & (grid_col < boxes[image, 3])
        )
        return jnp.where(inside, 0.0, 0.7), jnp.where(inside, 1.0, 0.3)

    def home(c):
        return [(q, i, mine * q + pair * c + i) for q in range(shares) for i in range(pair)]

    def permute(value):
        whole = perm_ref[...]
        return jnp.concatenate(
            [dot(whole, value[256 * i : 256 * i + 256]).astype(BF) for i in range(pair)], axis=0
        )

    def keep(c, j):
        return jnp.concatenate(
            [jnp.full((strip, 1), drops[image, j].astype(F32) * 1.25) for _, _, image in home(c)], axis=0
        )

    def half(c, tall):
        refs = (qt, kt, vt, pt) if tall else (qf, kf, vf, pf)
        return dict(zip("qkvp", [r.at[c] for r in refs]))

    def mix(c, _):
        for q, i, image in home(c):
            own, other = shares_of(image)
            m = own * x_ref[image].astype(F32) + other * x_ref[index[0, image]].astype(F32)
            mixed[image] = m
            u, _ = normalise(m)
            n1h[c, q, i] = (u * v(G1) + v(B1)).astype(BF)
        ex.send(N1, c, n1h, n1t)
        return 0

    def flat(c, _):
        qkv = dot(n1h[c].reshape(tokens, 256), wf_ref[...]).astype(BF)
        qf[c], kf[c], vf[c] = qkv[:, :128], qkv[:, 128:256], qkv[:, 256:]
        att_f[c] = attend_half(half(c, False), lm, taps_f, vec[CB : CB + 1, :128])
        return 0

    def tall(c, _):
        ex.receive(N1, c, n1h, n1t)
        n1 = permute(n1t[c].reshape(tokens, 256))
        n1p[c] = n1
        qkv = dot(n1, wt_ref[...]).astype(BF)
        qt[c], kt[c], vt[c] = qkv[:, :128], qkv[:, 128:256], qkv[:, 256:]
        att = attend_half(half(c, True), lm, taps_t, vec[CB : CB + 1, 128:])
        att_ts[c] = permute(att).reshape(att_ts.shape[1:])
        ex.send(AT, c, att_ts, att_th)
        return 0

    def mlp(c, _):
        ex.receive(AT, c, att_ts, att_th)
        keep1, keep2 = keep(c, 0), keep(c, 1)
        att = jnp.concatenate([att_f[c], att_th[c].reshape(tokens, 128)], axis=1)
        m = jnp.concatenate([mixed[image] for _, _, image in home(c)], axis=0)
        h1 = m + keep1 * (dot(att, wp[...]) + v(PB))
        u2, rstd2 = normalise(h1)
        n2 = (u2 * v(G2) + v(B2)).astype(BF)
        cot = jnp.concatenate([cot_ref[image] for _, _, image in home(c)], axis=0).astype(F32)
        db2 = (keep2 * cot).astype(BF)
        small[FB2] += sum8(db2.astype(F32))
        n2t = jnp.concatenate([n2.T, jnp.ones((16, tokens), BF)], axis=0)
        db2t = db2.T
        branch2 = jnp.zeros((tokens, 256), F32)
        dn2 = jnp.zeros((tokens, 256), F32)
        for f in range(w1.shape[1] // 256):
            fs = slice(256 * f, 256 * f + 256)
            act, slope = gelu_parts(dot(n2, w1[:, fs]) + v(FB1 + f))
            act = act.astype(BF)
            dpre = (slope * dot(db2, w2[fs, :], 1, 1)).astype(BF)
            branch2 = branch2 + dot(act, w2[fs, :])
            dn2 = dn2 + dot(dpre, w1[:, fs], 1, 1)
            grad = dot(n2t, dpre)
            gw1[:, fs] += grad[:256]
            gb1[:, fs] += grad[256:]
            gw2t[:, fs] += dot(db2t, act)
        done = (h1 + keep2 * (branch2 + v(FB2))).astype(BF)
        for n, (_, _, image) in enumerate(home(c)):
            out[image] = done[strip * n : strip * n + strip]
        small[G2] += sum8(dn2 * u2)
        small[B2] += sum8(dn2)
        d = cot + normalise_back(dn2, u2, rstd2, v(G2))
        dh1[c] = d
        db1 = (keep1 * d).astype(BF)
        small[PB] += sum8(db1.astype(F32))
        gp[...] += dot(att, db1, 0, 0)
        datt = dot(db1, wp[...], 1, 1).astype(BF)
        da_f[c] = datt[:, :128]
        da_ts[c] = datt[:, 128:].reshape(da_ts.shape[1:])
        ex.send(DA, c, da_ts, da_tt)
        return 0

    def add_qkv(grad, start):
        for part in range(3):
            cols = slice(256 * part + start, 256 * part + start + 128)
            gq[:, cols] += grad[:, 128 * part : 128 * part + 128]

    def put(stage, blocks):
        rows = stage.shape[2]
        spot = 0
        for value in blocks:
            done = 0
            while done < value.shape[0]:
                piece, at = divmod(spot, rows)
                n = min(rows - at, value.shape[0] - done)
                stage[piece // batch, piece % batch, at : at + n] = value[done : done + n]
                done += n
                spot += n
        while spot < 2 * batch * rows:
            piece, at = divmod(spot, rows)
            stage[piece // batch, piece % batch, at:] = jnp.zeros((rows - at, 256), BF)
            spot += rows - at

    def pack1():
        quarters = [slice(256 * f, 256 * f + 256) for f in range(w1.shape[1] // 256)]
        blocks = [gw1[:, fs].astype(BF) for fs in quarters]
        blocks += [gw2t[:, fs].astype(BF).T for fs in quarters]
        put(stage1, blocks + [gp[...].astype(BF)])

    def pack2():
        blocks = [gq[:, 256 * n : 256 * n + 256].astype(BF) for n in range(3)]
        row = lambda i: jnp.sum(small[i], axis=0, keepdims=True)
        rows = [row(i) for i in range(CONV)]
        conv = [row(CONV + i) for i in range(9)]
        for i in range(3):
            for j in range(3):
                rows.append(jnp.concatenate([conv[3 * i + j][:, :128], conv[3 * j + i][:, 128:]], axis=1))
        rows += [gb1[0:1, 256 * f : 256 * f + 256] for f in range(w1.shape[1] // 256)]
        rows.append(jnp.zeros((32 - len(rows), 256), F32))
        put(stage2, blocks + [jnp.concatenate(rows, axis=0).astype(BF)])

    def tall_back(c, _):
        ex.receive(DA, c, da_ts, da_tt)
        da = permute(da_tt[c].reshape(tokens, 128))
        s = dict(half(c, True), da=da)
        dqkv = attend_half_back(s, lm, taps_t, small, slice(128, 256))
        add_qkv(dot(n1p[c], dqkv, 0, 0), 128)
        dn_ts[c] = permute(dot(dqkv, wt_ref[...], 1, 1).astype(BF)).reshape(dn_ts.shape[1:])
        ex.send(DN, c, dn_ts, dn_th)
        return 0

    def flat_back(c, _):
        s = dict(half(c, False), da=da_f.at[c])
        dqkv = attend_half_back(s, lm, taps_f, small, slice(0, 128))
        add_qkv(dot(n1h[c].reshape(tokens, 256), dqkv, 0, 0), 0)
        dn1 = dot(dqkv, wf_ref[...], 1, 1)
        ex.receive(DN, c, dn_ts, dn_th)
        dn1 = dn1 + dn_th[c].reshape(tokens, 256).astype(F32)
        m = jnp.concatenate([mixed[image] for _, _, image in home(c)], axis=0)
        u1, rstd1 = normalise(m)
        small[G1] += sum8(dn1 * u1)
        small[B1] += sum8(dn1)
        d = dh1[c] + normalise_back(dn1, u1, rstd1, v(G1))
        for n, (_, _, image) in enumerate(home(c)):
            mixed[image] = d[strip * n : strip * n + strip]
        return 0

    def stores(c):
        return [
            pltpu.make_async_copy(n1h.at[c, q], ig.at[pl.ds(mine * q + pair * c, pair)], store_sem.at[c, q])
            for q in range(shares)
        ]

    def unmix(c, _):
        ex.sent(N1, c, n1h, n1t)
        for q, i, image in home(c):
            other = index[1, image]
            n1h[c, q, i] = (shares_of(image)[0] * mixed[image] + shares_of(other)[1] * mixed[other]).astype(BF)
        for store in stores(c):
            store.start()
        return 0

    lax.fori_loop(0, chunks, mix, 0)
    lax.fori_loop(0, chunks, flat, 0)
    lax.fori_loop(0, ahead, tall, 0)

    def forward(c, _):
        @pl.when(c < chunks - ahead)
        def _():
            tall(c + ahead, 0)

        mlp(c, 0)
        return 0

    lax.fori_loop(0, chunks, forward, 0)
    pack1()
    red1.step(0)
    lax.fori_loop(0, ahead, tall_back, 0)
    red1.step(1)

    def backward(c, _):
        @pl.when(c < chunks - ahead)
        def _():
            tall_back(c + ahead, 0)

        flat_back(c, 0)
        for n, at in ((2, chunks // 2), (3, chunks // 2 + 1)):

            @pl.when(c == at)
            def _():
                red1.step(n)

        return 0

    lax.fori_loop(0, chunks, backward, 0)
    pack2()
    red2.step(0)
    red1.step(4)
    red2.step(1)
    lax.fori_loop(0, chunks, unmix, 0)
    red2.step(2)
    red1.step(5)
    red2.step(3)
    red2.step(4)
    red2.step(5)

    def drain(c, _):
        for kind, src, dst in ((AT, att_ts, att_th), (DA, da_ts, da_tt), (DN, dn_ts, dn_th)):
            ex.sent(kind, c, src, dst)
        for store in stores(c):
            store.wait()
        return 0

    lax.fori_loop(0, chunks, drain, 0)


def share_rows(rows, batch):
    return -(-rows // (2 * batch * 16)) * 16


def block(inputs, cotangent, boxes, drops, index, vectors, weights, pair=2, ahead=2):
    images, grid_rows, side, width = inputs.shape
    shares, batch = lax.axis_size("row"), lax.axis_size("batch")
    strip = grid_rows * side
    chunks = images // shares // pair
    tokens = shares * pair * strip
    hidden = weights[2].shape[1]
    sds = jax.ShapeDtypeStruct
    vmem = pl.BlockSpec(memory_space=pltpu.VMEM)
    hbm = pl.BlockSpec(memory_space=pl.ANY)
    x = inputs.reshape(images, strip, width)
    cot = cotangent.reshape(images, strip, width)
    n1 = share_rows(2 * hidden + width, batch)
    n2 = share_rows(3 * width + 32, batch)
    rows = lambda ch, dt=BF: pltpu.VMEM((chunks, tokens, ch), dt)
    at_home = lambda ch: pltpu.VMEM((chunks, shares, pair, strip, ch), BF)
    at_tall = lambda ch: pltpu.VMEM((chunks, pair, shares, strip, ch), BF)
    part = lambda n, *lead: pltpu.VMEM((*lead, n, width), BF)
    return pl.pallas_call(
        functools.partial(block_kernel, shares, ahead),
        in_specs=[hbm] * 3 + [vmem] * (2 + len(vectors) + len(weights)),
        out_specs=[vmem, hbm, vmem, vmem],
        out_shape=[
            sds(x.shape, BF),
            sds(x.shape, BF),
            sds((2, batch, n1, width), BF),
            sds((2, batch, n2, width), BF),
        ],
        scratch_shapes=[
            pltpu.VMEM((2, batch, n1, width), BF),
            pltpu.VMEM((2, batch, n2, width), BF),
            pltpu.SMEM(boxes.shape, jnp.int32),
            pltpu.SMEM(drops.shape, jnp.int32),
            pltpu.SMEM(index.shape, jnp.int32),
            pltpu.VMEM((24, width), F32),
            pltpu.VMEM((width, hidden), F32),
            pltpu.VMEM((16, hidden), F32),
            pltpu.VMEM((width, hidden), F32),
            pltpu.VMEM((width, 3 * width), F32),
            pltpu.VMEM((width, width), F32),
            pltpu.VMEM((16, 8, width), F32),
            pltpu.VMEM((256, 256), BF),
            pltpu.VMEM((width, 384), BF),
            pltpu.VMEM((width, 384), BF),
            pltpu.VMEM(x.shape, F32),
            at_home(width),
            at_tall(width),
            rows(width),
        ]
        + [rows(128)] * 9
        + [at_tall(128), at_home(128), rows(width, F32), rows(128), at_home(128), at_tall(128), at_tall(width), at_home(width)]
        + [part(n1, batch), part(n1, batch), part(n1), part(n1)]
        + [part(n2, batch), part(n2, batch), part(n2), part(n2)]
        + [pltpu.SemaphoreType.DMA((4, chunks, shares - 1))] * 2
        + [pltpu.SemaphoreType.DMA((2, 2 * batch + 1))] * 2
        + [pltpu.SemaphoreType.DMA((3,)), pltpu.SemaphoreType.DMA((chunks, shares))],
        compiler_params=pltpu.CompilerParams(
            collective_id=0, has_side_effects=True, vmem_limit_bytes=63 * 2**20
        ),
    )(boxes, drops, index, x, cot, *vectors, *weights)


def finish_kernel(
    out_ref, ig_ref, sum1, sum2, out, ig, g1, b1, gq, conv, cb, gp, pb, g2, b2, gw1, fb1, gw2, fb2, sems
):
    copies = [pltpu.make_async_copy(out_ref, out, sems.at[0]), pltpu.make_async_copy(ig_ref, ig, sems.at[1])]
    for copy in copies:
        copy.start()
    hidden = gw1.shape[1]
    for f in range(hidden // 256):
        gw1[:, 256 * f : 256 * f + 256] = sum1[256 * f : 256 * f + 256].astype(F32)
    gw2[...] = sum1[hidden : 2 * hidden].astype(F32)
    gp[...] = sum1[2 * hidden : 2 * hidden + 256].astype(F32)
    for f in range(3):
        gq[:, 256 * f : 256 * f + 256] = sum2[256 * f : 256 * f + 256].astype(F32)
    rows = sum2[768:800].astype(F32)
    for n, ref in ((G1, g1), (B1, b1), (G2, g2), (B2, b2), (PB, pb), (FB2, fb2), (CB, cb)):
        ref[...] = rows[n]
    for i in range(3):
        for j in range(3):
            conv[i, j] = rows[CONV + 3 * i + j]
    for f in range(hidden // 256):
        fb1[256 * f : 256 * f + 256] = rows[FB1 + f]
    for copy in copies:
        copy.wait()


def finish(out, ig, sum1, sum2, hidden):
    width = out.shape[-1]
    sds = jax.ShapeDtypeStruct
    vmem = pl.BlockSpec(memory_space=pltpu.VMEM)
    hbm = pl.BlockSpec(memory_space=pl.ANY)
    flat = lambda n: sds((n,), F32)
    square = lambda *n: sds(n, F32)
    shapes = [
        flat(width),
        flat(width),
        square(width, 3 * width),
        square(3, 3, width),
        flat(width),
        square(width, width),
        flat(width),
        flat(width),
        flat(width),
        square(width, hidden),
        flat(hidden),
        square(hidden, width),
        flat(width),
    ]
    return pl.pallas_call(
        finish_kernel,
        in_specs=[hbm, hbm, vmem, vmem],
        out_specs=[hbm, hbm] + [vmem] * len(shapes),
        out_shape=[sds(out.shape, BF), sds(ig.shape, BF)] + shapes,
        scratch_shapes=[pltpu.SemaphoreType.DMA((2,))],
        compiler_params=pltpu.CompilerParams(vmem_limit_bytes=32 * 2**20),
    )(out, ig, sum1.reshape(-1, width), sum2.reshape(-1, width))


def per_device(
    inputs,
    partners,
    boxes,
    drops,
    norm1_gain,
    norm1_bias,
    qkv_weight,
    lepe_weight,
    lepe_bias,
    proj_weight,
    proj_bias,
    norm2_gain,
    norm2_bias,
    fc1_weight,
    fc1_bias,
    fc2_weight,
    fc2_bias,
    cotangent,
):
    images = inputs.shape[0]
    ids = jnp.arange(images)
    local = partners - lax.axis_index("batch") * images
    inverse = jnp.sum(jnp.where(local[:, None] == ids[None, :], ids[:, None], 0), axis=0)
    index = jnp.stack([local, inverse])
    vectors = (norm1_gain, norm1_bias, norm2_gain, norm2_bias, proj_bias, fc2_bias, lepe_bias, lepe_weight, fc1_bias)
    weights = (qkv_weight, proj_weight, fc1_weight, fc2_weight)
    out, ig, sum1, sum2 = block(inputs, cotangent, boxes, drops, index, vectors, weights)
    out, ig, *grads = finish(out, ig, sum1, sum2, fc1_weight.shape[1])
    return (out.reshape(inputs.shape), ig.reshape(inputs.shape), *grads)


def solution(mesh):
    tokens = P("batch", "row", None, None)
    return jax.shard_map(
        per_device,
        mesh=mesh,
        in_specs=(tokens, P("batch"), P("batch", None), P("batch", None)) + (P(),) * 13 + (tokens,),
        out_specs=(tokens, tokens) + (P(),) * 13,
        check_vma=False,
    )
```

```python
import functools
import math

import jax
import jax.numpy as jnp
from jax import lax
from jax.experimental import pallas as pl
from jax.experimental.pallas import tpu as pltpu
from jax.sharding import PartitionSpec as P

F32 = jnp.float32
BF = jnp.bfloat16
EPS = 1e-5
SCALE = 32**-0.5
LOG2E = math.log2(math.e)
SLOPE = 2.0 / math.sqrt(math.pi)
ROOT_HALF = math.sqrt(0.5)
G1, B1, G2, B2, PB, FB2, CB, CONV, FB1 = 0, 1, 2, 3, 4, 5, 6, 7, 16
N1, AT, DA, DN = 0, 1, 2, 3


def dot(a, b, ca=1, cb=0):
    return lax.dot_general(a, b, (((ca,), (cb,)), ((), ())), preferred_element_type=F32)


def gelu_twice(v):
    w = v * ROOT_HALF
    up = 1.0 + lax.erf(w)
    return v * up, up + (w * jnp.exp2(w * w * -LOG2E)) * SLOPE


def normalise(x):
    center = x - jnp.mean(x, axis=-1, keepdims=True)
    rstd = lax.rsqrt(jnp.mean(center * center, axis=-1, keepdims=True) + EPS)
    return center * rstd, rstd


def normalise_back(d, u, rstd, gain):
    e = d * gain
    m1 = jnp.mean(e, axis=-1, keepdims=True)
    m2 = jnp.mean(e * u, axis=-1, keepdims=True)
    return (e - m1 - u * m2) * rstd


def sum8(x):
    n, c = x.shape
    return jnp.sum(x.reshape(n // 8, 8, c), axis=0)


def four(x):
    return [x[32 * w : 32 * w + 32] for w in range(4)]


def masked(x, j, lm):
    return jnp.concatenate([r * lm[b ^ j : (b ^ j) + 1] for b, r in enumerate(four(x))], axis=0)


def spread(x, w, lm):
    return jnp.concatenate([x * lm[j ^ w : (j ^ w) + 1] for j in range(4)], axis=0)


def weave(parts, j, lane):
    r = parts[j]
    for h in (1, 2, 3):
        r = jnp.where(lane >= 32 * h, parts[h ^ j], r)
    return r


def two_dots(a, b):
    r = dot(jnp.concatenate(a, axis=0), jnp.concatenate(b, axis=1))
    n, m = a[0].shape[0], b[0].shape[1]
    return r[:n, :m], r[n:, m:]


def attend_groups(q, k, v, lm, lane):
    n = range(len(q))
    pairs = range(0, len(q), 2)
    qt = [x.T for x in q]
    k4, v4 = [four(x) for x in k], [four(x) for x in v]
    st = [[None] * 4 for _ in n]
    for j in range(4):
        for g in pairs:
            st[g][j], st[g + 1][j] = two_dots(
                [weave(x, j, lane) for x in k4[g : g + 2]], [masked(x, j, lm) for x in qt[g : g + 2]]
            )
    p = [[] for _ in n]
    for g in n:
        for s in st[g]:
            top = jnp.max(s, axis=0, keepdims=True)
            e = jnp.exp2((s - top) * (SCALE * LOG2E))
            p[g].append((e * (1.0 / jnp.sum(e, axis=0, keepdims=True))).astype(BF))
    p = [jnp.concatenate(x, axis=0) for x in p]
    pt = [four(x.T) for x in p]
    o = [[None] * 4 for _ in n]
    for w in range(4):
        for g in pairs:
            o[g][w], o[g + 1][w] = two_dots(
                [x[w] for x in pt[g : g + 2]], [spread(x[w], w, lm) for x in v4[g : g + 2]]
            )
    return p, [jnp.concatenate(x, axis=0) for x in o]


def attend_groups_back(q, k, v, p, da, lm, lane):
    n = range(len(q))
    pairs = range(0, len(q), 2)
    dat = [x.T for x in da]
    v4, k4, p4 = [four(x) for x in v], [four(x) for x in k], [four(x) for x in p]
    ds, dv, dk, dp, dq = ([[None] * 4 for _ in n] for _ in range(5))
    for j in range(4):
        for g in pairs:
            dp[g][j], dp[g + 1][j] = two_dots(
                [weave(x, j, lane) for x in v4[g : g + 2]], [masked(x, j, lm) for x in dat[g : g + 2]]
            )
            dv[g][j], dv[g + 1][j] = two_dots(
                [x[j] for x in p4[g : g + 2]], [masked(x, j, lm) for x in da[g : g + 2]]
            )
    for g in n:
        for j in range(4):
            pr = p4[g][j].astype(F32)
            t = pr * dp[g][j]
            ds[g][j] = (t - pr * jnp.sum(t, axis=0, keepdims=True)).astype(BF)
    dst = [four(jnp.concatenate(x, axis=0).T) for x in ds]
    for j in range(4):
        for g in pairs:
            dk[g][j], dk[g + 1][j] = two_dots(
                [x[j] for x in ds[g : g + 2]], [masked(x, j, lm) for x in q[g : g + 2]]
            )
    for w in range(4):
        for g in pairs:
            dq[g][w], dq[g + 1][w] = two_dots(
                [x[w] for x in dst[g : g + 2]], [spread(x[w], w, lm) for x in k4[g : g + 2]]
            )
    whole = lambda parts: jnp.concatenate([weave(parts, w, lane) for w in range(4)], axis=0)
    return [(jnp.concatenate(dq[g], axis=0), whole(dk[g]), whole(dv[g])) for g in n]


def shifts(a):
    n = a.shape[0]
    pos = lax.broadcasted_iota(jnp.int32, a.shape, 0) % 16
    return {
        -1: jnp.where(pos == 0, 0.0, pltpu.roll(a, 1, 0)),
        0: a,
        1: jnp.where(pos == 15, 0.0, pltpu.roll(a, n - 1, 0)),
    }


def lines(a):
    n, c = a.shape
    b = a.reshape(n // 32, 2, 16, c)
    return b[:, 0].reshape(n // 2, c), b[:, 1].reshape(n // 2, c)


def woven(a0, a1):
    n, c = a0.shape
    return jnp.stack([a0.reshape(n // 16, 16, c), a1.reshape(n // 16, 16, c)], axis=1).reshape(2 * n, c)


def attend_half(s, lm, taps, shift):
    tokens = s["q"].shape[0]
    lane = lax.broadcasted_iota(jnp.int32, (32, 128), 1)
    rows = [slice(128 * n, 128 * n + 128) for n in range(tokens // 128)]
    p, out = attend_groups(*([s[name][r] for r in rows] for name in "qkv"), lm, lane)
    for r, x in zip(rows, p):
        s["p"][r] = x
    tap = lambda i, j: taps[3 * (i + 1) + j + 1][None]
    near = {j: lines(z) for j, z in shifts(s["v"][...].astype(F32)).items()}
    line = lambda i, n: sum(near[j][n] * tap(i, j) for j in (-1, 0, 1))
    lepe = woven(line(0, 0) + line(1, 1), line(0, 1) + line(-1, 0))
    return (jnp.concatenate(out, axis=0) + (lepe + shift)).astype(BF)


def attend_half_back(s, lm, taps, small, cols):
    tokens = s["q"].shape[0]
    lane = lax.broadcasted_iota(jnp.int32, (32, 128), 1)
    rows = [slice(128 * n, 128 * n + 128) for n in range(tokens // 128)]
    parts = attend_groups_back(*([s[name][r] for r in rows] for name in ("q", "k", "v", "p", "da")), lm, lane)
    dq, dk, dv = (jnp.concatenate(z, axis=0) for z in zip(*parts))
    tap = lambda i, j: taps[3 * (i + 1) + j + 1][None]
    da = s["da"][...].astype(F32)
    small[CB, :, cols] += sum8(da)
    moved = {-j: lines(z) for j, z in shifts(da).items()}
    v0, v1 = lines(s["v"][...].astype(F32))
    line = lambda i, n: sum(moved[j][n] * tap(i, j) for j in (-1, 0, 1))
    dv = dv + woven(line(0, 0) + line(-1, 1), line(1, 0) + line(0, 1))
    for j in (-1, 0, 1):
        m0, m1 = moved[j]
        small[CONV + 3 + j + 1, :, cols] += sum8(m0 * v0 + m1 * v1)
        small[CONV + 6 + j + 1, :, cols] += sum8(m0 * v1)
        small[CONV + 0 + j + 1, :, cols] += sum8(m1 * v0)
    return jnp.concatenate([(dq * SCALE).astype(BF), (dk * SCALE).astype(BF), dv.astype(BF)], axis=1)


class Exchange:
    def __init__(self, me, shares, send_sem, recv_sem):
        self.me, self.shares, self.send_sem, self.recv_sem = me, shares, send_sem, recv_sem

    def copy(self, kind, c, d, src, dst, arriving):
        to = lax.rem(self.me + d, self.shares)
        far = lax.rem(self.me + self.shares - d, self.shares) if arriving else self.me
        if kind in (N1, DA):
            source, target = src.at[c, to], dst.at[c, :, far]
        else:
            source, target = src.at[c, :, to], dst.at[c, far]
        return pltpu.make_async_remote_copy(
            src_ref=source,
            dst_ref=target,
            send_sem=self.send_sem.at[kind, c, d - 1],
            recv_sem=self.recv_sem.at[kind, c, d - 1],
            device_id={"row": to},
            device_id_type=pl.DeviceIdType.MESH,
        )

    def send(self, kind, c, src, dst):
        me = self.me
        if kind in (N1, DA):
            dst[c, :, me] = src[c, me]
        else:
            dst[c, me] = src[c, :, me]
        for d in range(1, self.shares):
            self.copy(kind, c, d, src, dst, False).start()

    def receive(self, kind, c, src, dst):
        for d in range(1, self.shares):
            self.copy(kind, c, d, src, dst, True).wait_recv()

    def sent(self, kind, c, src, dst):
        for d in range(1, self.shares):
            self.copy(kind, c, d, src, dst, False).wait_send()


class Reduce:
    def __init__(self, group, me, mb, shares, stage, whole, r1, r2, r3, z, send_sem, recv_sem):
        self.whole = whole
        self.group, self.me, self.mb, self.shares = group, me, mb, shares
        self.stage, self.r1, self.r2, self.r3, self.z = stage, r1, r2, r3, z
        self.send_sem, self.recv_sem = send_sem, recv_sem
        self.core = lax.rem(me, 2)
        self.batch = stage.shape[1]

    def copy(self, slot, src, dst, device):
        return pltpu.make_async_remote_copy(
            src_ref=src,
            dst_ref=dst,
            send_sem=self.send_sem.at[self.group, slot],
            recv_sem=self.recv_sem.at[self.group, slot],
            device_id=device,
            device_id_type=pl.DeviceIdType.MESH,
        )

    def near(self):
        mate = {"row": self.me + 1 - 2 * self.core}
        return self.copy(0, self.stage.at[1 - self.core], self.r1, mate)

    def across(self):
        return self.copy(1, self.z, self.r3, {"row": lax.rem(self.me + 2, self.shares)})

    def back(self, arriving):
        mate = {"row": self.me + 1 - 2 * self.core}
        half = 1 - self.core if arriving else self.core
        return self.copy(2, self.whole.at[self.core], self.whole.at[half], mate)

    def peers(self, body):
        def one(d, _):
            body(d, lax.rem(self.mb + d, self.batch), lax.rem(self.mb + self.batch - d, self.batch))
            return 0

        lax.fori_loop(1, self.batch, one, 0)

    def scatter(self, d, to, far):
        return self.copy(2 + d, self.stage.at[self.core, to], self.r2.at[far], {"batch": to})

    def gather(self, d, to, far):
        return self.copy(1 + self.batch + d, self.whole.at[self.core, self.mb], self.whole.at[self.core, far], {"batch": to})

    def step(self, n):
        core, mb = self.core, self.mb
        if n == 0:
            self.near().start()
        if n == 1:
            self.near().wait_recv()

            def add(b, _):
                self.stage[core, b] = (self.stage[core, b].astype(F32) + self.r1[b].astype(F32)).astype(BF)
                return 0

            lax.fori_loop(0, self.batch, add, 0)
            self.peers(lambda d, to, far: self.scatter(d, to, mb).start())
        if n == 2:
            self.peers(lambda d, to, far: self.scatter(d, to, far).wait_recv())

            def more(d, total):
                return total + self.r2[lax.rem(mb + d, self.batch)].astype(F32)

            self.z[...] = lax.fori_loop(1, self.batch, more, self.stage[core, mb].astype(F32)).astype(BF)
            self.across().start()
        if n == 3:
            self.across().wait_recv()
            self.whole[core, mb] = (self.z[...].astype(F32) + self.r3[...].astype(F32)).astype(BF)
            self.peers(lambda d, to, far: self.gather(d, to, mb).start())
        if n == 4:
            self.peers(lambda d, to, far: self.gather(d, to, far).wait_recv())
            self.back(False).start()
        if n == 5:
            self.back(True).wait_recv()
            self.near().wait_send()
            self.across().wait_send()
            self.back(False).wait_send()
            self.peers(lambda d, to, far: self.scatter(d, to, mb).wait_send())
            self.peers(lambda d, to, far: self.gather(d, to, mb).wait_send())


class Tiny:
    def __init__(self, me, mb, own, row, col, send_sem, recv_sem):
        self.me, self.mb, self.own, self.row, self.col = me, mb, own, row, col
        self.send_sem, self.recv_sem = send_sem, recv_sem
        self.axes = (("row", me, own, row, 0), ("batch", mb, own, col, row.shape[0]))

    def each(self, n, body):
        axis, here, src, dst, base = self.axes[n]
        size = dst.shape[0]

        def one(d, _):
            def copy(arriving):
                at = lax.rem(here + size - d, size) if arriving else here
                return pltpu.make_async_remote_copy(
                    src_ref=src.at[n],
                    dst_ref=dst.at[at],
                    send_sem=self.send_sem.at[base + d],
                    recv_sem=self.recv_sem.at[base + d],
                    device_id={axis: lax.rem(here + d, size)},
                    device_id_type=pl.DeviceIdType.MESH,
                )

            body(copy)
            return 0

        lax.fori_loop(1, size, one, 0)

    def start(self, n, value):
        _, here, src, dst, _ = self.axes[n]
        src[n] = value
        dst[here] = value
        self.each(n, lambda copy: copy(False).start())

    def total(self, n):
        dst = self.axes[n][3]
        self.each(n, lambda copy: copy(True).wait_recv())
        return lax.fori_loop(0, dst.shape[0], lambda i, t: t + dst[i], jnp.zeros(dst.shape[1:], F32))

    def sent(self):
        for n in range(2):
            self.each(n, lambda copy: copy(False).wait_send())


def block_kernel(
    shares,
    ahead,
    early,
    boxes_ref,
    drops_ref,
    partners_ref,
    inverse_ref,
    cot_hbm,
    w1_hbm,
    w2_hbm,
    x_ref,
    norm1_gain,
    norm1_bias,
    norm2_gain,
    norm2_bias,
    proj_bias,
    fc2_bias,
    lepe_bias,
    lepe_weight,
    fc1_bias,
    wq,
    wp,
    out,
    ig,
    whole1,
    whole2,
    last,
    tiny,
    tiny_own,
    tiny_row,
    tiny_col,
    tiny_send,
    tiny_recv,
    cot_ref,
    w1,
    w2,
    out_s,
    stage1,
    stage2,
    boxes,
    drops,
    partners,
    inverse,
    vec,
    gw1,
    gb1,
    gw2t,
    gq,
    gp,
    small,
    perm_ref,
    wf_ref,
    wt_ref,
    mixed,
    n1h,
    n1t,
    n1p,
    qf,
    kf,
    vf,
    pf,
    qt,
    kt,
    vt,
    pt,
    att_f,
    att_ts,
    att_th,
    dh1,
    da_f,
    da_ts,
    da_tt,
    dn_ts,
    dn_th,
    r11,
    r12,
    r13,
    z1,
    r21,
    r22,
    r23,
    z2,
    send_sem,
    recv_sem,
    sum_send,
    sum_recv,
    load_sem,
    store_sem,
):
    chunks, _, pair, strip = n1h.shape[:4]
    images = x_ref.shape[0]
    mine = images // shares
    tokens = shares * pair * strip
    me = lax.axis_index("row")
    ex = Exchange(me, shares, send_sem, recv_sem)

    mb = lax.axis_index("batch")
    batch = stage1.shape[1]
    red1 = Reduce(0, me, mb, shares, stage1, whole1, r11, r12, r13, z1, sum_send, sum_recv)
    red2 = Reduce(1, me, mb, shares, stage2, whole2, r21, r22, r23, z2, sum_send, sum_recv)

    few = Tiny(me, mb, tiny_own, tiny_row, tiny_col, tiny_send, tiny_recv)

    loads = [
        pltpu.make_async_copy(src, dst, load_sem.at[n])
        for n, (src, dst) in enumerate(((boxes_ref, boxes), (drops_ref, drops), (partners_ref, partners), (inverse_ref, inverse)))
    ]
    late = [
        pltpu.make_async_copy(src, dst, load_sem.at[4 + n])
        for n, (src, dst) in enumerate(((cot_hbm, cot_ref), (w1_hbm, w1), (w2_hbm, w2)))
    ]
    for load in loads + late:
        load.start()
    barrier = pltpu.get_barrier_semaphore()
    for d in range(1, shares):
        pl.semaphore_signal(
            barrier, inc=1, device_id={"row": lax.rem(me + d, shares)}, device_id_type=pl.DeviceIdType.MESH
        )

    def greet(d, _):
        pl.semaphore_signal(
            barrier, inc=1, device_id={"batch": lax.rem(mb + d, batch)}, device_id_type=pl.DeviceIdType.MESH
        )
        return 0

    lax.fori_loop(1, batch, greet, 0)
    pl.semaphore_wait(barrier, shares + batch - 2)
    for load in loads:
        load.wait()

    params = (norm1_gain, norm1_bias, norm2_gain, norm2_bias, proj_bias, fc2_bias, lepe_bias)
    for n, ref in enumerate(params):
        vec[n : n + 1] = ref[...].astype(F32).reshape(1, 256)
    for i in range(3):
        for j in range(3):
            n = CONV + 3 * i + j
            vec[n : n + 1, :128] = lepe_weight[i, j : j + 1, :128].astype(F32)
            vec[n : n + 1, 128:] = lepe_weight[j, i : i + 1, 128:].astype(F32)
    for n in range(4):
        vec[FB1 + n : FB1 + n + 1] = fc1_bias[256 * n : 256 * n + 256].astype(F32).reshape(1, 256)
    v = lambda i: vec[i : i + 1]
    lm = (
        lax.broadcasted_iota(jnp.int32, (8, 128), 0) == lax.broadcasted_iota(jnp.int32, (8, 128), 1) // 32
    ).astype(F32).astype(BF)
    to_row = lax.broadcasted_iota(jnp.int32, (256, 256), 0)
    to_col = lax.broadcasted_iota(jnp.int32, (256, 256), 1)
    perm_ref[...] = jnp.where((to_row % 16) * 16 + to_row // 16 == to_col, 1.0, 0.0).astype(BF)
    for ref in (gw1, gb1, gw2t, gq, gp, small, tiny):
        ref[...] = jnp.zeros_like(ref)
    for part in range(3):
        cols = slice(128 * part, 128 * part + 128)
        wf_ref[:, cols] = wq[:, 256 * part : 256 * part + 128]
        wt_ref[:, cols] = wq[:, 256 * part + 128 : 256 * part + 256]
    taps = [vec[CONV + i] for i in range(9)]
    taps_f = [z[:128] for z in taps]
    taps_t = [z[128:] for z in taps]

    spot = lax.broadcasted_iota(jnp.int32, (strip, 1), 0)
    grid_row = me * (strip // 16) + spot // 16
    grid_col = spot % 16

    def shares_of(image):
        inside = (
            (grid_row >= boxes[0, image])
            & (grid_row < boxes[1, image])
            & (grid_col >= boxes[2, image])
            & (grid_col < boxes[3, image])
        )
        return jnp.where(inside, 0.0, 0.7), jnp.where(inside, 1.0, 0.3)

    def home(c):
        return [(q, i, mine * q + pair * c + i) for q in range(shares) for i in range(pair)]

    def permute(value):
        whole = perm_ref[...]
        return jnp.concatenate(
            [dot(whole, value[256 * i : 256 * i + 256]).astype(BF) for i in range(pair)], axis=0
        )

    def keep(c, j):
        return jnp.concatenate(
            [jnp.full((strip, 1), drops[j, image].astype(F32) * 1.25) for _, _, image in home(c)], axis=0
        )

    def half(c, tall):
        refs = (qt, kt, vt, pt) if tall else (qf, kf, vf, pf)
        return dict(zip("qkvp", [r.at[c] for r in refs]))

    def stores(c, src, dst, which):
        return [
            pltpu.make_async_copy(src.at[c, q], dst.at[pl.ds(mine * q + pair * c, pair)], store_sem.at[which, c, q])
            for q in range(shares)
        ]

    def mix(c, _):
        for q, i, image in home(c):
            own, other = shares_of(image)
            m = own * x_ref[image].astype(F32) + other * x_ref[lax.rem(partners[image], images)].astype(F32)
            mixed[image] = m
            u, _ = normalise(m)
            n1h[c, q, i] = (u * v(G1) + v(B1)).astype(BF)
        @pl.when(c < early)
        def _():
            ex.send(N1, c, n1h, n1t)

        return 0

    def flat(c, _):
        qkv = dot(n1h[c].reshape(tokens, 256), wf_ref[...]).astype(BF)
        qf[c], kf[c], vf[c] = qkv[:, :128], qkv[:, 128:256], qkv[:, 256:]
        att_f[c] = attend_half(half(c, False), lm, taps_f, vec[CB : CB + 1, :128])
        return 0

    def tall(c, _):
        ex.receive(N1, c, n1h, n1t)
        n1 = permute(n1t[c].reshape(tokens, 256))
        n1p[c] = n1
        qkv = dot(n1, wt_ref[...]).astype(BF)
        qt[c], kt[c], vt[c] = qkv[:, :128], qkv[:, 128:256], qkv[:, 256:]
        att = attend_half(half(c, True), lm, taps_t, vec[CB : CB + 1, 128:])
        att_ts[c] = permute(att).reshape(att_ts.shape[1:])
        ex.send(AT, c, att_ts, att_th)
        return 0

    def mlp(c, _):
        ex.receive(AT, c, att_ts, att_th)
        keep1, keep2 = keep(c, 0), keep(c, 1)
        att = jnp.concatenate([att_f[c], att_th[c].reshape(tokens, 128)], axis=1)
        m = jnp.concatenate([mixed[image] for _, _, image in home(c)], axis=0)
        h1 = m + keep1 * (dot(att, wp[...]) + v(PB))
        u2, rstd2 = normalise(h1)
        n2 = (u2 * v(G2) + v(B2)).astype(BF)
        cot = jnp.concatenate([cot_ref[image] for _, _, image in home(c)], axis=0).astype(F32)
        db2 = (keep2 * cot).astype(BF)
        small[FB2] += sum8(db2.astype(F32))
        n2t = jnp.concatenate([n2.T, jnp.ones((16, tokens), BF)], axis=0)
        db2t = db2.T
        branch2 = jnp.zeros((tokens, 256), F32)
        dn2 = jnp.zeros((tokens, 256), F32)
        for f in range(w1.shape[1] // 256):
            fs = slice(256 * f, 256 * f + 256)
            act, slope = gelu_twice(dot(n2, w1[:, fs]) + v(FB1 + f))
            act = act.astype(BF)
            dpre = (slope * dot(db2, w2[fs, :], 1, 1)).astype(BF)
            branch2 = branch2 + dot(act, w2[fs, :])
            dn2 = dn2 + dot(dpre, w1[:, fs], 1, 1)
            grad = dot(n2t, dpre)
            gw1[:, fs] += grad[:256]
            gb1[:, fs] += grad[256:]
            gw2t[:, fs] += dot(db2t, act)
        done = (h1 + (0.5 * keep2) * (branch2 + 2.0 * v(FB2))).astype(BF)
        out_s[c] = done.reshape(out_s.shape[1:])
        for store in stores(c, out_s, out, 0):
            store.start()
        small[G2] += sum8(dn2 * u2)
        small[B2] += sum8(dn2)
        d = cot + normalise_back(dn2, u2, rstd2, 0.5 * v(G2))
        dh1[c] = d
        db1 = (keep1 * d).astype(BF)
        small[PB] += sum8(db1.astype(F32))
        gp[...] += dot(att, db1, 0, 0)
        datt = dot(db1, wp[...], 1, 1).astype(BF)
        da_f[c] = datt[:, :128]
        da_ts[c] = datt[:, 128:].reshape(da_ts.shape[1:])
        ex.send(DA, c, da_ts, da_tt)
        return 0

    def add_qkv(grad, start):
        for part in range(3):
            cols = slice(256 * part + start, 256 * part + start + 128)
            gq[:, cols] += grad[:, 128 * part : 128 * part + 128]

    def put(stage, blocks):
        rows = stage.shape[2]
        spot = 0
        for value in blocks:
            done = 0
            while done < value.shape[0]:
                piece, at = divmod(spot, rows)
                n = min(rows - at, value.shape[0] - done)
                stage[piece // batch, piece % batch, at : at + n] = value[done : done + n]
                done += n
                spot += n
        while spot < 2 * batch * rows:
            piece, at = divmod(spot, rows)
            stage[piece // batch, piece % batch, at:] = jnp.zeros((rows - at, 256), BF)
            spot += rows - at

    def pack1():
        quarters = [slice(256 * f, 256 * f + 256) for f in range(w1.shape[1] // 256)]
        blocks = [(0.5 * gw1[:, fs]).astype(BF) for fs in quarters]
        blocks += [(0.5 * gw2t[:, fs]).astype(BF).T for fs in quarters]
        put(stage1, blocks + [gp[...].astype(BF)])

    def pack2():
        blocks = [gq[:, 256 * n : 256 * n + 256].astype(BF) for n in range(3)]
        row = lambda i: jnp.sum(small[i], axis=0, keepdims=True)
        rows = [row(i) * (0.5 if i in (G2, B2) else 1.0) for i in range(CONV)]
        conv = [row(CONV + i) for i in range(9)]
        for i in range(3):
            for j in range(3):
                rows.append(jnp.concatenate([conv[3 * i + j][:, :128], conv[3 * j + i][:, 128:]], axis=1))
        rows += [0.5 * gb1[0:1, 256 * f : 256 * f + 256] for f in range(w1.shape[1] // 256)]
        rows.append(jnp.zeros((32 - len(rows), 256), F32))
        put(stage2, blocks + [jnp.concatenate(rows, axis=0).astype(BF)])

    def tall_back(c, _):
        ex.receive(DA, c, da_ts, da_tt)
        da = permute(da_tt[c].reshape(tokens, 128))
        s = dict(half(c, True), da=da)
        dqkv = attend_half_back(s, lm, taps_t, small, slice(128, 256))
        add_qkv(dot(n1p[c], dqkv, 0, 0), 128)
        dn_ts[c] = permute(dot(dqkv, wt_ref[...], 1, 1).astype(BF)).reshape(dn_ts.shape[1:])
        ex.send(DN, c, dn_ts, dn_th)
        return 0

    def flat_back(c, _):
        s = dict(half(c, False), da=da_f.at[c])
        dqkv = attend_half_back(s, lm, taps_f, small, slice(0, 128))
        ex.sent(N1, c, n1h, n1t)
        add_qkv(dot(n1h[c].reshape(tokens, 256), dqkv, 0, 0), 0)
        n1h[c] = dot(dqkv, wf_ref[...], 1, 1).astype(BF).reshape(n1h.shape[1:])
        return 0

    def norm_back(c, _):
        ex.receive(DN, c, dn_ts, dn_th)
        dn1 = n1h[c].reshape(tokens, 256).astype(F32) + dn_th[c].reshape(tokens, 256).astype(F32)
        m = jnp.concatenate([mixed[image] for _, _, image in home(c)], axis=0)
        u1, rstd1 = normalise(m)
        tiny[0] += sum8(dn1 * u1)
        tiny[1] += sum8(dn1)
        d = dh1[c] + normalise_back(dn1, u1, rstd1, v(G1))
        for n, (_, _, image) in enumerate(home(c)):
            mixed[image] = d[strip * n : strip * n + strip]
        for n, at in ((1, 0), (2, chunks // 3), (3, chunks // 2), (4, chunks - 1)):

            @pl.when(c == at)
            def _():
                red2.step(n)

        return 0

    def unmix(c, _):
        for q, i, image in home(c):
            other = inverse[image]
            n1h[c, q, i] = (shares_of(image)[0] * mixed[image] + shares_of(other)[1] * mixed[other]).astype(BF)
        for store in stores(c, n1h, ig, 1):
            store.start()
        return 0

    lax.fori_loop(0, chunks, mix, 0)
    lax.fori_loop(0, chunks, flat, 0)
    lax.fori_loop(0, ahead, tall, 0)

    def forward(c, _):
        @pl.when(c < chunks - early)
        def _():
            ex.send(N1, c + early, n1h, n1t)

        @pl.when(c < chunks - ahead)
        def _():
            tall(c + ahead, 0)

        mlp(c, 0)
        return 0

    for load in late:
        load.wait()
    lax.fori_loop(0, chunks, forward, 0)
    pack1()
    red1.step(0)
    lax.fori_loop(0, ahead, tall_back, 0)
    red1.step(1)

    def backward(c, _):
        @pl.when(c < chunks - ahead)
        def _():
            tall_back(c + ahead, 0)

        flat_back(c, 0)
        for n, at in ((2, chunks // 2), (3, chunks // 2 + 1)):

            @pl.when(c == at)
            def _():
                red1.step(n)

        return 0

    lax.fori_loop(0, chunks, backward, 0)
    pack2()
    red2.step(0)
    red1.step(4)
    lax.fori_loop(0, chunks, norm_back, 0)
    rows = [jnp.sum(tiny[n], axis=0, keepdims=True) for n in range(2)] + [jnp.zeros((6, 256), F32)]
    few.start(0, jnp.concatenate(rows, axis=0))
    red1.step(5)
    half_way = chunks // 2
    lax.fori_loop(0, half_way, unmix, 0)
    few.start(1, few.total(0))
    lax.fori_loop(half_way, chunks, unmix, 0)
    last[...] = few.total(1)
    few.sent()
    red2.step(5)

    def drain(c, _):
        for kind, src, dst in ((AT, att_ts, att_th), (DA, da_ts, da_tt), (DN, dn_ts, dn_th)):
            ex.sent(kind, c, src, dst)
        for store in stores(c, out_s, out, 0) + stores(c, n1h, ig, 1):
            store.wait()
        return 0

    lax.fori_loop(0, chunks, drain, 0)


def share_rows(rows, batch):
    return -(-rows // (2 * batch * 16)) * 16


def block(inputs, cotangent, boxes, drops, partners, inverse, vectors, weights, pair=2, ahead=2, early=4):
    images, grid_rows, side, width = inputs.shape
    shares, batch = lax.axis_size("row"), lax.axis_size("batch")
    strip = grid_rows * side
    chunks = images // shares // pair
    tokens = shares * pair * strip
    hidden = weights[2].shape[1]
    sds = jax.ShapeDtypeStruct
    vmem = pl.BlockSpec(memory_space=pltpu.VMEM)
    hbm = pl.BlockSpec(memory_space=pl.ANY)
    x = inputs.reshape(images, strip, width)
    cot = cotangent.reshape(images, strip, width)
    n1 = share_rows(2 * hidden + width, batch)
    n2 = share_rows(3 * width + 32, batch)
    rows = lambda ch, dt=BF: pltpu.VMEM((chunks, tokens, ch), dt)
    at_home = lambda ch: pltpu.VMEM((chunks, shares, pair, strip, ch), BF)
    at_tall = lambda ch: pltpu.VMEM((chunks, pair, shares, strip, ch), BF)
    part = lambda n, *lead: pltpu.VMEM((*lead, n, width), BF)
    return pl.pallas_call(
        functools.partial(block_kernel, shares, ahead, early),
        in_specs=[hbm] * 7 + [vmem] * (1 + len(vectors) + 2),
        out_specs=[hbm, hbm, vmem, vmem, vmem],
        out_shape=[
            sds(x.shape, BF),
            sds(x.shape, BF),
            sds((2, batch, n1, width), BF),
            sds((2, batch, n2, width), BF),
            sds((8, width), F32),
        ],
        scratch_shapes=[
            pltpu.VMEM((2, 8, width), F32),
            pltpu.VMEM((2, 8, width), F32),
            pltpu.VMEM((shares, 8, width), F32),
            pltpu.VMEM((batch, 8, width), F32),
            pltpu.SemaphoreType.DMA((shares + batch,)),
            pltpu.SemaphoreType.DMA((shares + batch,)),
            pltpu.VMEM(x.shape, BF),
            pltpu.VMEM(weights[2].shape, BF),
            pltpu.VMEM(weights[3].shape, BF),
            at_home(width),
            pltpu.VMEM((2, batch, n1, width), BF),
            pltpu.VMEM((2, batch, n2, width), BF),
            pltpu.SMEM(boxes.shape, jnp.int32),
            pltpu.SMEM(drops.shape, jnp.int32),
            pltpu.SMEM(partners.shape, jnp.int32),
            pltpu.SMEM(inverse.shape, jnp.int32),
            pltpu.VMEM((24, width), F32),
            pltpu.VMEM((width, hidden), F32),
            pltpu.VMEM((16, hidden), F32),
            pltpu.VMEM((width, hidden), F32),
            pltpu.VMEM((width, 3 * width), F32),
            pltpu.VMEM((width, width), F32),
            pltpu.VMEM((16, 8, width), F32),
            pltpu.VMEM((256, 256), BF),
            pltpu.VMEM((width, 384), BF),
            pltpu.VMEM((width, 384), BF),
            pltpu.VMEM(x.shape, F32),
            at_home(width),
            at_tall(width),
            rows(width),
        ]
        + [rows(128)] * 9
        + [at_tall(128), at_home(128), rows(width, F32), rows(128), at_home(128), at_tall(128), at_tall(width), at_home(width)]
        + [part(n1, batch), part(n1, batch), part(n1), part(n1)]
        + [part(n2, batch), part(n2, batch), part(n2), part(n2)]
        + [pltpu.SemaphoreType.DMA((4, chunks, shares - 1))] * 2
        + [pltpu.SemaphoreType.DMA((2, 2 * batch + 1))] * 2
        + [pltpu.SemaphoreType.DMA((7,)), pltpu.SemaphoreType.DMA((2, chunks, shares))],
        compiler_params=pltpu.CompilerParams(
            collective_id=0, has_side_effects=True, vmem_limit_bytes=63 * 2**20
        ),
    )(boxes, drops, partners, inverse, cot, *weights[2:], x, *vectors, *weights[:2])


def finish_kernel(
    out_ref, ig_ref, sum1, sum2, last, out, ig, g1, b1, gq, conv, cb, gp, pb, g2, b2, gw1, fb1, gw2, fb2, held, sems
):
    third = out.shape[0] // 3
    parts = [(n, pl.ds(third * i, third), 3 * n + i) for i in range(3) for n in range(2)]
    loads = [pltpu.make_async_copy((out_ref, ig_ref)[n].at[rows], held.at[n, rows], sems.at[0, m]) for n, rows, m in parts]
    stores = [pltpu.make_async_copy(held.at[n, rows], (out, ig)[n].at[rows], sems.at[1, m]) for n, rows, m in parts]
    for load in loads:
        load.start()
    for load, store in zip(loads, stores):
        load.wait()
        store.start()
    hidden = gw1.shape[1]
    for f in range(hidden // 256):
        gw1[:, 256 * f : 256 * f + 256] = sum1[256 * f : 256 * f + 256].astype(F32)
    gw2[...] = sum1[hidden : 2 * hidden].astype(F32)
    gp[...] = sum1[2 * hidden : 2 * hidden + 256].astype(F32)
    for f in range(3):
        gq[:, 256 * f : 256 * f + 256] = sum2[256 * f : 256 * f + 256].astype(F32)
    rows = sum2[768:800].astype(F32)
    for n, ref in ((G2, g2), (B2, b2), (PB, pb), (FB2, fb2), (CB, cb)):
        ref[...] = rows[n]
    g1[...], b1[...] = last[0], last[1]
    for i in range(3):
        for j in range(3):
            conv[i, j] = rows[CONV + 3 * i + j]
    for f in range(hidden // 256):
        fb1[256 * f : 256 * f + 256] = rows[FB1 + f]
    for store in stores:
        store.wait()


def finish(out, ig, sum1, sum2, last, hidden):
    width = out.shape[-1]
    sds = jax.ShapeDtypeStruct
    vmem = pl.BlockSpec(memory_space=pltpu.VMEM)
    hbm = pl.BlockSpec(memory_space=pl.ANY)
    flat = lambda n: sds((n,), F32)
    square = lambda *n: sds(n, F32)
    shapes = [
        flat(width),
        flat(width),
        square(width, 3 * width),
        square(3, 3, width),
        flat(width),
        square(width, width),
        flat(width),
        flat(width),
        flat(width),
        square(width, hidden),
        flat(hidden),
        square(hidden, width),
        flat(width),
    ]
    return pl.pallas_call(
        finish_kernel,
        in_specs=[hbm, hbm, vmem, vmem, vmem],
        out_specs=[hbm, hbm] + [vmem] * len(shapes),
        out_shape=[sds(out.shape, BF), sds(ig.shape, BF)] + shapes,
        scratch_shapes=[pltpu.VMEM((2,) + out.shape, BF), pltpu.SemaphoreType.DMA((2, 6))],
        compiler_params=pltpu.CompilerParams(vmem_limit_bytes=62 * 2**20),
    )(out, ig, sum1.reshape(-1, width), sum2.reshape(-1, width), last)


def per_device(
    inputs,
    partners,
    boxes,
    drops,
    norm1_gain,
    norm1_bias,
    qkv_weight,
    lepe_weight,
    lepe_bias,
    proj_weight,
    proj_bias,
    norm2_gain,
    norm2_bias,
    fc1_weight,
    fc1_bias,
    fc2_weight,
    fc2_bias,
    cotangent,
):
    images = inputs.shape[0]
    ids = jnp.arange(images)
    inverse = jnp.sum(jnp.where(partners[:, None] % images == ids[None, :], ids[:, None], 0), axis=0)
    vectors = (norm1_gain, norm1_bias, norm2_gain, norm2_bias, proj_bias, fc2_bias, lepe_bias, lepe_weight, fc1_bias)
    weights = (qkv_weight, proj_weight, fc1_weight, fc2_weight)
    out, ig, sum1, sum2, last = block(inputs, cotangent, boxes.T, drops.T, partners, inverse, vectors, weights)
    out, ig, *grads = finish(out, ig, sum1, sum2, last, fc1_weight.shape[1])
    return (out.reshape(inputs.shape), ig.reshape(inputs.shape), *grads)


def solution(mesh):
    tokens = P("batch", "row", None, None)
    return jax.shard_map(
        per_device,
        mesh=mesh,
        in_specs=(tokens, P("batch"), P("batch", None), P("batch", None)) + (P(),) * 13 + (tokens,),
        out_specs=(tokens, tokens) + (P(),) * 13,
        check_vma=False,
    )
```

```python
import functools
import math

import jax
import jax.numpy as jnp
from jax import lax
from jax.experimental import pallas as pl
from jax.experimental.pallas import tpu as pltpu
from jax.sharding import PartitionSpec as P

F32 = jnp.float32
BF = jnp.bfloat16
EPS = 1e-5
SCALE = 32**-0.5
LOG2E = math.log2(math.e)
SLOPE = 2.0 / math.sqrt(math.pi)
ROOT_HALF = math.sqrt(0.5)
G1, B1, G2, B2, PB, FB2, CB, CONV, FB1 = 0, 1, 2, 3, 4, 5, 6, 7, 16
N1, AT, DA, DN = 0, 1, 2, 3


def dot(a, b, ca=1, cb=0):
    return lax.dot_general(a, b, (((ca,), (cb,)), ((), ())), preferred_element_type=F32)


def gelu_twice(v):
    w = v * ROOT_HALF
    up = 1.0 + lax.erf(w)
    return v * up, up + (w * jnp.exp2(w * w * -LOG2E)) * SLOPE


def normalise(x):
    center = x - jnp.mean(x, axis=-1, keepdims=True)
    rstd = lax.rsqrt(jnp.mean(center * center, axis=-1, keepdims=True) + EPS)
    return center * rstd, rstd


def normalise_back(d, u, rstd, gain):
    e = d * gain
    m1 = jnp.mean(e, axis=-1, keepdims=True)
    m2 = jnp.mean(e * u, axis=-1, keepdims=True)
    return (e - m1 - u * m2) * rstd


def sum8(x):
    n, c = x.shape
    return jnp.sum(x.reshape(n // 8, 8, c), axis=0)


def four(x):
    return [x[32 * w : 32 * w + 32] for w in range(4)]


def masked(x, j, lm):
    return jnp.concatenate([r * lm[b ^ j : (b ^ j) + 1] for b, r in enumerate(four(x))], axis=0)


def spread(x, w, lm):
    return jnp.concatenate([x * lm[j ^ w : (j ^ w) + 1] for j in range(4)], axis=0)


def weave(parts, j, lane):
    r = parts[j]
    for h in (1, 2, 3):
        r = jnp.where(lane >= 32 * h, parts[h ^ j], r)
    return r


def two_dots(a, b):
    r = dot(jnp.concatenate(a, axis=0), jnp.concatenate(b, axis=1))
    n, m = a[0].shape[0], b[0].shape[1]
    return r[:n, :m], r[n:, m:]


def attend_groups(q, k, v, lm, lane):
    n = range(len(q))
    pairs = range(0, len(q), 2)
    qt = [x.T for x in q]
    k4, v4 = [four(x) for x in k], [four(x) for x in v]
    st = [[None] * 4 for _ in n]
    for j in range(4):
        for g in pairs:
            st[g][j], st[g + 1][j] = two_dots(
                [weave(x, j, lane) for x in k4[g : g + 2]], [masked(x, j, lm) for x in qt[g : g + 2]]
            )
    p = [[] for _ in n]
    for g in n:
        for s in st[g]:
            top = jnp.max(s, axis=0, keepdims=True)
            e = jnp.exp2((s - top) * (SCALE * LOG2E))
            p[g].append((e * (1.0 / jnp.sum(e, axis=0, keepdims=True))).astype(BF))
    p = [jnp.concatenate(x, axis=0) for x in p]
    pt = [four(x.T) for x in p]
    o = [[None] * 4 for _ in n]
    for w in range(4):
        for g in pairs:
            o[g][w], o[g + 1][w] = two_dots(
                [x[w] for x in pt[g : g + 2]], [spread(x[w], w, lm) for x in v4[g : g + 2]]
            )
    return p, [jnp.concatenate(x, axis=0) for x in o]


def attend_groups_back(q, k, v, p, da, lm, lane):
    n = range(len(q))
    pairs = range(0, len(q), 2)
    dat = [x.T for x in da]
    v4, k4, p4 = [four(x) for x in v], [four(x) for x in k], [four(x) for x in p]
    ds, dv, dk, dp, dq = ([[None] * 4 for _ in n] for _ in range(5))
    for j in range(4):
        for g in pairs:
            dp[g][j], dp[g + 1][j] = two_dots(
                [weave(x, j, lane) for x in v4[g : g + 2]], [masked(x, j, lm) for x in dat[g : g + 2]]
            )
            dv[g][j], dv[g + 1][j] = two_dots(
                [x[j] for x in p4[g : g + 2]], [masked(x, j, lm) for x in da[g : g + 2]]
            )
    for g in n:
        for j in range(4):
            pr = p4[g][j].astype(F32)
            t = pr * dp[g][j]
            ds[g][j] = (t - pr * jnp.sum(t, axis=0, keepdims=True)).astype(BF)
    dst = [four(jnp.concatenate(x, axis=0).T) for x in ds]
    for j in range(4):
        for g in pairs:
            dk[g][j], dk[g + 1][j] = two_dots(
                [x[j] for x in ds[g : g + 2]], [masked(x, j, lm) for x in q[g : g + 2]]
            )
    for w in range(4):
        for g in pairs:
            dq[g][w], dq[g + 1][w] = two_dots(
                [x[w] for x in dst[g : g + 2]], [spread(x[w], w, lm) for x in k4[g : g + 2]]
            )
    whole = lambda parts: jnp.concatenate([weave(parts, w, lane) for w in range(4)], axis=0)
    return [(jnp.concatenate(dq[g], axis=0), whole(dk[g]), whole(dv[g])) for g in n]


def tiles(a):
    n, c = a.shape
    z = a.reshape(n // 32, 4, 8, c)
    return [z[:, i] for i in range(4)]


def untiled(parts):
    n, _, c = parts[0].shape
    return jnp.stack(parts, axis=1).reshape(32 * n, c)


def shifts(parts):
    row = lax.broadcasted_iota(jnp.int32, parts[0].shape, 1)
    up = [pltpu.roll(p, 1, 1) for p in parts]
    down = [pltpu.roll(p, 7, 1) for p in parts]
    early, late = [], []
    for lo in (0, 2):
        early += [jnp.where(row == 0, 0.0, up[lo]), jnp.where(row == 0, up[lo], up[lo + 1])]
        late += [jnp.where(row == 7, down[lo + 1], down[lo]), jnp.where(row == 7, 0.0, down[lo + 1])]
    return {-1: early, 0: parts, 1: late}


def taps_sum(near, taps, pairs):
    return [
        sum(near[j][2 * line + h] * taps[3 * (i + 1) + j + 1][None, None] for i, line in pairs for j in (-1, 0, 1))
        for h in range(2)
    ]


def attend_half(s, lm, taps, shift):
    tokens = s["q"].shape[0]
    lane = lax.broadcasted_iota(jnp.int32, (32, 128), 1)
    rows = [slice(128 * n, 128 * n + 128) for n in range(tokens // 128)]
    p, out = attend_groups(*([s[name][r] for r in rows] for name in "qkv"), lm, lane)
    for r, x in zip(rows, p):
        s["p"][r] = x
    near = shifts(tiles(s["v"][...].astype(F32)))
    lepe = untiled(taps_sum(near, taps, ((0, 0), (1, 1))) + taps_sum(near, taps, ((0, 1), (-1, 0))))
    return (jnp.concatenate(out, axis=0) + (lepe + shift)).astype(BF)


def attend_half_back(s, lm, taps, small, cols):
    tokens = s["q"].shape[0]
    lane = lax.broadcasted_iota(jnp.int32, (32, 128), 1)
    rows = [slice(128 * n, 128 * n + 128) for n in range(tokens // 128)]
    parts = attend_groups_back(*([s[name][r] for r in rows] for name in ("q", "k", "v", "p", "da")), lm, lane)
    dq, dk, dv = (jnp.concatenate(z, axis=0) for z in zip(*parts))
    da = s["da"][...].astype(F32)
    small[CB, :, cols] += sum8(da)
    moved = {-j: parts for j, parts in shifts(tiles(da)).items()}
    vt = tiles(s["v"][...].astype(F32))
    dv = dv + untiled(taps_sum(moved, taps, ((0, 0), (-1, 1))) + taps_sum(moved, taps, ((1, 0), (0, 1))))
    over = lambda z: jnp.sum(z, axis=0)
    for j in (-1, 0, 1):
        m = moved[j]
        small[CONV + 3 + j + 1, :, cols] += over(m[0] * vt[0] + m[1] * vt[1] + m[2] * vt[2] + m[3] * vt[3])
        small[CONV + 6 + j + 1, :, cols] += over(m[0] * vt[2] + m[1] * vt[3])
        small[CONV + 0 + j + 1, :, cols] += over(m[2] * vt[0] + m[3] * vt[1])
    return jnp.concatenate([(dq * SCALE).astype(BF), (dk * SCALE).astype(BF), dv.astype(BF)], axis=1)


class Exchange:
    def __init__(self, me, shares, send_sem, recv_sem):
        self.me, self.shares, self.send_sem, self.recv_sem = me, shares, send_sem, recv_sem

    def copy(self, kind, c, d, src, dst, arriving):
        to = lax.rem(self.me + d, self.shares)
        far = lax.rem(self.me + self.shares - d, self.shares) if arriving else self.me
        if kind in (N1, DA):
            source, target = src.at[c, to], dst.at[c, :, far]
        else:
            source, target = src.at[c, :, to], dst.at[c, far]
        return pltpu.make_async_remote_copy(
            src_ref=source,
            dst_ref=target,
            send_sem=self.send_sem.at[kind, c, d - 1],
            recv_sem=self.recv_sem.at[kind, c, d - 1],
            device_id={"row": to},
            device_id_type=pl.DeviceIdType.MESH,
        )

    def send(self, kind, c, src, dst):
        me = self.me
        if kind in (N1, DA):
            dst[c, :, me] = src[c, me]
        else:
            dst[c, me] = src[c, :, me]
        for d in range(1, self.shares):
            self.copy(kind, c, d, src, dst, False).start()

    def receive(self, kind, c, src, dst):
        for d in range(1, self.shares):
            self.copy(kind, c, d, src, dst, True).wait_recv()

    def sent(self, kind, c, src, dst):
        for d in range(1, self.shares):
            self.copy(kind, c, d, src, dst, False).wait_send()


class Reduce:
    def __init__(self, group, me, mb, shares, stage, whole, r1, r2, r3, z, send_sem, recv_sem):
        self.whole = whole
        self.group, self.me, self.mb, self.shares = group, me, mb, shares
        self.stage, self.r1, self.r2, self.r3, self.z = stage, r1, r2, r3, z
        self.send_sem, self.recv_sem = send_sem, recv_sem
        self.core = lax.rem(me, 2)
        self.batch = stage.shape[1]

    def copy(self, slot, src, dst, device):
        return pltpu.make_async_remote_copy(
            src_ref=src,
            dst_ref=dst,
            send_sem=self.send_sem.at[self.group, slot],
            recv_sem=self.recv_sem.at[self.group, slot],
            device_id=device,
            device_id_type=pl.DeviceIdType.MESH,
        )

    def near(self):
        mate = {"row": self.me + 1 - 2 * self.core}
        return self.copy(0, self.stage.at[1 - self.core], self.r1, mate)

    def across(self):
        return self.copy(1, self.z, self.r3, {"row": lax.rem(self.me + 2, self.shares)})

    def back(self, arriving):
        mate = {"row": self.me + 1 - 2 * self.core}
        half = 1 - self.core if arriving else self.core
        return self.copy(2, self.whole.at[self.core], self.whole.at[half], mate)

    def peers(self, body):
        def one(d, _):
            body(d, lax.rem(self.mb + d, self.batch), lax.rem(self.mb + self.batch - d, self.batch))
            return 0

        lax.fori_loop(1, self.batch, one, 0)

    def scatter(self, d, to, far):
        return self.copy(2 + d, self.stage.at[self.core, to], self.r2.at[far], {"batch": to})

    def gather(self, d, to, far):
        return self.copy(1 + self.batch + d, self.whole.at[self.core, self.mb], self.whole.at[self.core, far], {"batch": to})

    def step(self, n):
        core, mb = self.core, self.mb
        if n == 0:
            self.near().start()
        if n == 1:
            self.near().wait_recv()

            def add(b, _):
                self.stage[core, b] = (self.stage[core, b].astype(F32) + self.r1[b].astype(F32)).astype(BF)
                return 0

            lax.fori_loop(0, self.batch, add, 0)
            self.peers(lambda d, to, far: self.scatter(d, to, mb).start())
        if n == 2:
            self.peers(lambda d, to, far: self.scatter(d, to, far).wait_recv())

            def more(d, total):
                return total + self.r2[lax.rem(mb + d, self.batch)].astype(F32)

            self.z[...] = lax.fori_loop(1, self.batch, more, self.stage[core, mb].astype(F32)).astype(BF)
            self.across().start()
        if n == 3:
            self.across().wait_recv()
            self.whole[core, mb] = (self.z[...].astype(F32) + self.r3[...].astype(F32)).astype(BF)
            self.peers(lambda d, to, far: self.gather(d, to, mb).start())
        if n == 4:
            self.peers(lambda d, to, far: self.gather(d, to, far).wait_recv())
            self.back(False).start()
        if n == 5:
            self.back(True).wait_recv()
            self.near().wait_send()
            self.across().wait_send()
            self.back(False).wait_send()
            self.peers(lambda d, to, far: self.scatter(d, to, mb).wait_send())
            self.peers(lambda d, to, far: self.gather(d, to, mb).wait_send())


class Tiny:
    def __init__(self, me, mb, own, row, col, send_sem, recv_sem):
        self.me, self.mb, self.own, self.row, self.col = me, mb, own, row, col
        self.send_sem, self.recv_sem = send_sem, recv_sem
        self.axes = (("row", me, own, row, 0), ("batch", mb, own, col, row.shape[0]))

    def each(self, n, body):
        axis, here, src, dst, base = self.axes[n]
        size = dst.shape[0]

        def one(d, _):
            def copy(arriving):
                at = lax.rem(here + size - d, size) if arriving else here
                return pltpu.make_async_remote_copy(
                    src_ref=src.at[n],
                    dst_ref=dst.at[at],
                    send_sem=self.send_sem.at[base + d],
                    recv_sem=self.recv_sem.at[base + d],
                    device_id={axis: lax.rem(here + d, size)},
                    device_id_type=pl.DeviceIdType.MESH,
                )

            body(copy)
            return 0

        lax.fori_loop(1, size, one, 0)

    def start(self, n, value):
        _, here, src, dst, _ = self.axes[n]
        src[n] = value
        dst[here] = value
        self.each(n, lambda copy: copy(False).start())

    def total(self, n):
        dst = self.axes[n][3]
        self.each(n, lambda copy: copy(True).wait_recv())
        return lax.fori_loop(0, dst.shape[0], lambda i, t: t + dst[i], jnp.zeros(dst.shape[1:], F32))

    def sent(self):
        for n in range(2):
            self.each(n, lambda copy: copy(False).wait_send())


def block_kernel(
    shares,
    ahead,
    early,
    boxes_ref,
    drops_ref,
    partners_ref,
    inverse_ref,
    cot_hbm,
    w1_hbm,
    w2_hbm,
    x_ref,
    norm1_gain,
    norm1_bias,
    norm2_gain,
    norm2_bias,
    proj_bias,
    fc2_bias,
    lepe_bias,
    lepe_weight,
    fc1_bias,
    wq,
    wp,
    out,
    ig,
    *refs,
):
    n_sums = 4
    wholes = refs[:n_sums]
    (
    last,
    tiny,
    tiny_own,
    tiny_row,
    tiny_col,
    tiny_send,
    tiny_recv,
    cot_ref,
    w1,
    w2,
    boxes,
    drops,
    partners,
    inverse,
    vec,
    gw1,
    gb1,
    gw2t,
    gq,
    gp,
    small,
    perm_ref,
    wf_ref,
    wt_ref,
    mixed,
    n1h,
    n1t,
    n1p,
    qf,
    kf,
    vf,
    pf,
    qt,
    kt,
    vt,
    pt,
    att_f,
    att_ts,
    att_th,
    dh1,
    da_f,
    da_ts,
    da_tt,
    dn_ts,
    dn_th,
    send_sem,
    recv_sem,
    sum_send,
    sum_recv,
    load_sem,
    store_sem,
    *spare,
    ) = refs[n_sums:]
    chunks, _, pair, strip = n1h.shape[:4]
    images = x_ref.shape[0]
    mine = images // shares
    tokens = shares * pair * strip
    me = lax.axis_index("row")
    ex = Exchange(me, shares, send_sem, recv_sem)

    mb = lax.axis_index("batch")
    batch = tiny_col.shape[0]
    sums = [
        Reduce(n, me, mb, shares, spare[5 * n], wholes[n], *spare[5 * n + 1 : 5 * n + 5], sum_send, sum_recv)
        for n in range(n_sums)
    ]
    sum_a, sum_b, sum_c, sum_d = sums

    few = Tiny(me, mb, tiny_own, tiny_row, tiny_col, tiny_send, tiny_recv)

    loads = [
        pltpu.make_async_copy(src, dst, load_sem.at[n])
        for n, (src, dst) in enumerate(((boxes_ref, boxes), (drops_ref, drops), (partners_ref, partners), (inverse_ref, inverse)))
    ]
    late = [
        pltpu.make_async_copy(src, dst, load_sem.at[4 + n])
        for n, (src, dst) in enumerate(((cot_hbm, cot_ref), (w1_hbm, w1), (w2_hbm, w2)))
    ]
    for load in loads + late:
        load.start()
    barrier = pltpu.get_barrier_semaphore()
    for d in range(1, shares):
        pl.semaphore_signal(
            barrier, inc=1, device_id={"row": lax.rem(me + d, shares)}, device_id_type=pl.DeviceIdType.MESH
        )

    def greet(d, _):
        pl.semaphore_signal(
            barrier, inc=1, device_id={"batch": lax.rem(mb + d, batch)}, device_id_type=pl.DeviceIdType.MESH
        )
        return 0

    lax.fori_loop(1, batch, greet, 0)
    pl.semaphore_wait(barrier, shares + batch - 2)
    for load in loads:
        load.wait()

    params = (norm1_gain, norm1_bias, norm2_gain, norm2_bias, proj_bias, fc2_bias, lepe_bias)
    for n, ref in enumerate(params):
        vec[n : n + 1] = ref[...].astype(F32).reshape(1, 256)
    for i in range(3):
        for j in range(3):
            n = CONV + 3 * i + j
            vec[n : n + 1, :128] = lepe_weight[i, j : j + 1, :128].astype(F32)
            vec[n : n + 1, 128:] = lepe_weight[j, i : i + 1, 128:].astype(F32)
    for n in range(4):
        vec[FB1 + n : FB1 + n + 1] = fc1_bias[256 * n : 256 * n + 256].astype(F32).reshape(1, 256)
    v = lambda i: vec[i : i + 1]
    lm = (
        lax.broadcasted_iota(jnp.int32, (8, 128), 0) == lax.broadcasted_iota(jnp.int32, (8, 128), 1) // 32
    ).astype(F32).astype(BF)
    to_row = lax.broadcasted_iota(jnp.int32, (256, 256), 0)
    to_col = lax.broadcasted_iota(jnp.int32, (256, 256), 1)
    perm_ref[...] = jnp.where((to_row % 16) * 16 + to_row // 16 == to_col, 1.0, 0.0).astype(BF)
    for ref in (gw1, gb1, gw2t, gq, gp, small, tiny):
        ref[...] = jnp.zeros_like(ref)
    for part in range(3):
        cols = slice(128 * part, 128 * part + 128)
        wf_ref[:, cols] = wq[:, 256 * part : 256 * part + 128]
        wt_ref[:, cols] = wq[:, 256 * part + 128 : 256 * part + 256]
    taps = [vec[CONV + i] for i in range(9)]
    taps_f = [z[:128] for z in taps]
    taps_t = [z[128:] for z in taps]

    spot = lax.broadcasted_iota(jnp.int32, (strip, 1), 0)
    grid_row = me * (strip // 16) + spot // 16
    grid_col = spot % 16

    def shares_of(image):
        inside = (
            (grid_row >= boxes[0, image])
            & (grid_row < boxes[1, image])
            & (grid_col >= boxes[2, image])
            & (grid_col < boxes[3, image])
        )
        return jnp.where(inside, 0.0, 0.7), jnp.where(inside, 1.0, 0.3)

    def home(c):
        return [(q, i, mine * q + pair * c + i) for q in range(shares) for i in range(pair)]

    def permute(value):
        whole = perm_ref[...]
        return jnp.concatenate(
            [dot(whole, value[256 * i : 256 * i + 256]).astype(BF) for i in range(pair)], axis=0
        )

    def keep(c, j):
        return jnp.concatenate(
            [jnp.full((strip, 1), drops[j, image].astype(F32) * 1.25) for _, _, image in home(c)], axis=0
        )

    def half(c, tall):
        refs = (qt, kt, vt, pt) if tall else (qf, kf, vf, pf)
        return dict(zip("qkvp", [r.at[c] for r in refs]))

    def stores(c, which):
        copies = []
        for q in range(shares):
            rows = pl.ds(mine * q + pair * c, pair)
            src, dst = ((cot_ref.at[rows], out), (n1h.at[c, q], ig))[which]
            copies.append(pltpu.make_async_copy(src, dst.at[rows], store_sem.at[which, c, q]))
        return copies

    def mix(c, _):
        for q, i, image in home(c):
            own, other = shares_of(image)
            m = own * x_ref[image].astype(F32) + other * x_ref[lax.rem(partners[image], images)].astype(F32)
            mixed[image] = m
            u, _ = normalise(m)
            n1h[c, q, i] = (u * v(G1) + v(B1)).astype(BF)
        @pl.when(c < early)
        def _():
            ex.send(N1, c, n1h, n1t)

        return 0

    def flat(c, _):
        qkv = dot(n1h[c].reshape(tokens, 256), wf_ref[...]).astype(BF)
        qf[c], kf[c], vf[c] = qkv[:, :128], qkv[:, 128:256], qkv[:, 256:]
        att_f[c] = attend_half(half(c, False), lm, taps_f, vec[CB : CB + 1, :128])
        return 0

    def tall(c, _):
        ex.receive(N1, c, n1h, n1t)
        n1 = permute(n1t[c].reshape(tokens, 256))
        n1p[c] = n1
        qkv = dot(n1, wt_ref[...]).astype(BF)
        qt[c], kt[c], vt[c] = qkv[:, :128], qkv[:, 128:256], qkv[:, 256:]
        att = attend_half(half(c, True), lm, taps_t, vec[CB : CB + 1, 128:])
        att_ts[c] = permute(att).reshape(att_ts.shape[1:])
        ex.send(AT, c, att_ts, att_th)
        return 0

    def mlp(c, _):
        ex.receive(AT, c, att_ts, att_th)
        keep1, keep2 = keep(c, 0), keep(c, 1)
        att = jnp.concatenate([att_f[c], att_th[c].reshape(tokens, 128)], axis=1)
        m = jnp.concatenate([mixed[image] for _, _, image in home(c)], axis=0)
        h1 = m + keep1 * (dot(att, wp[...]) + v(PB))
        u2, rstd2 = normalise(h1)
        n2 = (u2 * v(G2) + v(B2)).astype(BF)
        cot = jnp.concatenate([cot_ref[image] for _, _, image in home(c)], axis=0).astype(F32)
        db2 = (keep2 * cot).astype(BF)
        small[FB2] += sum8(db2.astype(F32))
        n2t = jnp.concatenate([n2.T, jnp.ones((16, tokens), BF)], axis=0)
        db2t = db2.T
        branch2 = jnp.zeros((tokens, 256), F32)
        dn2 = jnp.zeros((tokens, 256), F32)
        for f in range(w1.shape[1] // 256):
            fs = slice(256 * f, 256 * f + 256)
            act, slope = gelu_twice(dot(n2, w1[:, fs]) + v(FB1 + f))
            act = act.astype(BF)
            dpre = (slope * dot(db2, w2[fs, :], 1, 1)).astype(BF)
            branch2 = branch2 + dot(act, w2[fs, :])
            dn2 = dn2 + dot(dpre, w1[:, fs], 1, 1)
            grad = dot(n2t, dpre)
            gw1[:, fs] += grad[:256]
            gb1[:, fs] += grad[256:]
            gw2t[:, fs] += dot(db2t, act)
        done = (h1 + (0.5 * keep2) * (branch2 + 2.0 * v(FB2))).astype(BF)
        for n, (_, _, image) in enumerate(home(c)):
            cot_ref[image] = done[strip * n : strip * n + strip]
        for store in stores(c, 0):
            store.start()
        small[G2] += sum8(dn2 * u2)
        small[B2] += sum8(dn2)
        d = cot + normalise_back(dn2, u2, rstd2, 0.5 * v(G2))
        dh1[c] = d
        db1 = (keep1 * d).astype(BF)
        small[PB] += sum8(db1.astype(F32))
        gp[...] += dot(att, db1, 0, 0)
        datt = dot(db1, wp[...], 1, 1).astype(BF)
        da_f[c] = datt[:, :128]
        da_ts[c] = datt[:, 128:].reshape(da_ts.shape[1:])
        ex.send(DA, c, da_ts, da_tt)
        return 0

    def add_qkv(grad, start):
        for part in range(3):
            cols = slice(256 * part + start, 256 * part + start + 128)
            gq[:, cols] += grad[:, 128 * part : 128 * part + 128]

    def put(stage, blocks):
        rows = stage.shape[2]
        spot = 0
        for value in blocks:
            done = 0
            while done < value.shape[0]:
                piece, at = divmod(spot, rows)
                n = min(rows - at, value.shape[0] - done)
                stage[piece // batch, piece % batch, at : at + n] = value[done : done + n]
                done += n
                spot += n
        while spot < 2 * batch * rows:
            piece, at = divmod(spot, rows)
            stage[piece // batch, piece % batch, at:] = jnp.zeros((rows - at, 256), BF)
            spot += rows - at

    quarters = [slice(256 * f, 256 * f + 256) for f in range(w1.shape[1] // 256)]

    def pack_fc1():
        put(sum_a.stage, [(0.5 * gw1[:, fs]).astype(BF) for fs in quarters])

    def pack_fc2():
        put(sum_b.stage, [(0.5 * gw2t[:, fs]).astype(BF).T for fs in quarters] + [gp[...].astype(BF)])

    def qkv_blocks(start):
        one, two, three = (gq[:, 256 * n + start : 256 * n + start + 128].astype(BF) for n in range(3))
        return [jnp.concatenate([one, two], axis=1), jnp.concatenate([three[:128], three[128:]], axis=1)]

    def pack_flat():
        row = lambda i: jnp.sum(small[i], axis=0, keepdims=True)
        rows = [row(i) * (0.5 if i in (G2, B2) else 1.0) for i in range(CONV)]
        conv = [row(CONV + i) for i in range(9)]
        for i in range(3):
            for j in range(3):
                rows.append(jnp.concatenate([conv[3 * i + j][:, :128], conv[3 * j + i][:, 128:]], axis=1))
        rows += [0.5 * gb1[0:1, fs] for fs in quarters]
        rows.append(jnp.zeros((32 - len(rows), 256), F32))
        put(sum_d.stage, qkv_blocks(0) + [jnp.concatenate(rows, axis=0).astype(BF)])

    def tall_back(c, _):
        ex.receive(DA, c, da_ts, da_tt)
        da = permute(da_tt[c].reshape(tokens, 128))
        s = dict(half(c, True), da=da)
        dqkv = attend_half_back(s, lm, taps_t, small, slice(128, 256))
        add_qkv(dot(n1p[c], dqkv, 0, 0), 128)
        dn_ts[c] = permute(dot(dqkv, wt_ref[...], 1, 1).astype(BF)).reshape(dn_ts.shape[1:])
        return 0

    def at(c, steps):
        for spot, total, n in steps:

            @pl.when(c == min(spot, chunks - 1))
            def _():
                total.step(n)

    def pace(c, first, last):
        @pl.when((c % 2 == 0) & (first + c // 2 < last))
        def _():
            ex.send(DN, first + c // 2, dn_ts, dn_th)

    def tall_loop(c, _):
        tall_back(c, 0)
        pace(c, 0, chunks)
        at(c, TALL_STEPS)
        return 0

    def flat_back(c, _):
        s = dict(half(c, False), da=da_f.at[c])
        dqkv = attend_half_back(s, lm, taps_f, small, slice(0, 128))
        add_qkv(dot(n1h[c].reshape(tokens, 256), dqkv, 0, 0), 0)
        qf[c], kf[c], vf[c] = dqkv[:, :128], dqkv[:, 128:256], dqkv[:, 256:]
        pace(c, (chunks + 1) // 2, chunks)
        at(c, FLAT_STEPS)
        return 0

    def norm_back(c, _):
        ex.sent(N1, c, n1h, n1t)
        ex.receive(DN, c, dn_ts, dn_th)
        dqkv = jnp.concatenate([qf[c], kf[c], vf[c]], axis=1)
        dn1 = dot(dqkv, wf_ref[...], 1, 1) + dn_th[c].reshape(tokens, 256).astype(F32)
        m = jnp.concatenate([mixed[image] for _, _, image in home(c)], axis=0)
        u1, rstd1 = normalise(m)
        tiny[0] += sum8(dn1 * u1)
        tiny[1] += sum8(dn1)
        d = dh1[c] + normalise_back(dn1, u1, rstd1, v(G1))
        for n, (_, _, image) in enumerate(home(c)):
            mixed[image] = d[strip * n : strip * n + strip]
        at(c, NORM_STEPS)
        return 0

    def unmix(c, _):
        for q, i, image in home(c):
            other = inverse[image]
            n1h[c, q, i] = (shares_of(image)[0] * mixed[image] + shares_of(other)[1] * mixed[other]).astype(BF)
        for store in stores(c, 1):
            store.start()
        return 0

    def drain(c, _):
        for kind, src, dst in ((AT, att_ts, att_th), (DA, da_ts, da_tt), (DN, dn_ts, dn_th)):
            ex.sent(kind, c, src, dst)
        for store in stores(c, 0) + stores(c, 1):
            store.wait()
        return 0

    lax.fori_loop(0, chunks, mix, 0)
    lax.fori_loop(0, chunks, flat, 0)
    lax.fori_loop(0, ahead, tall, 0)

    def forward(c, _):
        @pl.when(c < chunks - early)
        def _():
            ex.send(N1, c + early, n1h, n1t)

        @pl.when(c < chunks - ahead)
        def _():
            tall(c + ahead, 0)

        mlp(c, 0)
        return 0

    for load in late:
        load.wait()
    lax.fori_loop(0, chunks, forward, 0)
    TALL_STEPS = ((0, sum_a, 1), (4, sum_b, 1), (5, sum_a, 2), (7, sum_a, 3))
    FLAT_STEPS = (
        (1, sum_c, 1),
        (1, sum_b, 2),
        (3, sum_b, 3),
        (4, sum_a, 4),
        (5, sum_c, 2),
        (6, sum_a, 5),
        (7, sum_c, 3),
    )
    NORM_STEPS = ((1, sum_d, 1), (6, sum_b, 4), (7, sum_c, 4), (8, sum_d, 2))
    pack_fc1()
    sum_a.step(0)
    pack_fc2()
    sum_b.step(0)
    lax.fori_loop(0, chunks, tall_loop, 0)
    put(sum_c.stage, qkv_blocks(128))
    sum_c.step(0)
    lax.fori_loop(0, chunks, flat_back, 0)
    pack_flat()
    sum_d.step(0)
    lax.fori_loop(0, chunks, norm_back, 0)
    rows = [jnp.sum(tiny[n], axis=0, keepdims=True) for n in range(2)] + [jnp.zeros((6, 256), F32)]
    few.start(0, jnp.concatenate(rows, axis=0))
    sum_b.step(5)
    sum_c.step(5)
    half_way = 2 * chunks // 3
    lax.fori_loop(0, half_way, unmix, 0)
    sum_d.step(3)
    few.start(1, few.total(0))
    lax.fori_loop(half_way, chunks, unmix, 0)
    sum_d.step(4)
    last[...] = few.total(1)
    few.sent()
    lax.fori_loop(0, chunks, drain, 0)
    sum_d.step(5)


def share_rows(rows, batch):
    return -(-rows // (2 * batch * 16)) * 16


def block(inputs, cotangent, boxes, drops, partners, inverse, vectors, weights, pair=2, ahead=2, early=4):
    images, grid_rows, side, width = inputs.shape
    shares, batch = lax.axis_size("row"), lax.axis_size("batch")
    strip = grid_rows * side
    chunks = images // shares // pair
    tokens = shares * pair * strip
    hidden = weights[2].shape[1]
    sds = jax.ShapeDtypeStruct
    vmem = pl.BlockSpec(memory_space=pltpu.VMEM)
    hbm = pl.BlockSpec(memory_space=pl.ANY)
    x = inputs.reshape(images, strip, width)
    cot = cotangent.reshape(images, strip, width)
    sizes = [hidden, hidden + width, 3 * width // 2, 3 * width // 2 + 32]
    sizes = [share_rows(n, batch) for n in sizes]
    rows = lambda ch, dt=BF: pltpu.VMEM((chunks, tokens, ch), dt)
    at_home = lambda ch: pltpu.VMEM((chunks, shares, pair, strip, ch), BF)
    at_tall = lambda ch: pltpu.VMEM((chunks, pair, shares, strip, ch), BF)
    part = lambda n, *lead: pltpu.VMEM((*lead, n, width), BF)
    return pl.pallas_call(
        functools.partial(block_kernel, shares, ahead, early),
        in_specs=[hbm] * 7 + [vmem] * (1 + len(vectors) + 2),
        out_specs=[hbm, hbm] + [vmem] * 5,
        out_shape=[
            sds(x.shape, BF),
            sds(x.shape, BF),
        ]
        + [sds((2, batch, n, width), BF) for n in sizes]
        + [sds((8, width), F32)],
        scratch_shapes=[
            pltpu.VMEM((2, 8, width), F32),
            pltpu.VMEM((2, 8, width), F32),
            pltpu.VMEM((shares, 8, width), F32),
            pltpu.VMEM((batch, 8, width), F32),
            pltpu.SemaphoreType.DMA((shares + batch,)),
            pltpu.SemaphoreType.DMA((shares + batch,)),
            pltpu.VMEM(x.shape, BF),
            pltpu.VMEM(weights[2].shape, BF),
            pltpu.VMEM(weights[3].shape, BF),
            pltpu.SMEM(boxes.shape, jnp.int32),
            pltpu.SMEM(drops.shape, jnp.int32),
            pltpu.SMEM(partners.shape, jnp.int32),
            pltpu.SMEM(inverse.shape, jnp.int32),
            pltpu.VMEM((24, width), F32),
            pltpu.VMEM((width, hidden), F32),
            pltpu.VMEM((16, hidden), F32),
            pltpu.VMEM((width, hidden), F32),
            pltpu.VMEM((width, 3 * width), F32),
            pltpu.VMEM((width, width), F32),
            pltpu.VMEM((16, 8, width), F32),
            pltpu.VMEM((256, 256), BF),
            pltpu.VMEM((width, 384), BF),
            pltpu.VMEM((width, 384), BF),
            pltpu.VMEM(x.shape, F32),
            at_home(width),
            at_tall(width),
            rows(width),
        ]
        + [rows(128)] * 9
        + [at_tall(128), at_home(128), rows(width, F32), rows(128), at_home(128), at_tall(128), at_tall(width), at_home(width)]
        + [pltpu.SemaphoreType.DMA((4, chunks, shares - 1))] * 2
        + [pltpu.SemaphoreType.DMA((len(sizes), 2 * batch + 1))] * 2
        + [pltpu.SemaphoreType.DMA((7,)), pltpu.SemaphoreType.DMA((2, chunks, shares))]
        + [z for n in sizes for z in (part(n, 2, batch), part(n, batch), part(n, batch), part(n), part(n))],
        compiler_params=pltpu.CompilerParams(
            collective_id=0, has_side_effects=True, vmem_limit_bytes=63 * 2**20
        ),
    )(boxes, drops, partners, inverse, cot, *weights[2:], x, *vectors, *weights[:2])


def finish_kernel(out_ref, ig_ref, hbm_a, hbm_b, hbm_c, hbm_d, last, *refs):
    out, ig, g1, b1, gq_hbm, conv, cb, gp_hbm, pb, g2, b2, gw1_hbm, fb1, gw2_hbm, fb2 = refs[:15]
    held, sum_a, sum_b, sum_c, sum_d, gq, gp, gw1, gw2, load_sem, store_sem = refs[15:]
    sixth = out.shape[0] // 6
    loads = [
        pltpu.make_async_copy(src, dst, load_sem.at[m])
        for m, (src, dst) in enumerate(((hbm_a, sum_a), (hbm_b, sum_b), (hbm_c, sum_c), (hbm_d, sum_d)))
    ]
    stores = [
        pltpu.make_async_copy(src, dst, store_sem.at[m])
        for m, (src, dst) in enumerate(((gw1, gw1_hbm), (gw2, gw2_hbm), (gp, gp_hbm), (gq, gq_hbm)))
    ]
    parts = [(n, pl.ds(sixth * i, sixth), 6 * n + i + 4) for i in range(6) for n in range(2)]
    loads += [pltpu.make_async_copy((out_ref, ig_ref)[n].at[r], held.at[n, r], load_sem.at[m]) for n, r, m in parts]
    stores += [pltpu.make_async_copy(held.at[n, r], (out, ig)[n].at[r], store_sem.at[m]) for n, r, m in parts]
    for load in loads:
        load.start()
    hidden = gw1.shape[1]
    loads[0].wait()
    for f in range(hidden // 256):
        gw1[:, 256 * f : 256 * f + 256] = sum_a[256 * f : 256 * f + 256].astype(F32)
    stores[0].start()
    loads[1].wait()
    gw2[...] = sum_b[:hidden].astype(F32)
    gp[...] = sum_b[hidden : hidden + 256].astype(F32)
    stores[1].start()
    stores[2].start()
    loads[2].wait()
    loads[3].wait()
    for ref, start in ((sum_d, 0), (sum_c, 128)):
        gq[:, start : start + 128] = ref[:256, :128].astype(F32)
        gq[:, 256 + start : 384 + start] = ref[:256, 128:].astype(F32)
        gq[:128, 512 + start : 640 + start] = ref[256:384, :128].astype(F32)
        gq[128:, 512 + start : 640 + start] = ref[256:384, 128:].astype(F32)
    stores[3].start()
    for load, store in zip(loads[4:], stores[4:]):
        load.wait()
        store.start()
    rows = sum_d[384:416].astype(F32)
    for n, ref in ((G2, g2), (B2, b2), (PB, pb), (FB2, fb2), (CB, cb)):
        ref[...] = rows[n]
    g1[...], b1[...] = last[0], last[1]
    for i in range(3):
        for j in range(3):
            conv[i, j] = rows[CONV + 3 * i + j]
    for f in range(hidden // 256):
        fb1[256 * f : 256 * f + 256] = rows[FB1 + f]
    for store in stores:
        store.wait()


def finish(out, ig, sums, last, hidden):
    width = out.shape[-1]
    sds = jax.ShapeDtypeStruct
    vmem = pl.BlockSpec(memory_space=pltpu.VMEM)
    hbm = pl.BlockSpec(memory_space=pl.ANY)
    flat = lambda n: sds((n,), F32)
    square = lambda *n: sds(n, F32)
    large = [square(width, 3 * width), square(width, width), square(width, hidden), square(hidden, width)]
    shapes = [
        flat(width),
        flat(width),
        large[0],
        square(3, 3, width),
        flat(width),
        large[1],
        flat(width),
        flat(width),
        flat(width),
        large[2],
        flat(hidden),
        large[3],
        flat(width),
    ]
    sums = [z.reshape(-1, width) for z in sums]
    return pl.pallas_call(
        finish_kernel,
        in_specs=[hbm] * 6 + [vmem],
        out_specs=[hbm, hbm] + [hbm if z in large else vmem for z in shapes],
        out_shape=[sds(out.shape, BF), sds(ig.shape, BF)] + shapes,
        scratch_shapes=[pltpu.VMEM((2,) + out.shape, BF)]
        + [pltpu.VMEM(z.shape, BF) for z in sums]
        + [pltpu.VMEM(z.shape, F32) for z in large]
        + [pltpu.SemaphoreType.DMA((16,))] * 2,
        compiler_params=pltpu.CompilerParams(vmem_limit_bytes=62 * 2**20),
    )(out, ig, *sums, last)


def per_device(
    inputs,
    partners,
    boxes,
    drops,
    norm1_gain,
    norm1_bias,
    qkv_weight,
    lepe_weight,
    lepe_bias,
    proj_weight,
    proj_bias,
    norm2_gain,
    norm2_bias,
    fc1_weight,
    fc1_bias,
    fc2_weight,
    fc2_bias,
    cotangent,
):
    images = inputs.shape[0]
    ids = jnp.arange(images)
    inverse = jnp.sum(jnp.where(partners[:, None] % images == ids[None, :], ids[:, None], 0), axis=0)
    vectors = (norm1_gain, norm1_bias, norm2_gain, norm2_bias, proj_bias, fc2_bias, lepe_bias, lepe_weight, fc1_bias)
    weights = (qkv_weight, proj_weight, fc1_weight, fc2_weight)
    out, ig, *sums, last = block(inputs, cotangent, boxes.T, drops.T, partners, inverse, vectors, weights)
    out, ig, *grads = finish(out, ig, sums, last, fc1_weight.shape[1])
    return (out.reshape(inputs.shape), ig.reshape(inputs.shape), *grads)


def solution(mesh):
    tokens = P("batch", "row", None, None)
    return jax.shard_map(
        per_device,
        mesh=mesh,
        in_specs=(tokens, P("batch"), P("batch", None), P("batch", None)) + (P(),) * 13 + (tokens,),
        out_specs=(tokens, tokens) + (P(),) * 13,
        check_vma=False,
    )
```

```python
import functools
import math

import jax
import jax.numpy as jnp
from jax import lax
from jax.experimental import pallas as pl
from jax.experimental.pallas import tpu as pltpu
from jax.sharding import PartitionSpec as P

F32 = jnp.float32
BF = jnp.bfloat16
EPS = 1e-5
SCALE = 32**-0.5
LOG2E = math.log2(math.e)
SLOPE = 2.0 / math.sqrt(math.pi)
ROOT_HALF = math.sqrt(0.5)
G1, B1, G2, B2, PB, FB2, CB, CONV, FB1 = 0, 1, 2, 3, 4, 5, 6, 7, 16
N1, AT, DA, DN = 0, 1, 2, 3


def dot(a, b, ca=1, cb=0):
    return lax.dot_general(a, b, (((ca,), (cb,)), ((), ())), preferred_element_type=F32)


def gelu_twice(v):
    w = v * ROOT_HALF
    up = 1.0 + lax.erf(w)
    return v * up, up + (w * jnp.exp2(w * w * -LOG2E)) * SLOPE


def normalise(x):
    center = x - jnp.mean(x, axis=-1, keepdims=True)
    rstd = lax.rsqrt(jnp.mean(center * center, axis=-1, keepdims=True) + EPS)
    return center * rstd, rstd


def normalise_back(d, u, rstd, gain):
    e = d * gain
    m1 = jnp.mean(e, axis=-1, keepdims=True)
    m2 = jnp.mean(e * u, axis=-1, keepdims=True)
    return (e - m1 - u * m2) * rstd


def sum8(x):
    n, c = x.shape
    return jnp.sum(x.reshape(n // 8, 8, c), axis=0)


def four(x):
    return [x[32 * w : 32 * w + 32] for w in range(4)]


def masked(x, j, lm):
    return jnp.concatenate([r * lm[b ^ j : (b ^ j) + 1] for b, r in enumerate(four(x))], axis=0)


def spread(x, w, lm):
    return jnp.concatenate([x * lm[j ^ w : (j ^ w) + 1] for j in range(4)], axis=0)


def weave(parts, j, lane):
    r = parts[j]
    for h in (1, 2, 3):
        r = jnp.where(lane >= 32 * h, parts[h ^ j], r)
    return r


def two_dots(a, b):
    r = dot(jnp.concatenate(a, axis=0), jnp.concatenate(b, axis=1))
    n, m = a[0].shape[0], b[0].shape[1]
    return r[:n, :m], r[n:, m:]


def attend_groups(q, k, v, lm, lane):
    n = range(len(q))
    pairs = range(0, len(q), 2)
    qt = [x.T for x in q]
    k4, v4 = [four(x) for x in k], [four(x) for x in v]
    st = [[None] * 4 for _ in n]
    for j in range(4):
        for g in pairs:
            st[g][j], st[g + 1][j] = two_dots(
                [weave(x, j, lane) for x in k4[g : g + 2]], [masked(x, j, lm) for x in qt[g : g + 2]]
            )
    p = [[] for _ in n]
    for g in n:
        for s in st[g]:
            top = jnp.max(s, axis=0, keepdims=True)
            e = jnp.exp2((s - top) * (SCALE * LOG2E))
            p[g].append((e * (1.0 / jnp.sum(e, axis=0, keepdims=True))).astype(BF))
    p = [jnp.concatenate(x, axis=0) for x in p]
    pt = [four(x.T) for x in p]
    o = [[None] * 4 for _ in n]
    for w in range(4):
        for g in pairs:
            o[g][w], o[g + 1][w] = two_dots(
                [x[w] for x in pt[g : g + 2]], [spread(x[w], w, lm) for x in v4[g : g + 2]]
            )
    return p, [jnp.concatenate(x, axis=0) for x in o]


def attend_groups_back(q, k, v, p, da, lm, lane):
    n = range(len(q))
    pairs = range(0, len(q), 2)
    dat = [x.T for x in da]
    v4, k4, p4 = [four(x) for x in v], [four(x) for x in k], [four(x) for x in p]
    ds, dv, dk, dp, dq = ([[None] * 4 for _ in n] for _ in range(5))
    for j in range(4):
        for g in pairs:
            dp[g][j], dp[g + 1][j] = two_dots(
                [weave(x, j, lane) for x in v4[g : g + 2]], [masked(x, j, lm) for x in dat[g : g + 2]]
            )
            dv[g][j], dv[g + 1][j] = two_dots(
                [x[j] for x in p4[g : g + 2]], [masked(x, j, lm) for x in da[g : g + 2]]
            )
    for g in n:
        for j in range(4):
            pr = p4[g][j].astype(F32)
            t = pr * dp[g][j]
            ds[g][j] = (t - pr * jnp.sum(t, axis=0, keepdims=True)).astype(BF)
    dst = [four(jnp.concatenate(x, axis=0).T) for x in ds]
    for j in range(4):
        for g in pairs:
            dk[g][j], dk[g + 1][j] = two_dots(
                [x[j] for x in ds[g : g + 2]], [masked(x, j, lm) for x in q[g : g + 2]]
            )
    for w in range(4):
        for g in pairs:
            dq[g][w], dq[g + 1][w] = two_dots(
                [x[w] for x in dst[g : g + 2]], [spread(x[w], w, lm) for x in k4[g : g + 2]]
            )
    whole = lambda parts: jnp.concatenate([weave(parts, w, lane) for w in range(4)], axis=0)
    return [(jnp.concatenate(dq[g], axis=0), whole(dk[g]), whole(dv[g])) for g in n]


def tiles(a):
    n, c = a.shape
    z = a.reshape(n // 32, 4, 8, c)
    return [z[:, i] for i in range(4)]


def untiled(parts):
    n, _, c = parts[0].shape
    return jnp.stack(parts, axis=1).reshape(32 * n, c)


def shifts(parts):
    row = lax.broadcasted_iota(jnp.int32, parts[0].shape, 1)
    up = [pltpu.roll(p, 1, 1) for p in parts]
    down = [pltpu.roll(p, 7, 1) for p in parts]
    early, late = [], []
    for lo in (0, 2):
        early += [jnp.where(row == 0, 0.0, up[lo]), jnp.where(row == 0, up[lo], up[lo + 1])]
        late += [jnp.where(row == 7, down[lo + 1], down[lo]), jnp.where(row == 7, 0.0, down[lo + 1])]
    return {-1: early, 0: parts, 1: late}


def taps_sum(near, taps, pairs):
    return [
        sum(near[j][2 * line + h] * taps[3 * (i + 1) + j + 1][None, None] for i, line in pairs for j in (-1, 0, 1))
        for h in range(2)
    ]


def attend_half(s, lm, taps, shift):
    tokens = s["q"].shape[0]
    lane = lax.broadcasted_iota(jnp.int32, (32, 128), 1)
    rows = [slice(128 * n, 128 * n + 128) for n in range(tokens // 128)]
    p, out = attend_groups(*([s[name][r] for r in rows] for name in "qkv"), lm, lane)
    for r, x in zip(rows, p):
        s["p"][r] = x
    near = shifts(tiles(s["v"][...].astype(F32)))
    lepe = untiled(taps_sum(near, taps, ((0, 0), (1, 1))) + taps_sum(near, taps, ((0, 1), (-1, 0))))
    return (jnp.concatenate(out, axis=0) + (lepe + shift)).astype(BF)


def attend_half_back(s, lm, taps, small, cols):
    tokens = s["q"].shape[0]
    lane = lax.broadcasted_iota(jnp.int32, (32, 128), 1)
    rows = [slice(128 * n, 128 * n + 128) for n in range(tokens // 128)]
    parts = attend_groups_back(*([s[name][r] for r in rows] for name in ("q", "k", "v", "p", "da")), lm, lane)
    dq, dk, dv = (jnp.concatenate(z, axis=0) for z in zip(*parts))
    da = s["da"][...].astype(F32)
    small[CB, :, cols] += sum8(da)
    moved = {-j: parts for j, parts in shifts(tiles(da)).items()}
    vt = tiles(s["v"][...].astype(F32))
    dv = dv + untiled(taps_sum(moved, taps, ((0, 0), (-1, 1))) + taps_sum(moved, taps, ((1, 0), (0, 1))))
    over = lambda z: jnp.sum(z, axis=0)
    for j in (-1, 0, 1):
        m = moved[j]
        small[CONV + 3 + j + 1, :, cols] += over(m[0] * vt[0] + m[1] * vt[1] + m[2] * vt[2] + m[3] * vt[3])
        small[CONV + 6 + j + 1, :, cols] += over(m[0] * vt[2] + m[1] * vt[3])
        small[CONV + 0 + j + 1, :, cols] += over(m[2] * vt[0] + m[3] * vt[1])
    return jnp.concatenate([(dq * SCALE).astype(BF), (dk * SCALE).astype(BF), dv.astype(BF)], axis=1)


class Exchange:
    def __init__(self, me, shares, send_sem, recv_sem):
        self.me, self.shares, self.send_sem, self.recv_sem = me, shares, send_sem, recv_sem

    def copy(self, kind, c, d, src, dst, arriving):
        to = lax.rem(self.me + d, self.shares)
        far = lax.rem(self.me + self.shares - d, self.shares) if arriving else self.me
        if kind in (N1, DA):
            source, target = src.at[c, to], dst.at[c, :, far]
        else:
            source, target = src.at[c, :, to], dst.at[c, far]
        return pltpu.make_async_remote_copy(
            src_ref=source,
            dst_ref=target,
            send_sem=self.send_sem.at[kind, c, d - 1],
            recv_sem=self.recv_sem.at[kind, c, d - 1],
            device_id={"row": to},
            device_id_type=pl.DeviceIdType.MESH,
        )

    def send(self, kind, c, src, dst):
        me = self.me
        if kind in (N1, DA):
            dst[c, :, me] = src[c, me]
        else:
            dst[c, me] = src[c, :, me]
        for d in range(1, self.shares):
            self.copy(kind, c, d, src, dst, False).start()

    def receive(self, kind, c, src, dst):
        for d in range(1, self.shares):
            self.copy(kind, c, d, src, dst, True).wait_recv()

    def sent(self, kind, c, src, dst):
        for d in range(1, self.shares):
            self.copy(kind, c, d, src, dst, False).wait_send()


class Reduce:
    def __init__(self, group, paired, me, mb, shares, stage, whole, r1, r2, r3, z, send_sem, recv_sem):
        self.whole = whole
        self.group, self.me, self.mb, self.shares = group, me, mb, shares
        self.stage, self.r1, self.r2, self.r3, self.z = stage, r1, r2, r3, z
        self.send_sem, self.recv_sem = send_sem, recv_sem
        self.core = lax.rem(me, 2)
        self.batch = stage.shape[1]
        self.paired = paired
        self.side = lax.rem(mb, 2) if paired else 0
        self.size = self.batch // 2 if paired else self.batch
        self.spot = lax.div(mb, 2) if paired else mb
        self.base = self.side * self.size

    def copy(self, slot, src, dst, device):
        return pltpu.make_async_remote_copy(
            src_ref=src,
            dst_ref=dst,
            send_sem=self.send_sem.at[self.group, slot],
            recv_sem=self.recv_sem.at[self.group, slot],
            device_id=device,
            device_id_type=pl.DeviceIdType.MESH,
        )

    def near(self):
        mate = {"row": self.me + 1 - 2 * self.core}
        return self.copy(0, self.stage.at[1 - self.core], self.r1, mate)

    def across(self):
        return self.copy(1, self.z, self.r3, {"row": lax.rem(self.me + 2, self.shares)})

    def back(self, arriving):
        mate = {"row": self.me + 1 - 2 * self.core}
        half = 1 - self.core if arriving else self.core
        return self.copy(2, self.whole.at[self.core], self.whole.at[half], mate)

    def peers(self, body):
        def one(d, _):
            body(d, lax.rem(self.spot + d, self.size), lax.rem(self.spot + self.size - d, self.size))
            return 0

        lax.fori_loop(1, self.size, one, 0)

    def device(self, spot):
        return {"batch": 2 * spot + self.side if self.paired else spot}

    def scatter(self, d, to, far):
        return self.copy(2 + d, self.stage.at[self.core, self.base + to], self.r2.at[far], self.device(to))

    def gather(self, d, to, far):
        mine, theirs = self.base + self.spot, self.base + far
        return self.copy(
            1 + self.batch + d, self.whole.at[self.core, mine], self.whole.at[self.core, theirs], self.device(to)
        )

    def pair(self):
        half, partner = self.size, {"batch": self.mb + 1 - 2 * self.side}
        src = self.stage.at[self.core, pl.ds((1 - self.side) * half, half)]
        return self.copy(1 + self.batch, src, self.r2.at[pl.ds(half, half)], partner)

    def pair_back(self, arriving):
        half, partner = self.size, {"batch": self.mb + 1 - 2 * self.side}
        side = 1 - self.side if arriving else self.side
        src = self.whole.at[self.core, pl.ds(self.base, half)]
        return self.copy(2 * self.batch, src, self.whole.at[self.core, pl.ds(side * half, half)], partner)

    def add(self, first, count, other, start):
        def one(b, _):
            total = self.stage[self.core, first + b].astype(F32) + other[start + b].astype(F32)
            self.stage[self.core, first + b] = total.astype(BF)
            return 0

        lax.fori_loop(0, count, one, 0)

    def step(self, n):
        steps = [self.begin, self.after_near]
        if self.paired:
            steps.append(self.after_pair)
        steps += [self.after_scatter, self.after_across, self.after_gather]
        if self.paired:
            steps.append(self.after_pair_back)
        steps.append(self.end)
        steps[n]()

    def begin(self):
        self.near().start()

    def after_near(self):
        self.near().wait_recv()
        self.add(0, self.batch, self.r1, 0)
        if self.paired:
            self.pair().start()
        else:
            self.peers(lambda d, to, far: self.scatter(d, to, self.spot).start())

    def after_pair(self):
        self.pair().wait_recv()
        self.add(self.base, self.size, self.r2, self.size)
        self.peers(lambda d, to, far: self.scatter(d, to, self.spot).start())

    def after_scatter(self):
        self.peers(lambda d, to, far: self.scatter(d, to, far).wait_recv())

        def more(d, total):
            return total + self.r2[lax.rem(self.spot + d, self.size)].astype(F32)

        own = self.stage[self.core, self.base + self.spot].astype(F32)
        self.z[...] = lax.fori_loop(1, self.size, more, own).astype(BF)
        self.across().start()

    def after_across(self):
        self.across().wait_recv()
        self.whole[self.core, self.base + self.spot] = (self.z[...].astype(F32) + self.r3[...].astype(F32)).astype(BF)
        self.peers(lambda d, to, far: self.gather(d, to, self.spot).start())

    def after_gather(self):
        self.peers(lambda d, to, far: self.gather(d, to, far).wait_recv())
        if self.paired:
            self.pair_back(False).start()
        else:
            self.back(False).start()

    def after_pair_back(self):
        self.pair_back(True).wait_recv()
        self.back(False).start()

    def end(self):
        self.back(True).wait_recv()
        self.near().wait_send()
        self.across().wait_send()
        self.back(False).wait_send()
        self.peers(lambda d, to, far: self.scatter(d, to, self.spot).wait_send())
        self.peers(lambda d, to, far: self.gather(d, to, self.spot).wait_send())
        if self.paired:
            self.pair().wait_send()
            self.pair_back(False).wait_send()


class Tiny:
    def __init__(self, me, mb, own, row, col, send_sem, recv_sem):
        self.me, self.mb, self.own, self.row, self.col = me, mb, own, row, col
        self.send_sem, self.recv_sem = send_sem, recv_sem
        self.axes = (("row", me, own, row, 0), ("batch", mb, own, col, row.shape[0]))

    def each(self, n, body):
        axis, here, src, dst, base = self.axes[n]
        size = dst.shape[0]

        def one(d, _):
            def copy(arriving):
                at = lax.rem(here + size - d, size) if arriving else here
                return pltpu.make_async_remote_copy(
                    src_ref=src.at[n],
                    dst_ref=dst.at[at],
                    send_sem=self.send_sem.at[base + d],
                    recv_sem=self.recv_sem.at[base + d],
                    device_id={axis: lax.rem(here + d, size)},
                    device_id_type=pl.DeviceIdType.MESH,
                )

            body(copy)
            return 0

        lax.fori_loop(1, size, one, 0)

    def start(self, n, value):
        _, here, src, dst, _ = self.axes[n]
        src[n] = value
        dst[here] = value
        self.each(n, lambda copy: copy(False).start())

    def total(self, n):
        dst = self.axes[n][3]
        self.each(n, lambda copy: copy(True).wait_recv())
        return lax.fori_loop(0, dst.shape[0], lambda i, t: t + dst[i], jnp.zeros(dst.shape[1:], F32))

    def sent(self):
        for n in range(2):
            self.each(n, lambda copy: copy(False).wait_send())


def block_kernel(
    shares,
    ahead,
    early,
    boxes_ref,
    drops_ref,
    partners_ref,
    inverse_ref,
    cot_hbm,
    w1_hbm,
    w2_hbm,
    x_ref,
    norm1_gain,
    norm1_bias,
    norm2_gain,
    norm2_bias,
    proj_bias,
    fc2_bias,
    lepe_bias,
    lepe_weight,
    fc1_bias,
    wq,
    wp,
    out,
    ig,
    *refs,
):
    n_sums = 4
    wholes = refs[:n_sums]
    (
    last,
    tiny,
    tiny_own,
    tiny_row,
    tiny_col,
    tiny_send,
    tiny_recv,
    cot_ref,
    w1,
    w2,
    boxes,
    drops,
    partners,
    inverse,
    vec,
    gw1,
    gb1,
    gw2t,
    gq,
    gp,
    small,
    perm_ref,
    wf_ref,
    wt_ref,
    mixed,
    n1h,
    n1t,
    n1p,
    qf,
    kf,
    vf,
    pf,
    qt,
    kt,
    vt,
    pt,
    att_f,
    att_ts,
    att_th,
    dh1,
    da_f,
    da_ts,
    da_tt,
    dn_ts,
    dn_th,
    send_sem,
    recv_sem,
    sum_send,
    sum_recv,
    load_sem,
    store_sem,
    *spare,
    ) = refs[n_sums:]
    chunks, _, pair, strip = n1h.shape[:4]
    images = x_ref.shape[0]
    mine = images // shares
    tokens = shares * pair * strip
    me = lax.axis_index("row")
    ex = Exchange(me, shares, send_sem, recv_sem)

    mb = lax.axis_index("batch")
    batch = tiny_col.shape[0]
    sums = [
        Reduce(n, n < 2, me, mb, shares, spare[5 * n], wholes[n], *spare[5 * n + 1 : 5 * n + 5], sum_send, sum_recv)
        for n in range(n_sums)
    ]
    sum_a, sum_b, sum_c, sum_d = sums

    few = Tiny(me, mb, tiny_own, tiny_row, tiny_col, tiny_send, tiny_recv)

    loads = [
        pltpu.make_async_copy(src, dst, load_sem.at[n])
        for n, (src, dst) in enumerate(((boxes_ref, boxes), (drops_ref, drops), (partners_ref, partners), (inverse_ref, inverse)))
    ]
    late = [
        pltpu.make_async_copy(src, dst, load_sem.at[4 + n])
        for n, (src, dst) in enumerate(((cot_hbm, cot_ref), (w1_hbm, w1), (w2_hbm, w2)))
    ]
    for load in loads + late:
        load.start()
    barrier = pltpu.get_barrier_semaphore()
    for d in range(1, shares):
        pl.semaphore_signal(
            barrier, inc=1, device_id={"row": lax.rem(me + d, shares)}, device_id_type=pl.DeviceIdType.MESH
        )

    def greet(d, _):
        pl.semaphore_signal(
            barrier, inc=1, device_id={"batch": lax.rem(mb + d, batch)}, device_id_type=pl.DeviceIdType.MESH
        )
        return 0

    lax.fori_loop(1, batch, greet, 0)
    pl.semaphore_wait(barrier, shares + batch - 2)
    for load in loads:
        load.wait()

    params = (norm1_gain, norm1_bias, norm2_gain, norm2_bias, proj_bias, fc2_bias, lepe_bias)
    for n, ref in enumerate(params):
        vec[n : n + 1] = ref[...].astype(F32).reshape(1, 256)
    for i in range(3):
        for j in range(3):
            n = CONV + 3 * i + j
            vec[n : n + 1, :128] = lepe_weight[i, j : j + 1, :128].astype(F32)
            vec[n : n + 1, 128:] = lepe_weight[j, i : i + 1, 128:].astype(F32)
    for n in range(4):
        vec[FB1 + n : FB1 + n + 1] = fc1_bias[256 * n : 256 * n + 256].astype(F32).reshape(1, 256)
    v = lambda i: vec[i : i + 1]
    lm = (
        lax.broadcasted_iota(jnp.int32, (8, 128), 0) == lax.broadcasted_iota(jnp.int32, (8, 128), 1) // 32
    ).astype(F32).astype(BF)
    to_row = lax.broadcasted_iota(jnp.int32, (256, 256), 0)
    to_col = lax.broadcasted_iota(jnp.int32, (256, 256), 1)
    perm_ref[...] = jnp.where((to_row % 16) * 16 + to_row // 16 == to_col, 1.0, 0.0).astype(BF)
    for ref in (gw1, gb1, gw2t, gq, gp, small, tiny):
        ref[...] = jnp.zeros_like(ref)
    for part in range(3):
        cols = slice(128 * part, 128 * part + 128)
        wf_ref[:, cols] = wq[:, 256 * part : 256 * part + 128]
        wt_ref[:, cols] = wq[:, 256 * part + 128 : 256 * part + 256]
    taps = [vec[CONV + i] for i in range(9)]
    taps_f = [z[:128] for z in taps]
    taps_t = [z[128:] for z in taps]

    spot = lax.broadcasted_iota(jnp.int32, (strip, 1), 0)
    grid_row = me * (strip // 16) + spot // 16
    grid_col = spot % 16

    def shares_of(image):
        inside = (
            (grid_row >= boxes[0, image])
            & (grid_row < boxes[1, image])
            & (grid_col >= boxes[2, image])
            & (grid_col < boxes[3, image])
        )
        return jnp.where(inside, 0.0, 0.7), jnp.where(inside, 1.0, 0.3)

    def home(c):
        return [(q, i, mine * q + pair * c + i) for q in range(shares) for i in range(pair)]

    def permute(value):
        whole = perm_ref[...]
        return jnp.concatenate(
            [dot(whole, value[256 * i : 256 * i + 256]).astype(BF) for i in range(pair)], axis=0
        )

    def keep(c, j):
        return jnp.concatenate(
            [jnp.full((strip, 1), drops[j, image].astype(F32) * 1.25) for _, _, image in home(c)], axis=0
        )

    def half(c, tall):
        refs = (qt, kt, vt, pt) if tall else (qf, kf, vf, pf)
        return dict(zip("qkvp", [r.at[c] for r in refs]))

    def stores(c, which):
        copies = []
        for q in range(shares):
            rows = pl.ds(mine * q + pair * c, pair)
            src, dst = ((cot_ref.at[rows], out), (n1h.at[c, q], ig))[which]
            copies.append(pltpu.make_async_copy(src, dst.at[rows], store_sem.at[which, c, q]))
        return copies

    def mix(c, _):
        for q, i, image in home(c):
            own, other = shares_of(image)
            m = own * x_ref[image].astype(F32) + other * x_ref[lax.rem(partners[image], images)].astype(F32)
            mixed[image] = m
            u, _ = normalise(m)
            n1h[c, q, i] = (u * v(G1) + v(B1)).astype(BF)
        @pl.when(c < early)
        def _():
            ex.send(N1, c, n1h, n1t)

        return 0

    def flat(c, _):
        qkv = dot(n1h[c].reshape(tokens, 256), wf_ref[...]).astype(BF)
        qf[c], kf[c], vf[c] = qkv[:, :128], qkv[:, 128:256], qkv[:, 256:]
        att_f[c] = attend_half(half(c, False), lm, taps_f, vec[CB : CB + 1, :128])
        return 0

    def tall(c, _):
        ex.receive(N1, c, n1h, n1t)
        n1 = permute(n1t[c].reshape(tokens, 256))
        n1p[c] = n1
        qkv = dot(n1, wt_ref[...]).astype(BF)
        qt[c], kt[c], vt[c] = qkv[:, :128], qkv[:, 128:256], qkv[:, 256:]
        att = attend_half(half(c, True), lm, taps_t, vec[CB : CB + 1, 128:])
        att_ts[c] = permute(att).reshape(att_ts.shape[1:])
        ex.send(AT, c, att_ts, att_th)
        return 0

    def mlp(c, _):
        ex.receive(AT, c, att_ts, att_th)
        keep1, keep2 = keep(c, 0), keep(c, 1)
        att = jnp.concatenate([att_f[c], att_th[c].reshape(tokens, 128)], axis=1)
        m = jnp.concatenate([mixed[image] for _, _, image in home(c)], axis=0)
        h1 = m + keep1 * (dot(att, wp[...]) + v(PB))
        u2, rstd2 = normalise(h1)
        n2 = (u2 * v(G2) + v(B2)).astype(BF)
        cot = jnp.concatenate([cot_ref[image] for _, _, image in home(c)], axis=0).astype(F32)
        db2 = (keep2 * cot).astype(BF)
        small[FB2] += sum8(db2.astype(F32))
        n2t = jnp.concatenate([n2.T, jnp.ones((16, tokens), BF)], axis=0)
        db2t = db2.T
        branch2 = jnp.zeros((tokens, 256), F32)
        dn2 = jnp.zeros((tokens, 256), F32)
        for f in range(w1.shape[1] // 256):
            fs = slice(256 * f, 256 * f + 256)
            act, slope = gelu_twice(dot(n2, w1[:, fs]) + v(FB1 + f))
            act = act.astype(BF)
            dpre = (slope * dot(db2, w2[fs, :], 1, 1)).astype(BF)
            branch2 = branch2 + dot(act, w2[fs, :])
            dn2 = dn2 + dot(dpre, w1[:, fs], 1, 1)
            grad = dot(n2t, dpre)
            gw1[:, fs] += grad[:256]
            gb1[:, fs] += grad[256:]
            gw2t[:, fs] += dot(db2t, act)
        done = (h1 + (0.5 * keep2) * (branch2 + 2.0 * v(FB2))).astype(BF)
        for n, (_, _, image) in enumerate(home(c)):
            cot_ref[image] = done[strip * n : strip * n + strip]
        for store in stores(c, 0):
            store.start()
        small[G2] += sum8(dn2 * u2)
        small[B2] += sum8(dn2)
        d = cot + normalise_back(dn2, u2, rstd2, 0.5 * v(G2))
        dh1[c] = d
        db1 = (keep1 * d).astype(BF)
        small[PB] += sum8(db1.astype(F32))
        gp[...] += dot(att, db1, 0, 0)
        datt = dot(db1, wp[...], 1, 1).astype(BF)
        da_f[c] = datt[:, :128]
        da_ts[c] = datt[:, 128:].reshape(da_ts.shape[1:])
        ex.send(DA, c, da_ts, da_tt)
        return 0

    def add_qkv(grad, start):
        for part in range(3):
            cols = slice(256 * part + start, 256 * part + start + 128)
            gq[:, cols] += grad[:, 128 * part : 128 * part + 128]

    def put(stage, blocks):
        rows = stage.shape[2]
        spot = 0
        for value in blocks:
            done = 0
            while done < value.shape[0]:
                piece, at = divmod(spot, rows)
                n = min(rows - at, value.shape[0] - done)
                stage[piece // batch, piece % batch, at : at + n] = value[done : done + n]
                done += n
                spot += n
        while spot < 2 * batch * rows:
            piece, at = divmod(spot, rows)
            stage[piece // batch, piece % batch, at:] = jnp.zeros((rows - at, 256), BF)
            spot += rows - at

    quarters = [slice(256 * f, 256 * f + 256) for f in range(w1.shape[1] // 256)]

    def pack_fc1():
        put(sum_a.stage, [(0.5 * gw1[:, fs]).astype(BF) for fs in quarters])

    def pack_fc2():
        put(sum_b.stage, [(0.5 * gw2t[:, fs]).astype(BF).T for fs in quarters] + [gp[...].astype(BF)])

    def qkv_blocks(start):
        one, two, three = (gq[:, 256 * n + start : 256 * n + start + 128].astype(BF) for n in range(3))
        return [jnp.concatenate([one, two], axis=1), jnp.concatenate([three[:128], three[128:]], axis=1)]

    def pack_flat():
        row = lambda i: jnp.sum(small[i], axis=0, keepdims=True)
        rows = [row(i) * (0.5 if i in (G2, B2) else 1.0) for i in range(CONV)]
        conv = [row(CONV + i) for i in range(9)]
        for i in range(3):
            for j in range(3):
                rows.append(jnp.concatenate([conv[3 * i + j][:, :128], conv[3 * j + i][:, 128:]], axis=1))
        rows += [0.5 * gb1[0:1, fs] for fs in quarters]
        rows.append(jnp.zeros((32 - len(rows), 256), F32))
        put(sum_d.stage, qkv_blocks(0) + [jnp.concatenate(rows, axis=0).astype(BF)])

    def tall_back(c, _):
        ex.receive(DA, c, da_ts, da_tt)
        da = permute(da_tt[c].reshape(tokens, 128))
        s = dict(half(c, True), da=da)
        dqkv = attend_half_back(s, lm, taps_t, small, slice(128, 256))
        add_qkv(dot(n1p[c], dqkv, 0, 0), 128)
        dn_ts[c] = permute(dot(dqkv, wt_ref[...], 1, 1).astype(BF)).reshape(dn_ts.shape[1:])
        return 0

    def at(c, steps):
        for spot, total, n in steps:

            @pl.when(c == min(spot, chunks - 1))
            def _():
                total.step(n)

    def pace(c, first, last):
        @pl.when((c % 2 == 0) & (first + c // 2 < last))
        def _():
            ex.send(DN, first + c // 2, dn_ts, dn_th)

    def tall_loop(c, _):
        tall_back(c, 0)
        pace(c, 0, chunks)
        at(c, TALL_STEPS)
        return 0

    def flat_back(c, _):
        s = dict(half(c, False), da=da_f.at[c])
        dqkv = attend_half_back(s, lm, taps_f, small, slice(0, 128))
        add_qkv(dot(n1h[c].reshape(tokens, 256), dqkv, 0, 0), 0)
        qf[c], kf[c], vf[c] = dqkv[:, :128], dqkv[:, 128:256], dqkv[:, 256:]
        pace(c, (chunks + 1) // 2, chunks)
        at(c, FLAT_STEPS)
        return 0

    def norm_back(c, _):
        ex.sent(N1, c, n1h, n1t)
        ex.receive(DN, c, dn_ts, dn_th)
        dqkv = jnp.concatenate([qf[c], kf[c], vf[c]], axis=1)
        dn1 = dot(dqkv, wf_ref[...], 1, 1) + dn_th[c].reshape(tokens, 256).astype(F32)
        m = jnp.concatenate([mixed[image] for _, _, image in home(c)], axis=0)
        u1, rstd1 = normalise(m)
        tiny[0] += sum8(dn1 * u1)
        tiny[1] += sum8(dn1)
        d = dh1[c] + normalise_back(dn1, u1, rstd1, v(G1))
        for n, (_, _, image) in enumerate(home(c)):
            mixed[image] = d[strip * n : strip * n + strip]
        at(c, NORM_STEPS)
        return 0

    def unmix(c, _):
        for q, i, image in home(c):
            other = inverse[image]
            n1h[c, q, i] = (shares_of(image)[0] * mixed[image] + shares_of(other)[1] * mixed[other]).astype(BF)
        for store in stores(c, 1):
            store.start()
        return 0

    def drain(c, _):
        for kind, src, dst in ((AT, att_ts, att_th), (DA, da_ts, da_tt), (DN, dn_ts, dn_th)):
            ex.sent(kind, c, src, dst)
        for store in stores(c, 0) + stores(c, 1):
            store.wait()
        return 0

    lax.fori_loop(0, chunks, mix, 0)
    lax.fori_loop(0, chunks, flat, 0)
    lax.fori_loop(0, ahead, tall, 0)

    def forward(c, _):
        @pl.when(c < chunks - early)
        def _():
            ex.send(N1, c + early, n1h, n1t)

        @pl.when(c < chunks - ahead)
        def _():
            tall(c + ahead, 0)

        mlp(c, 0)
        return 0

    for load in late:
        load.wait()
    lax.fori_loop(0, chunks, forward, 0)
    TALL_STEPS = ((0, sum_a, 1), (1, sum_b, 1), (3, sum_a, 2), (5, sum_b, 2), (7, sum_a, 3),)
    FLAT_STEPS = ((0, sum_b, 3), (1, sum_c, 1), (1, sum_a, 4), (3, sum_b, 4), (4, sum_a, 5), (5, sum_c, 2), (6, sum_b, 5), (7, sum_c, 3), (7, sum_a, 6),)
    NORM_STEPS = ((0, sum_a, 7), (1, sum_d, 1), (2, sum_b, 6), (5, sum_c, 4), (8, sum_d, 2),)
    pack_fc1()
    sum_a.step(0)
    pack_fc2()
    sum_b.step(0)
    lax.fori_loop(0, chunks, tall_loop, 0)
    put(sum_c.stage, qkv_blocks(128))
    sum_c.step(0)
    lax.fori_loop(0, chunks, flat_back, 0)
    pack_flat()
    sum_d.step(0)
    lax.fori_loop(0, chunks, norm_back, 0)
    rows = [jnp.sum(tiny[n], axis=0, keepdims=True) for n in range(2)] + [jnp.zeros((6, 256), F32)]
    few.start(0, jnp.concatenate(rows, axis=0))
    sum_b.step(7)
    sum_c.step(5)
    half_way = 2 * chunks // 3
    lax.fori_loop(0, half_way, unmix, 0)
    sum_d.step(3)
    few.start(1, few.total(0))
    lax.fori_loop(half_way, chunks, unmix, 0)
    sum_d.step(4)
    last[...] = few.total(1)
    few.sent()
    lax.fori_loop(0, chunks, drain, 0)
    sum_d.step(5)


def share_rows(rows, batch):
    return -(-rows // (2 * batch * 16)) * 16


def block(inputs, cotangent, boxes, drops, partners, inverse, vectors, weights, pair=2, ahead=2, early=4):
    images, grid_rows, side, width = inputs.shape
    shares, batch = lax.axis_size("row"), lax.axis_size("batch")
    strip = grid_rows * side
    chunks = images // shares // pair
    tokens = shares * pair * strip
    hidden = weights[2].shape[1]
    sds = jax.ShapeDtypeStruct
    vmem = pl.BlockSpec(memory_space=pltpu.VMEM)
    hbm = pl.BlockSpec(memory_space=pl.ANY)
    x = inputs.reshape(images, strip, width)
    cot = cotangent.reshape(images, strip, width)
    sizes = [hidden, hidden + width, 3 * width // 2, 3 * width // 2 + 32]
    sizes = [share_rows(n, batch) for n in sizes]
    rows = lambda ch, dt=BF: pltpu.VMEM((chunks, tokens, ch), dt)
    at_home = lambda ch: pltpu.VMEM((chunks, shares, pair, strip, ch), BF)
    at_tall = lambda ch: pltpu.VMEM((chunks, pair, shares, strip, ch), BF)
    part = lambda n, *lead: pltpu.VMEM((*lead, n, width), BF)
    return pl.pallas_call(
        functools.partial(block_kernel, shares, ahead, early),
        in_specs=[hbm] * 7 + [vmem] * (1 + len(vectors) + 2),
        out_specs=[hbm, hbm] + [vmem] * 5,
        out_shape=[
            sds(x.shape, BF),
            sds(x.shape, BF),
        ]
        + [sds((2, batch, n, width), BF) for n in sizes]
        + [sds((8, width), F32)],
        scratch_shapes=[
            pltpu.VMEM((2, 8, width), F32),
            pltpu.VMEM((2, 8, width), F32),
            pltpu.VMEM((shares, 8, width), F32),
            pltpu.VMEM((batch, 8, width), F32),
            pltpu.SemaphoreType.DMA((shares + batch,)),
            pltpu.SemaphoreType.DMA((shares + batch,)),
            pltpu.VMEM(x.shape, BF),
            pltpu.VMEM(weights[2].shape, BF),
            pltpu.VMEM(weights[3].shape, BF),
            pltpu.SMEM(boxes.shape, jnp.int32),
            pltpu.SMEM(drops.shape, jnp.int32),
            pltpu.SMEM(partners.shape, jnp.int32),
            pltpu.SMEM(inverse.shape, jnp.int32),
            pltpu.VMEM((24, width), F32),
            pltpu.VMEM((width, hidden), F32),
            pltpu.VMEM((16, hidden), F32),
            pltpu.VMEM((width, hidden), F32),
            pltpu.VMEM((width, 3 * width), F32),
            pltpu.VMEM((width, width), F32),
            pltpu.VMEM((16, 8, width), F32),
            pltpu.VMEM((256, 256), BF),
            pltpu.VMEM((width, 384), BF),
            pltpu.VMEM((width, 384), BF),
            pltpu.VMEM(x.shape, F32),
            at_home(width),
            at_tall(width),
            rows(width),
        ]
        + [rows(128)] * 9
        + [at_tall(128), at_home(128), rows(width, F32), rows(128), at_home(128), at_tall(128), at_tall(width), at_home(width)]
        + [pltpu.SemaphoreType.DMA((4, chunks, shares - 1))] * 2
        + [pltpu.SemaphoreType.DMA((len(sizes), 2 * batch + 1))] * 2
        + [pltpu.SemaphoreType.DMA((7,)), pltpu.SemaphoreType.DMA((2, chunks, shares))]
        + [z for n in sizes for z in (part(n, 2, batch), part(n, batch), part(n, batch), part(n), part(n))],
        compiler_params=pltpu.CompilerParams(
            collective_id=0, has_side_effects=True, vmem_limit_bytes=63 * 2**20
        ),
    )(boxes, drops, partners, inverse, cot, *weights[2:], x, *vectors, *weights[:2])


def finish_kernel(out_ref, ig_ref, hbm_a, hbm_b, hbm_c, hbm_d, last, *refs):
    out, ig, g1, b1, gq_hbm, conv, cb, gp_hbm, pb, g2, b2, gw1_hbm, fb1, gw2_hbm, fb2 = refs[:15]
    held, sum_a, sum_b, sum_c, sum_d, gq, gp, gw1, gw2, load_sem, store_sem = refs[15:]
    sixth = out.shape[0] // 6
    loads = [
        pltpu.make_async_copy(src, dst, load_sem.at[m])
        for m, (src, dst) in enumerate(((hbm_a, sum_a), (hbm_b, sum_b), (hbm_c, sum_c), (hbm_d, sum_d)))
    ]
    stores = [
        pltpu.make_async_copy(src, dst, store_sem.at[m])
        for m, (src, dst) in enumerate(((gw1, gw1_hbm), (gw2, gw2_hbm), (gp, gp_hbm), (gq, gq_hbm)))
    ]
    parts = [(n, pl.ds(sixth * i, sixth), 6 * n + i + 4) for i in range(6) for n in range(2)]
    loads += [pltpu.make_async_copy((out_ref, ig_ref)[n].at[r], held.at[n, r], load_sem.at[m]) for n, r, m in parts]
    stores += [pltpu.make_async_copy(held.at[n, r], (out, ig)[n].at[r], store_sem.at[m]) for n, r, m in parts]
    for load in loads:
        load.start()
    hidden = gw1.shape[1]
    loads[0].wait()
    for f in range(hidden // 256):
        gw1[:, 256 * f : 256 * f + 256] = sum_a[256 * f : 256 * f + 256].astype(F32)
    stores[0].start()
    loads[1].wait()
    gw2[...] = sum_b[:hidden].astype(F32)
    gp[...] = sum_b[hidden : hidden + 256].astype(F32)
    stores[1].start()
    stores[2].start()
    loads[2].wait()
    loads[3].wait()
    for ref, start in ((sum_d, 0), (sum_c, 128)):
        gq[:, start : start + 128] = ref[:256, :128].astype(F32)
        gq[:, 256 + start : 384 + start] = ref[:256, 128:].astype(F32)
        gq[:128, 512 + start : 640 + start] = ref[256:384, :128].astype(F32)
        gq[128:, 512 + start : 640 + start] = ref[256:384, 128:].astype(F32)
    stores[3].start()
    for load, store in zip(loads[4:], stores[4:]):
        load.wait()
        store.start()
    rows = sum_d[384:416].astype(F32)
    for n, ref in ((G2, g2), (B2, b2), (PB, pb), (FB2, fb2), (CB, cb)):
        ref[...] = rows[n]
    g1[...], b1[...] = last[0], last[1]
    for i in range(3):
        for j in range(3):
            conv[i, j] = rows[CONV + 3 * i + j]
    for f in range(hidden // 256):
        fb1[256 * f : 256 * f + 256] = rows[FB1 + f]
    for store in stores:
        store.wait()


def finish(out, ig, sums, last, hidden):
    width = out.shape[-1]
    sds = jax.ShapeDtypeStruct
    vmem = pl.BlockSpec(memory_space=pltpu.VMEM)
    hbm = pl.BlockSpec(memory_space=pl.ANY)
    flat = lambda n: sds((n,), F32)
    square = lambda *n: sds(n, F32)
    large = [square(width, 3 * width), square(width, width), square(width, hidden), square(hidden, width)]
    shapes = [
        flat(width),
        flat(width),
        large[0],
        square(3, 3, width),
        flat(width),
        large[1],
        flat(width),
        flat(width),
        flat(width),
        large[2],
        flat(hidden),
        large[3],
        flat(width),
    ]
    sums = [z.reshape(-1, width) for z in sums]
    return pl.pallas_call(
        finish_kernel,
        in_specs=[hbm] * 6 + [vmem],
        out_specs=[hbm, hbm] + [hbm if z in large else vmem for z in shapes],
        out_shape=[sds(out.shape, BF), sds(ig.shape, BF)] + shapes,
        scratch_shapes=[pltpu.VMEM((2,) + out.shape, BF)]
        + [pltpu.VMEM(z.shape, BF) for z in sums]
        + [pltpu.VMEM(z.shape, F32) for z in large]
        + [pltpu.SemaphoreType.DMA((16,))] * 2,
        compiler_params=pltpu.CompilerParams(vmem_limit_bytes=62 * 2**20),
    )(out, ig, *sums, last)


def per_device(
    inputs,
    partners,
    boxes,
    drops,
    norm1_gain,
    norm1_bias,
    qkv_weight,
    lepe_weight,
    lepe_bias,
    proj_weight,
    proj_bias,
    norm2_gain,
    norm2_bias,
    fc1_weight,
    fc1_bias,
    fc2_weight,
    fc2_bias,
    cotangent,
):
    images = inputs.shape[0]
    ids = jnp.arange(images)
    inverse = jnp.sum(jnp.where(partners[:, None] % images == ids[None, :], ids[:, None], 0), axis=0)
    vectors = (norm1_gain, norm1_bias, norm2_gain, norm2_bias, proj_bias, fc2_bias, lepe_bias, lepe_weight, fc1_bias)
    weights = (qkv_weight, proj_weight, fc1_weight, fc2_weight)
    out, ig, *sums, last = block(inputs, cotangent, boxes.T, drops.T, partners, inverse, vectors, weights)
    out, ig, *grads = finish(out, ig, sums, last, fc1_weight.shape[1])
    return (out.reshape(inputs.shape), ig.reshape(inputs.shape), *grads)


def solution(mesh):
    tokens = P("batch", "row", None, None)
    return jax.shard_map(
        per_device,
        mesh=mesh,
        in_specs=(tokens, P("batch"), P("batch", None), P("batch", None)) + (P(),) * 13 + (tokens,),
        out_specs=(tokens, tokens) + (P(),) * 13,
        check_vma=False,
    )
```
